128 devices in a mesh: fsdp: 16 (over x_lo, y, core), sp: 8 (over x_hi, z).
Axes of the slice: x: 4 (x_hi: 2, x_lo: 2; x = x_hi * 2 + x_lo), y: 4, z: 4, core: 2. Of those that a mesh axis runs over, the one named last changes fastest.
Arguments:
- tokens: bfloat16 [16, 1024, 1024], P('fsdp', 'sp'), may hold values from -6 to 6
- cotangent: bfloat16 [16, 1024, 1024], P('fsdp', 'sp'), may hold values from -6 to 6
- w_qkv: bfloat16 [1024, 3072], P('fsdp'), may hold values from -0.1875 to 0.1875
- bias_q: bfloat16 [1024], P('fsdp'), may hold values from -3 to 3
- bias_v: bfloat16 [1024], P('fsdp'), may hold values from -0.125 to 0.125
- w_out: bfloat16 [1024, 1024], P('fsdp'), may hold values from -3 to 3
- bias_out: bfloat16 [1024], P('fsdp'), may hold values from -3 to 3
- gain_one: bfloat16 [1024], P('fsdp'), may hold values from 0.5 to 1.5
- shift_one: bfloat16 [1024], P('fsdp'), may hold values from -3 to 3
- w_up: bfloat16 [1024, 4096], P('fsdp'), may hold values from -0.1875 to 0.1875
- bias_up: bfloat16 [4096], P('fsdp'), may hold values from -3 to 3
- w_down: bfloat16 [4096, 1024], P('fsdp'), may hold values from -0.09375 to 0.09375
- bias_down: bfloat16 [1024], P('fsdp'), may hold values from -3 to 3
- gain_two: bfloat16 [1024], P('fsdp'), may hold values from 0.5 to 1.5
- shift_two: bfloat16 [1024], P('fsdp'), may hold values from -3 to 3
Outputs:
- output: bfloat16 [16, 1024, 1024], P('fsdp', 'sp')
- grad_tokens: bfloat16 [16, 1024, 1024], P('fsdp', 'sp')
- grad_w_qkv: float32 [1024, 3072], P('fsdp')
- grad_bias_q: float32 [1024], P('fsdp')
- grad_bias_v: float32 [1024], P('fsdp')
- grad_w_out: float32 [1024, 1024], P('fsdp')
- grad_bias_out: float32 [1024], P('fsdp')
- grad_gain_one: float32 [1024], P('fsdp')
- grad_shift_one: float32 [1024], P('fsdp')
- grad_w_up: float32 [1024, 4096], P('fsdp')
- grad_bias_up: float32 [4096], P('fsdp')
- grad_w_down: float32 [4096, 1024], P('fsdp')
- grad_bias_down: float32 [1024], P('fsdp')
- grad_gain_two: float32 [1024], P('fsdp')
- grad_shift_two: float32 [1024], P('fsdp')
The draws below stay inside these ranges and needn't reach their ends.
All inputs are finite; a program needn't handle non-finite values.
Results may differ from the reference program's by a relative error of at most 0.024.
Values may be sent and summed in bfloat16 or wider, within the bound.
A program may use at most 128 MiB of HBM per device.

```python
import math
import jax
import jax.numpy as jnp
from jax import lax

D = 1024
H = 16
HD = 64
FF = 4096
LEN = 1024
SEQUENCES = 16


def shard_levels(key, dims, shards, smallest, high):
    def one(position, blocks):
        draws = jax.random.uniform(jax.random.fold_in(jax.random.fold_in(key, 6), position), (blocks,), jnp.float32, smallest / len(shards), high / len(shards))
        return jnp.repeat(jnp.exp(draws), dims[position] // blocks).reshape((-1,) + (1,) * (len(dims) - position - 1))

    level = one(*shards[0])
    for cut in shards[1:]:
        level = level * one(*cut)
    return level


def normal_values(rng, extent, scale, reach, split=(), kind=jnp.bfloat16):
    drawn = jax.random.normal(rng, extent, jnp.float32) * scale
    if len(split) > 0:
        drawn = shard_levels(rng, extent, split, -0.22, 0.18) * drawn
    return jnp.clip(drawn, min=-reach, max=reach).astype(kind)


def setup_inputs(seed: int = 0) -> dict:
    key_list = jax.random.split(jax.random.key(seed), 16)
    return {
        "tokens": normal_values(key_list[0], (SEQUENCES, LEN, D), 1.0, 6.0, ((0, 16), (1, 8))),
        "cotangent": normal_values(key_list[1], (SEQUENCES, LEN, D), 1.0, 6.0, ((0, 16), (1, 8))),
        "w_qkv": normal_values(key_list[2], (D, 3 * D), D ** -0.5, 0.1875, ((0, 16),)),
        "bias_q": normal_values(key_list[3], (D,), 0.5, 3.0, ((0, 16),)),
        "bias_v": normal_values(key_list[4], (D,), 0.02, 0.125, ((0, 16),)),
        "w_out": normal_values(key_list[5], (D, D), (max(1, 4 * D // LEN)) ** -0.5, 3.0, ((0, 16),)),
        "bias_out": normal_values(key_list[6], (D,), 0.5, 3.0, ((0, 16),)),
        "gain_one": jnp.clip(1.0 + 0.1 * jax.random.normal(key_list[7], (D,), jnp.float32), 0.5, 1.5).astype(jnp.bfloat16),
        "shift_one": normal_values(key_list[8], (D,), 0.5, 3.0, ((0, 16),)),
        "w_up": normal_values(key_list[9], (D, FF), D ** -0.5, 0.1875, ((0, 16),)),
        "bias_up": normal_values(key_list[10], (FF,), 0.5, 3.0, ((0, 16),)),
        "w_down": normal_values(key_list[11], (FF, D), FF ** -0.5, 0.09375, ((0, 16),)),
        "bias_down": normal_values(key_list[12], (D,), 0.5, 3.0, ((0, 16),)),
        "gain_two": jnp.clip(1.0 + 0.1 * jax.random.normal(key_list[13], (D,), jnp.float32), 0.5, 1.5).astype(jnp.bfloat16),
        "shift_two": normal_values(key_list[14], (D,), 0.5, 3.0, ((0, 16),)),
    }


@jax.custom_vjp
def low(v):
    return lax.optimization_barrier(v.astype(jnp.bfloat16)).astype(jnp.float32)

@jax.custom_vjp
def low_back(v):
    return v

def low_keep(v):
    return (low(v), None)

def low_pass(kept, grad):
    return (grad,)

def back_keep(v):
    return (v, None)

def back_low(kept, grad):
    return (low(grad),)
low.defvjp(low_keep, low_pass)
low_back.defvjp(back_keep, back_low)
epsilon = 1e-05
highest = lax.Precision.HIGHEST

def product(left_op, right_op):
    return jnp.dot(left_op, right_op, precision=highest, preferred_element_type=jnp.float32)

def norm_rows(values, scale_vec, shift_vec):
    center = values - lax.optimization_barrier(jnp.mean(values, axis=-1, keepdims=True))
    spread = lax.optimization_barrier(jnp.mean(center * center, axis=-1, keepdims=True))
    return center * lax.rsqrt(spread + epsilon) * scale_vec + shift_vec

def attend_sequence(triple):
    queries, keys_all, values_all = triple
    scores = low_back(jnp.einsum('qhd,khd->hqk', queries, keys_all, precision=highest) * 0.125)
    row_peak = lax.optimization_barrier(jnp.max(scores, axis=-1, keepdims=True))
    raised = jnp.exp(scores - row_peak)
    attn_probs = raised / lax.optimization_barrier(jnp.sum(raised, axis=-1, keepdims=True))
    context = jnp.einsum('hqk,khd->qhd', low(attn_probs), values_all, precision=highest)
    return low_back(low(context))

def layer_group(seq_block, params):
    w_qkv, bias_q, bias_v, w_out, bias_out, gain_one, shift_one, w_up, bias_up, w_down, bias_down, gain_two, shift_two = params
    seq_count, seq_len, model_width = seq_block.shape
    flat_rows = seq_block.reshape(seq_count * seq_len, model_width)
    projected = product(flat_rows, w_qkv)
    queries = low_back(low(projected[:, :model_width] + bias_q))
    keys_all = low_back(low(projected[:, model_width:2 * model_width]))
    values_all = low_back(low(projected[:, 2 * model_width:] + bias_v))
    head_shape = (seq_count, seq_len, H, HD)
    context = lax.map(jax.checkpoint(attend_sequence), (queries.reshape(head_shape), keys_all.reshape(head_shape), values_all.reshape(head_shape)))
    context = context.reshape(seq_count * seq_len, model_width)
    branch = low_back(product(context, w_out) + bias_out)
    normed_one = norm_rows(flat_rows + branch, gain_one, shift_one)
    pre_act = low_back(product(low(normed_one), w_up) + bias_up)
    ffn_out = low_back(product(low(jax.nn.gelu(pre_act, approximate=False)), w_down) + bias_down)
    second = norm_rows(normed_one + ffn_out, gain_two, shift_two)
    return second.reshape(seq_block.shape)

def reference(tokens, cotangent, w_qkv, bias_q, bias_v, w_out, bias_out, gain_one, shift_one, w_up, bias_up, w_down, bias_down, gain_two, shift_two):
    params = tuple((weight_arg.astype(jnp.float32) for weight_arg in (w_qkv, bias_q, bias_v, w_out, bias_out, gain_one, shift_one, w_up, bias_up, w_down, bias_down, gain_two, shift_two)))
    seq_group = math.gcd(SEQUENCES, max(1, 4096 // LEN))

    def forward(inputs, weights):
        seq_blocks = inputs.reshape(SEQUENCES // seq_group, seq_group, LEN, D)

        def run_block(seq_block):
            return layer_group(seq_block, weights)
        results = lax.map(jax.checkpoint(run_block), seq_blocks)
        return results.reshape(inputs.shape)
    output, pullback = jax.vjp(forward, tokens.astype(jnp.float32), params)
    grad_input, grad_list = pullback(cotangent.astype(jnp.float32))
    return (output.astype(jnp.bfloat16), grad_input.astype(jnp.bfloat16), grad_list[0], grad_list[1], grad_list[2], grad_list[3], grad_list[4], grad_list[5], grad_list[6], grad_list[7], grad_list[8], grad_list[9], grad_list[10], grad_list[11], grad_list[12])
```

```python
import functools
import math

import jax
import jax.numpy as jnp
from jax import lax
from jax.experimental import pallas as pl
from jax.experimental.pallas import tpu as pltpu
from jax.sharding import PartitionSpec as P

HD = 64
MESH = pl.DeviceIdType.MESH
BF = jnp.bfloat16
F32 = jnp.float32

epsilon = 1e-05
root_half = 0.7071067811865476
inv_root_two_pi = 0.3989422804014327


class Place:
    def __init__(self):
        f = lax.axis_index("fsdp")
        s = lax.axis_index("sp")
        self.xh, self.xl, self.y, self.z, self.c = s // 4, f // 8, (f // 2) % 4, s % 4, f % 2
        self.x = 2 * self.xh + self.xl

    def to(self, dx=0, dy=0, dz=0, dc=0):
        x = lax.rem(self.x + dx + 4, 4)
        y = lax.rem(self.y + dy + 4, 4)
        z = lax.rem(self.z + dz + 4, 4)
        c = self.c if dc == 0 else 1 - self.c
        return ((x % 2) * 8 + y * 2 + c, (x // 2) * 4 + z)


class Copies:
    def __init__(self, send, recv):
        self.send, self.recv, self.n = send, recv, 0

    def remote(self, src, dst, dev):
        i = self.n
        self.n += 1
        cp = pltpu.make_async_remote_copy(
            src_ref=src,
            dst_ref=dst,
            send_sem=self.send.at[i],
            recv_sem=self.recv.at[i],
            device_id=dev,
            device_id_type=MESH,
        )
        cp.start()
        return cp

    def local(self, src, dst):
        i = self.n
        self.n += 1
        cp = pltpu.make_async_copy(src, dst, self.recv.at[i])
        cp.start()
        return cp


def greet(targets):
    bar = pltpu.get_barrier_semaphore()
    for t in targets:
        pl.semaphore_signal(bar, inc=1, device_id=t, device_id_type=MESH)
    pl.semaphore_wait(bar, len(targets))


class Gather:
    def __init__(self, place, copies, src, out, lo, n, quarters):
        self.p, self.s, self.src, self.out = place, copies, src, out
        self.lo, self.n, self.quarters = lo, n, quarters
        self.sent, self.core = [], []

    def cols(self, half=None):
        if half is None:
            return pl.ds(self.lo, self.n)
        return pl.ds(self.lo + half * (self.n // 2), self.n // 2)

    def go(self, src, dst, **k):
        cp = self.s.remote(src, dst, self.p.to(**k))
        self.sent.append(cp)
        return cp

    def q(self):
        return self.p.z if self.quarters else slice(None)

    def start(self):
        p, o, q = self.p, self.out, self.q()
        self.own = self.s.local(
            self.src.at[:, :, self.cols()], o.at[p.xl, p.y, p.c, :, :, self.cols()]
        )
        self.ycp = [
            self.go(
                self.src.at[q, :, self.cols()], o.at[p.xl, p.y, p.c, q, :, self.cols()], dy=k
            )
            for k in (1, 3, 2)
        ]
        self.xcp = [
            self.go(
                self.src.at[q, :, self.cols(h)], o.at[p.xl, p.y, p.c, q, :, self.cols(h)], dx=dx
            )
            for h, dx in ((0, 1), (1, -1))
        ]

    def stage_x(self):
        p, o, q = self.p, self.out, self.q()
        for k, cp in zip((3, 1, 2), self.ycp):
            cp.wait_recv()
            for h, dx in ((0, 1), (1, -1)):
                r = o.at[p.xl, lax.rem(p.y + k, 4), p.c, q, :, self.cols(h)]
                self.xcp.append(self.go(r, r, dx=dx))
        if self.quarters:
            self.zcp = []
            for dz in (1, 3, 2):
                for k in (1, 2, 3):
                    r = o.at[p.xl, lax.rem(p.y + k, 4), p.c, q, :, self.cols()]
                    self.zcp.append(self.go(r, r, dz=dz))
        else:
            self.own.wait()
            r = o.at[p.xl, :, p.c, :, :, self.cols()]
            self.core.append(self.go(r, r, dc=1))

    def stage_z(self):
        if not self.quarters:
            return
        p, o, q = self.p, self.out, self.q()
        for cp in self.xcp:
            cp.wait_recv()
        for dz in (1, 3, 2):
            r = o.at[1 - p.xl, :, p.c, q, :, self.cols()]
            self.zcp.append(self.go(r, r, dz=dz))

    def stage_core(self):
        p, o = self.p, self.out
        if self.quarters:
            for cp in self.zcp:
                cp.wait_recv()
            self.own.wait()
            r = o.at[p.xl, :, p.c, :, :, self.cols()]
            self.core.append(self.go(r, r, dc=1))
        else:
            for cp in self.xcp:
                cp.wait_recv()
        r = o.at[1 - p.xl, :, p.c, :, :, self.cols()]
        self.core.append(self.go(r, r, dc=1))

    def arrived(self):
        for cp in self.core:
            cp.wait_recv()
        self.core = []

    def finish(self):
        self.arrived()
        for cp in self.sent:
            cp.wait_send()


class Reduce:
    def __init__(self, place, copies, order, g, bufs, total):
        self.p, self.s, self.order, self.g = place, copies, order, g
        self.r1, self.s1, self.r2, self.s2, self.r3 = bufs
        self.tot = total
        self.n = g.shape[-1]
        self.sent = []

    def go(self, src, dst, **k):
        cp = self.s.remote(src, dst, self.p.to(**k))
        self.sent.append(cp)
        return cp

    def half(self, xh):
        m = self.n // 2
        return pl.ds(pl.multiple_of(xh * m, 128), m)

    def me(self, i):
        return {"x": self.p.x, "y": self.p.y, "z": self.p.z}[self.order[i]]

    def pick(self, ref, i, v):
        o, ax = self.order, self.order[i]
        if ax == "x":
            rest = [slice(None)] * (len(ref.shape) - 2)
            return ref.at[(lax.rem(v, 2),) + tuple(rest) + (self.half(v // 2),)]
        lead = 0 if "x" in o[:i] else 1
        if ax == "z" and "y" not in o[:i]:
            lead += 1
        return ref.at[(slice(None),) * lead + (v,)]

    def scatter(self, i, src, recv):
        me = self.me(i)
        return [
            self.go(
                self.pick(src, i, lax.rem(me + k, 4)), recv.at[k - 1], **{"d" + self.order[i]: k}
            )
            for k in (1, 3, 2)
        ]

    def add(self, i, src, recv, out, cps):
        for cp in cps:
            cp.wait_recv()
        own = self.pick(src, i, self.me(i))
        shape = out.shape
        rows = (slice(None), slice(None))

        def one(idx):
            acc = own[idx].astype(F32)
            for k in range(3):
                acc = acc + recv[(k,) + idx].astype(F32)
            out[idx] = acc.astype(out.dtype)

        if len(shape) == 2:
            one(rows)
            return

        def body(j, _):
            idx = []
            for d in reversed(shape[:-2]):
                idx.insert(0, lax.rem(j, d))
                j = j // d
            one(tuple(idx) + rows)
            return 0

        lax.fori_loop(0, math.prod(shape[:-2]), body, 0)

    def first(self):
        self.c1 = self.scatter(0, self.g, self.r1)

    def second(self):
        self.add(0, self.g, self.r1, self.s1, self.c1)
        self.c2 = self.scatter(1, self.s1, self.r2)

    def third(self):
        self.add(1, self.s1, self.r2, self.s2, self.c2)
        self.c3 = self.scatter(2, self.s2, self.r3)

    def share(self):
        p = self.p
        mine = self.tot.at[p.z, :, self.half(p.xh)]
        self.add(2, self.s2, self.r3, mine, self.c3)
        self.c4 = self.go(mine, mine, dx=2)

    def spread(self):
        self.c4.wait_recv()
        r = self.tot.at[self.p.z]
        self.c5 = [self.go(r, r, dz=k) for k in (1, 3, 2)]

    def done(self):
        for cp in self.c5:
            cp.wait_recv()

    def finish(self):
        for cp in self.sent:
            cp.wait_send()


def reduce_shapes(order, q, n):
    full = {"x": 2, "y": 4, "z": 4}
    left, width, out = ["x", "y", "z"], n, []
    for i, ax in enumerate(order):
        left.remove(ax)
        if ax == "x":
            width = n // 2
        s = tuple(full[a] for a in left) + (q, width)
        out.append((3,) + s)
        if i < 2:
            out.append(s)
    return out


def run_pipe(steps, offsets, count):
    for t in range(count + max(offsets)):
        for step, d in zip(steps, offsets):
            if 0 <= t - d < count:
                step(t - d)


ROWS = {"small": 16, "qkv": 64, "out": 64, "up": 64, "down": 256}
COLS = {"small": 256, "qkv": 3072, "out": 1024, "up": 4096, "down": 1024}
GATHER_NAMES = ("small", "qkv", "out", "up", "down")
GATHER_PARTS = (
    ("small", 0, 256, False),
    ("qkv", 0, 1536, False),
    ("qkv", 1536, 1536, True),
    ("out", 0, 1024, False),
    ("up", 0, 1024, True),
    ("up", 1024, 1024, False),
    ("up", 2048, 1024, True),
    ("up", 3072, 1024, False),
    ("down", 0, 512, False),
    ("down", 512, 512, False),
)


def quarters_of(m):
    return 1 if m == "small" else 4


def gather_kernel(*refs):
    k = len(GATHER_NAMES)
    ins = dict(zip(GATHER_NAMES, refs[:k]))
    outs = dict(zip(GATHER_NAMES, refs[k : 2 * k]))
    p, s = Place(), Copies(*refs[2 * k :])
    greet(
        [p.to(dy=1), p.to(dy=2), p.to(dy=3), p.to(dx=1), p.to(dx=3)]
        + [p.to(dz=1), p.to(dz=2), p.to(dz=3), p.to(dc=1)]
    )
    parts = [Gather(p, s, ins[m], outs[m], lo, n, quarters) for m, lo, n, quarters in GATHER_PARTS]
    run_pipe(
        (
            lambda i: parts[i].start(),
            lambda i: parts[i].stage_x(),
            lambda i: parts[i].stage_z(),
            lambda i: parts[i].stage_core(),
        ),
        (0, 3, 5, 6),
        len(parts),
    )
    for g in parts:
        g.finish()


def gather_parameters(arrays):
    ins, shapes = [], []
    for m, a in zip(GATHER_NAMES, arrays):
        q = quarters_of(m)
        a = a.reshape(q, ROWS[m] // q, COLS[m])
        ins.append(a)
        shapes.append(jax.ShapeDtypeStruct((2, 4, 2) + a.shape, BF))
    anywhere = pl.BlockSpec(memory_space=pl.ANY)
    out = pl.pallas_call(
        gather_kernel,
        out_shape=shapes,
        in_specs=[anywhere] * len(ins),
        out_specs=[anywhere] * len(ins),
        scratch_shapes=[pltpu.SemaphoreType.DMA((200,)), pltpu.SemaphoreType.DMA((200,))],
        compiler_params=pltpu.CompilerParams(collective_id=1, has_side_effects=True),
        name="gather_parameters",
    )(*ins)
    return [o.reshape(16 * ROWS[m], COLS[m]) for m, o in zip(GATHER_NAMES, out)]


SMALL_SHAPE = (2, 4, 4, 8, 256)


class Products:
    def __init__(self, place, copies, left, right, both_left, both_right, totals, pieces, g, bufs):
        self.p, self.s = place, copies
        self.left, self.right = left, right
        self.both_left, self.both_right = both_left, both_right
        self.pieces, self.g = pieces, g
        self.swaps, self.ready = {}, set()
        self.red = [
            Reduce(place, copies, o, gi, b, totals[m].at[:, :, pl.ds(lo, n)])
            for (m, lo, n, o), gi, b in zip(pieces, g, bufs)
        ]

    def swap(self, m):
        p, s = self.p, self.s
        here = [
            s.local(self.left[m].at[:, :, p.c], self.both_left[m].at[:, :, :, pl.ds(0, 128)]),
            s.local(self.right[m], self.both_right[m].at[pl.ds(0, 128)]),
        ]
        there = [
            s.remote(
                self.left[m].at[:, :, 1 - p.c],
                self.both_left[m].at[:, :, :, pl.ds(128, 128)],
                p.to(dc=1),
            ),
            s.remote(self.right[m], self.both_right[m].at[pl.ds(128, 128)], p.to(dc=1)),
        ]
        self.swaps[m] = (here, there)

    def begin(self, i):
        m, lo, n, _ = self.pieces[i]
        if m not in self.ready:
            for cp in self.swaps[m][0]:
                cp.wait()
            for cp in self.swaps[m][1]:
                cp.wait_recv()
            self.ready.add(m)
        left, right, g = self.both_left[m], self.both_right[m], self.g[i]
        rows = left.shape[2]
        tile = min(512, n)

        def body(j, _):
            b, t = j // (n // tile), lax.rem(j, n // tile)
            c0 = pl.multiple_of(lo + t * tile, tile)
            v = jnp.dot(
                left[b].reshape(4 * rows, 256),
                right[:, pl.ds(c0, tile)],
                preferred_element_type=F32,
            ).astype(BF)
            g[b, :, :, :, pl.ds(pl.multiple_of(t * tile, tile), tile)] = v.reshape(
                4, 4, rows // 4, tile
            )
            return 0

        lax.fori_loop(0, 2 * (n // tile), body, 0)
        self.red[i].first()

    def finish(self):
        for r in self.red:
            r.finish()
        for m in self.swaps:
            for cp in self.swaps[m][1]:
                cp.wait_send()


def piece_scratch(pieces):
    sc = []
    for m, _, n, o in pieces:
        q = ROWS[m] // 4
        sc.append(pltpu.VMEM((2, 4, 4, q, n), BF))
        sc += [pltpu.VMEM(x, BF) for x in reduce_shapes(o, q, n)]
    return sc


PIECES = (
    ("up", 0, 1024, "xyz"),
    ("up", 1024, 1024, "yzx"),
    ("up", 2048, 1024, "zxy"),
    ("up", 3072, 1024, "xyz"),
    ("down", 0, 512, "yzx"),
    ("down", 512, 512, "zxy"),
    ("qkv", 0, 1024, "xyz"),
    ("qkv", 1024, 1024, "yzx"),
    ("qkv", 2048, 1024, "zxy"),
    ("out", 0, 1024, "xyz"),
)
GRAD_NAMES = ("up", "down", "qkv", "out")


def grads_kernel(*refs):
    refs = list(refs)

    def take(n):
        head = refs[:n]
        del refs[:n]
        return head

    k = len(GRAD_NAMES)
    left = dict(zip(GRAD_NAMES, take(k)))
    right = dict(zip(GRAD_NAMES, take(k)))
    (small,) = take(1)
    totals = dict(zip(GRAD_NAMES, take(k)))
    (small_total,) = take(1)
    both_left = dict(zip(GRAD_NAMES, take(k)))
    both_right = dict(zip(GRAD_NAMES, take(k)))
    small_in, small_g = take(2)
    small_bufs = take(5)
    g, bufs = [], []
    for _ in PIECES:
        g += take(1)
        bufs.append(take(5))
    p, s = Place(), Copies(*refs)
    greet(
        [p.to(dy=1), p.to(dy=2), p.to(dy=3), p.to(dx=1), p.to(dx=2), p.to(dx=3)]
        + [p.to(dz=1), p.to(dz=2), p.to(dz=3), p.to(dc=1)]
    )
    prod = Products(p, s, left, right, both_left, both_right, totals, PIECES, g, bufs)
    for m in GRAD_NAMES:
        prod.swap(m)
    small_swap = s.remote(small.at[:, :, 1 - p.c], small_in, p.to(dc=1))
    small_own = s.local(small.at[:, :, p.c], small_g)
    small_red = Reduce(p, s, "xyz", small_g, small_bufs, small_total)

    def begin(i):
        if i < len(PIECES):
            prod.begin(i)
            return
        small_own.wait()
        small_swap.wait_recv()
        small_g[...] = small_g[...] + small_in[...]
        small_red.first()

    red = prod.red + [small_red]
    n = len(PIECES) + 1
    run_pipe(
        (
            begin,
            lambda i: red[i].second(),
            lambda i: red[i].third(),
            lambda i: red[i].share(),
            lambda i: red[i].spread(),
            lambda i: red[i].done(),
        ),
        (0, 5, 6, 7, 8, 9),
        n,
    )
    prod.finish()
    small_red.finish()
    small_swap.wait_send()


def weight_gradients(pairs, small):
    lefts = [pairs[m][0].T.reshape(2, 4, 2, ROWS[m], 128) for m in GRAD_NAMES]
    rights = [pairs[m][1] for m in GRAD_NAMES]
    packed = jnp.pad(small.reshape(2, 4, 2, 4, 1, 2, 96), ((0, 0),) * 4 + ((0, 7), (0, 0), (0, 32)))
    packed = packed.reshape(2, 4, 2, 4, 8, 256)
    scratch = [pltpu.VMEM((2, 4, ROWS[m], 256), BF) for m in GRAD_NAMES]
    scratch += [pltpu.VMEM((256, COLS[m]), BF) for m in GRAD_NAMES]
    scratch += [pltpu.VMEM(SMALL_SHAPE, F32)] * 2
    scratch += [pltpu.VMEM(x, F32) for x in reduce_shapes("xyz", 8, 256)]
    scratch += piece_scratch(PIECES)
    scratch += [pltpu.SemaphoreType.DMA((250,)), pltpu.SemaphoreType.DMA((250,))]
    anywhere = pl.BlockSpec(memory_space=pl.ANY)
    here = pl.BlockSpec(memory_space=pltpu.VMEM)
    out = pl.pallas_call(
        grads_kernel,
        out_shape=[jax.ShapeDtypeStruct((4, ROWS[m] // 4, COLS[m]), BF) for m in GRAD_NAMES]
        + [jax.ShapeDtypeStruct((4, 8, 256), F32)],
        in_specs=[anywhere] * (2 * len(GRAD_NAMES) + 1),
        out_specs=[here] * (len(GRAD_NAMES) + 1),
        scratch_shapes=scratch,
        compiler_params=pltpu.CompilerParams(
            collective_id=2, has_side_effects=True, vmem_limit_bytes=62 * 2**20
        ),
        name="weight_gradients",
    )(*lefts, *rights, packed)
    grads = {
        m: o.reshape(ROWS[m], COLS[m]).astype(F32) for m, o in zip(GRAD_NAMES, out[:-1])
    }
    flat = out[-1][:, 0].reshape(4, 2, 128)[:, :, :96].reshape(768)
    return grads, flat


def norm_rows(values, scale_vec, shift_vec):
    center = values - jnp.mean(values, axis=-1, keepdims=True)
    spread = jnp.mean(center * center, axis=-1, keepdims=True)
    inverse = lax.rsqrt(spread + epsilon)
    normed = center * inverse
    return (normed * scale_vec + shift_vec, normed, inverse)


def norm_back(grad_out, normed, inverse, scale_vec):
    scaled = grad_out * scale_vec
    centered = scaled - jnp.mean(scaled, axis=-1, keepdims=True)
    return inverse * (centered - normed * jnp.mean(scaled * normed, axis=-1, keepdims=True))


def left_product(left_op, right_op):
    return lax.dot_general(
        left_op, right_op, (((0,), (0,)), ((), ())), preferred_element_type=jnp.float32
    )


def right_product(left_op, right_op):
    return lax.dot_general(
        left_op, right_op, (((1,), (1,)), ((), ())), preferred_element_type=jnp.float32
    )


def attend_items(packed):
    length = packed.shape[1]
    local_width = packed.shape[-1]
    heads_local = local_width // HD
    block_rows = min(512, length)
    block_count = length // block_rows

    def one_sequence(single):
        queries = single[:, 0, 0].reshape(block_count, block_rows, heads_local, HD)
        keys_all = single[:, 1, 0].reshape(length, heads_local, HD)
        values_all = single[:, 2, 0].reshape(length, heads_local, HD)

        def one_one_block(query_part):
            scores = (
                jnp.einsum("qhd,khd->hqk", query_part, keys_all, preferred_element_type=jnp.float32)
                * 0.125
            )
            row_peak = jnp.max(scores, axis=-1, keepdims=True)
            raised = jnp.exp(scores - row_peak)
            row_total = jnp.sum(raised, axis=-1, keepdims=True)
            attn_probs = (raised / row_total).astype(jnp.bfloat16)
            context = jnp.einsum(
                "hqk,khd->qhd", attn_probs, values_all, preferred_element_type=jnp.float32
            )
            log_total = (row_peak + jnp.log(row_total))[..., 0]
            return (context.astype(jnp.bfloat16).reshape(block_rows, local_width), log_total)

        context, log_total = lax.map(one_one_block, queries)
        return (context.reshape(length, local_width), log_total)

    context, log_total = lax.map(one_sequence, packed)
    return (context, log_total, packed)


def attend_back(triple):
    single, log_total, grad_ctx = triple
    length = single.shape[0]
    local_width = single.shape[-1]
    heads_local = local_width // HD
    block_rows = min(512, length)
    block_count = length // block_rows
    queries = single[:, 0, 0].reshape(block_count, block_rows, heads_local, HD)
    keys_all = single[:, 1, 0].reshape(length, heads_local, HD)
    values_all = single[:, 2, 0].reshape(length, heads_local, HD)
    grad_blocks = grad_ctx[:, 0].reshape(block_count, block_rows, heads_local, HD)

    def attend_one_block(carry, pieces):
        grad_keys, grad_values = carry
        query_part, grad_part, total_part = pieces
        scores = (
            jnp.einsum("qhd,khd->hqk", query_part, keys_all, preferred_element_type=jnp.float32)
            * 0.125
        )
        attn_probs = jnp.exp(scores - total_part[..., None])
        grad_probs = jnp.einsum(
            "qhd,khd->hqk", grad_part, values_all, preferred_element_type=jnp.float32
        )
        inner = jnp.sum(attn_probs * grad_probs, axis=-1, keepdims=True)
        grad_scores = (attn_probs * (grad_probs - inner)).astype(jnp.bfloat16)
        grad_query = (
            jnp.einsum("hqk,khd->qhd", grad_scores, keys_all, preferred_element_type=jnp.float32)
            * 0.125
        )
        grad_keys = (
            grad_keys
            + jnp.einsum(
                "hqk,qhd->khd", grad_scores, query_part, preferred_element_type=jnp.float32
            )
            * 0.125
        )
        grad_values = grad_values + jnp.einsum(
            "hqk,qhd->khd",
            attn_probs.astype(jnp.bfloat16),
            grad_part,
            preferred_element_type=jnp.float32,
        )
        return ((grad_keys, grad_values), grad_query)

    zero_state = jnp.zeros((length, heads_local, HD), jnp.float32)
    (grad_keys, grad_values), grad_query = lax.scan(
        attend_one_block, (zero_state, zero_state), (queries, grad_blocks, log_total)
    )
    stacked = jnp.stack(
        [
            grad_query.reshape(length, local_width),
            grad_keys.reshape(length, local_width),
            grad_values.reshape(length, local_width),
        ],
        axis=1,
    )
    return stacked.astype(jnp.bfloat16)[:, :, None, :]


SMALL = (
    ("bias_q", 64),
    ("bias_v", 64),
    ("bias_out", 64),
    ("gain_one", 64),
    ("shift_one", 64),
    ("bias_up", 256),
    ("bias_down", 64),
    ("gain_two", 64),
    ("shift_two", 64),
)


def on_device(
    tokens,
    cotangent,
    w_qkv,
    bias_q,
    bias_v,
    w_out,
    bias_out,
    gain_one,
    shift_one,
    w_up,
    bias_up,
    w_down,
    bias_down,
    gain_two,
    shift_two,
):
    num_seqs, slice_len, model_width = tokens.shape
    groups = lax.axis_size("sp")
    row_count = num_seqs * slice_len
    local_width = model_width // groups
    inputs = tokens.reshape(row_count, model_width)
    own = dict(
        bias_q=bias_q,
        bias_v=bias_v,
        bias_out=bias_out,
        gain_one=gain_one,
        shift_one=shift_one,
        bias_up=bias_up,
        bias_down=bias_down,
        gain_two=gain_two,
        shift_two=shift_two,
    )
    packed = jnp.concatenate([own[k] for k, _ in SMALL]).reshape(3, 256)
    packed = jnp.pad(packed, ((0, 13), (0, 0)))
    small, full_qkv, full_out, full_up, full_down = gather_parameters(
        [packed, w_qkv, w_out, w_up, w_down]
    )
    small = small.reshape(16, 16, 256)[:, :3].reshape(16, 768).astype(F32)
    vec, at = {}, 0
    for k, n in SMALL:
        vec[k] = small[:, at : at + n].reshape(16 * n)
        at += n
    projected = jnp.dot(inputs, full_qkv, preferred_element_type=F32)
    bias_row = jnp.concatenate([vec["bias_q"], jnp.zeros((model_width,), F32), vec["bias_v"]])
    qkv_low = (
        (projected + bias_row).astype(BF).reshape(num_seqs, slice_len, 3, groups, local_width)
    )
    context_heads, log_total, qkv_heads = attend_items(
        lax.all_to_all(qkv_low, "sp", split_axis=3, concat_axis=1, tiled=True)
    )
    context_tokens = lax.all_to_all(
        context_heads.reshape(num_seqs, slice_len * groups, 1, local_width),
        "sp",
        split_axis=1,
        concat_axis=2,
        tiled=True,
    ).reshape(row_count, model_width)
    branch = jnp.dot(context_tokens, full_out, preferred_element_type=F32) + vec["bias_out"]
    normed_one, hat_one, inv_one = norm_rows(
        inputs.astype(F32) + branch, vec["gain_one"], vec["shift_one"]
    )
    normed_low = normed_one.astype(BF)
    pre_act = jnp.dot(normed_low, full_up, preferred_element_type=F32) + vec["bias_up"]
    act_low = jax.nn.gelu(pre_act, approximate=False).astype(BF)
    ffn_out = jnp.dot(act_low, full_down, preferred_element_type=F32) + vec["bias_down"]
    normed_two, hat_two, inv_two = norm_rows(
        normed_one + ffn_out, vec["gain_two"], vec["shift_two"]
    )
    output = normed_two.astype(BF).reshape(tokens.shape)
    grad_out = cotangent.reshape(row_count, model_width).astype(F32)
    gs = {}
    gs["gain_two"] = jnp.sum(grad_out * hat_two, axis=0)
    gs["shift_two"] = jnp.sum(grad_out, axis=0)
    grad_sum_two = norm_back(grad_out, hat_two, inv_two, vec["gain_two"])
    grad_ffn_low = grad_sum_two.astype(BF)
    gs["bias_down"] = jnp.sum(grad_ffn_low.astype(F32), axis=0)
    grad_act = right_product(grad_ffn_low, full_down)
    cdf_part = 0.5 * (1.0 + lax.erf(pre_act * root_half))
    slope = cdf_part + pre_act * jnp.exp(-0.5 * pre_act * pre_act) * inv_root_two_pi
    grad_pre_low = (grad_act * slope).astype(BF)
    gs["bias_up"] = jnp.sum(grad_pre_low.astype(F32), axis=0)
    grad_normed_one = grad_sum_two + right_product(grad_pre_low, full_up)
    gs["gain_one"] = jnp.sum(grad_normed_one * hat_one, axis=0)
    gs["shift_one"] = jnp.sum(grad_normed_one, axis=0)
    grad_sum_one = norm_back(grad_normed_one, hat_one, inv_one, vec["gain_one"])
    grad_branch_low = grad_sum_one.astype(BF)
    gs["bias_out"] = jnp.sum(grad_branch_low.astype(F32), axis=0)
    grad_context = right_product(grad_branch_low, full_out).astype(BF)
    grad_heads = lax.all_to_all(
        grad_context.reshape(num_seqs, slice_len, groups, local_width),
        "sp",
        split_axis=2,
        concat_axis=1,
        tiled=True,
    )
    grad_qkv_heads = lax.map(attend_back, (qkv_heads, log_total, grad_heads))
    grad_qkv = lax.all_to_all(
        grad_qkv_heads, "sp", split_axis=1, concat_axis=3, tiled=True
    ).reshape(row_count, 3 * model_width)
    gs["bias_q"] = jnp.sum(grad_qkv[:, :model_width].astype(F32), axis=0)
    gs["bias_v"] = jnp.sum(grad_qkv[:, 2 * model_width :].astype(F32), axis=0)
    grad_inputs = grad_sum_one + right_product(grad_qkv, full_qkv)
    grads, flat = weight_gradients(
        {
            "up": (normed_low, grad_pre_low),
            "down": (act_low, grad_ffn_low),
            "qkv": (inputs, grad_qkv),
            "out": (context_tokens, grad_branch_low),
        },
        jnp.concatenate([gs[k].reshape(16, n) for k, n in SMALL], axis=1),
    )
    res, at = {}, 0
    for k, n in SMALL:
        res[k] = flat[at : at + n]
        at += n
    return (
        output,
        grad_inputs.astype(BF).reshape(tokens.shape),
        grads["qkv"],
        res["bias_q"],
        res["bias_v"],
        grads["out"],
        res["bias_out"],
        res["gain_one"],
        res["shift_one"],
        grads["up"],
        res["bias_up"],
        grads["down"],
        res["bias_down"],
        res["gain_two"],
        res["shift_two"],
    )


def solution(mesh):
    rows, vector = P("fsdp", None), P("fsdp")
    block = P("fsdp", "sp", None)
    params = (rows, vector, vector, rows, vector, vector, vector)
    params += (rows, vector, rows, vector, vector, vector)
    return jax.shard_map(
        on_device,
        mesh=mesh,
        in_specs=(block, block) + params,
        out_specs=(block, block) + params,
        check_vma=False,
    )
```

```python
import functools
import math

import jax
import jax.numpy as jnp
from jax import lax
from jax.experimental import pallas as pl
from jax.experimental.pallas import tpu as pltpu
from jax.sharding import PartitionSpec as P

HD = 64
MESH = pl.DeviceIdType.MESH
BF = jnp.bfloat16
F32 = jnp.float32

epsilon = 1e-05
root_half = 0.7071067811865476
inv_root_two_pi = 0.3989422804014327


class Place:
    def __init__(self):
        f = lax.axis_index("fsdp")
        s = lax.axis_index("sp")
        self.xh, self.xl, self.y, self.z, self.c = s // 4, f // 8, (f // 2) % 4, s % 4, f % 2
        self.x = 2 * self.xh + self.xl

    def to(self, dx=0, dy=0, dz=0, dc=0):
        x = lax.rem(self.x + dx + 4, 4)
        y = lax.rem(self.y + dy + 4, 4)
        z = lax.rem(self.z + dz + 4, 4)
        c = self.c if dc == 0 else 1 - self.c
        return ((x % 2) * 8 + y * 2 + c, (x // 2) * 4 + z)


class Copies:
    def __init__(self, send, recv):
        self.send, self.recv, self.n = send, recv, 0

    def remote(self, src, dst, dev):
        i = self.n
        self.n += 1
        cp = pltpu.make_async_remote_copy(
            src_ref=src,
            dst_ref=dst,
            send_sem=self.send.at[i],
            recv_sem=self.recv.at[i],
            device_id=dev,
            device_id_type=MESH,
        )
        cp.start()
        return cp

    def local(self, src, dst):
        i = self.n
        self.n += 1
        cp = pltpu.make_async_copy(src, dst, self.recv.at[i])
        cp.start()
        return cp


def greet(targets):
    bar = pltpu.get_barrier_semaphore()
    for t in targets:
        pl.semaphore_signal(bar, inc=1, device_id=t, device_id_type=MESH)
    pl.semaphore_wait(bar, len(targets))


class Gather:
    def __init__(self, place, copies, src, out, lo, n, quarters):
        self.p, self.s, self.src, self.out = place, copies, src, out
        self.lo, self.n, self.quarters = lo, n, quarters
        self.sent, self.core = [], []

    def cols(self, half=None):
        if half is None:
            return pl.ds(self.lo, self.n)
        return pl.ds(self.lo + half * (self.n // 2), self.n // 2)

    def go(self, src, dst, **k):
        cp = self.s.remote(src, dst, self.p.to(**k))
        self.sent.append(cp)
        return cp

    def q(self):
        return self.p.z if self.quarters else slice(None)

    def start(self):
        p, o, q = self.p, self.out, self.q()
        self.own = self.s.local(
            self.src.at[:, :, self.cols()], o.at[p.xl, p.y, p.c, :, :, self.cols()]
        )
        self.ycp = [
            self.go(
                self.src.at[q, :, self.cols()], o.at[p.xl, p.y, p.c, q, :, self.cols()], dy=k
            )
            for k in (1, 3, 2)
        ]
        self.xcp = [
            self.go(
                self.src.at[q, :, self.cols(h)], o.at[p.xl, p.y, p.c, q, :, self.cols(h)], dx=dx
            )
            for h, dx in ((0, 1), (1, -1))
        ]

    def stage_x(self):
        p, o, q = self.p, self.out, self.q()
        for k, cp in zip((3, 1, 2), self.ycp):
            cp.wait_recv()
            for h, dx in ((0, 1), (1, -1)):
                r = o.at[p.xl, lax.rem(p.y + k, 4), p.c, q, :, self.cols(h)]
                self.xcp.append(self.go(r, r, dx=dx))
        if self.quarters:
            self.zcp = []
            for dz in (1, 3, 2):
                for k in (1, 2, 3):
                    r = o.at[p.xl, lax.rem(p.y + k, 4), p.c, q, :, self.cols()]
                    self.zcp.append(self.go(r, r, dz=dz))
        else:
            self.own.wait()
            r = o.at[p.xl, :, p.c, :, :, self.cols()]
            self.core.append(self.go(r, r, dc=1))

    def stage_z(self):
        if not self.quarters:
            return
        p, o, q = self.p, self.out, self.q()
        for cp in self.xcp:
            cp.wait_recv()
        for dz in (1, 3, 2):
            r = o.at[1 - p.xl, :, p.c, q, :, self.cols()]
            self.zcp.append(self.go(r, r, dz=dz))

    def stage_core(self):
        p, o = self.p, self.out
        if self.quarters:
            for cp in self.zcp:
                cp.wait_recv()
            self.own.wait()
            r = o.at[p.xl, :, p.c, :, :, self.cols()]
            self.core.append(self.go(r, r, dc=1))
        else:
            for cp in self.xcp:
                cp.wait_recv()
        r = o.at[1 - p.xl, :, p.c, :, :, self.cols()]
        self.core.append(self.go(r, r, dc=1))

    def arrived(self):
        for cp in self.core:
            cp.wait_recv()
        self.core = []

    def finish(self):
        self.arrived()
        for cp in self.sent:
            cp.wait_send()


class Reduce:
    def __init__(self, place, copies, order, g, bufs, total):
        self.p, self.s, self.order, self.g = place, copies, order, g
        self.r1, self.s1, self.r2, self.s2, self.r3 = bufs
        self.tot = total
        self.n = g.shape[-1]
        self.sent = []

    def go(self, src, dst, **k):
        cp = self.s.remote(src, dst, self.p.to(**k))
        self.sent.append(cp)
        return cp

    def half(self, xh):
        m = self.n // 2
        return pl.ds(pl.multiple_of(xh * m, 128), m)

    def me(self, i):
        return {"x": self.p.x, "y": self.p.y, "z": self.p.z}[self.order[i]]

    def pick(self, ref, i, v):
        o, ax = self.order, self.order[i]
        if ax == "x":
            rest = [slice(None)] * (len(ref.shape) - 2)
            return ref.at[(lax.rem(v, 2),) + tuple(rest) + (self.half(v // 2),)]
        lead = 0 if "x" in o[:i] else 1
        if ax == "z" and "y" not in o[:i]:
            lead += 1
        return ref.at[(slice(None),) * lead + (v,)]

    def scatter(self, i, src, recv):
        me = self.me(i)
        return [
            self.go(
                self.pick(src, i, lax.rem(me + k, 4)), recv.at[k - 1], **{"d" + self.order[i]: k}
            )
            for k in (1, 3, 2)
        ]

    def add(self, i, src, recv, out, cps):
        for cp in cps:
            cp.wait_recv()
        own = self.pick(src, i, self.me(i))
        shape = out.shape
        rows = (slice(None), slice(None))

        def one(idx):
            acc = own[idx].astype(F32)
            for k in range(3):
                acc = acc + recv[(k,) + idx].astype(F32)
            out[idx] = acc.astype(out.dtype)

        if len(shape) == 2:
            one(rows)
            return

        def body(j, _):
            idx = []
            for d in reversed(shape[:-2]):
                idx.insert(0, lax.rem(j, d))
                j = j // d
            one(tuple(idx) + rows)
            return 0

        lax.fori_loop(0, math.prod(shape[:-2]), body, 0)

    def first(self):
        self.c1 = self.scatter(0, self.g, self.r1)

    def second(self):
        self.add(0, self.g, self.r1, self.s1, self.c1)
        self.c2 = self.scatter(1, self.s1, self.r2)

    def third(self):
        self.add(1, self.s1, self.r2, self.s2, self.c2)
        self.c3 = self.scatter(2, self.s2, self.r3)

    def share(self):
        p = self.p
        mine = self.tot.at[p.z, :, self.half(p.xh)]
        self.add(2, self.s2, self.r3, mine, self.c3)
        self.c4 = self.go(mine, mine, dx=2)

    def spread(self):
        self.c4.wait_recv()
        r = self.tot.at[self.p.z]
        self.c5 = [self.go(r, r, dz=k) for k in (1, 3, 2)]

    def done(self):
        for cp in self.c5:
            cp.wait_recv()

    def finish(self):
        for cp in self.sent:
            cp.wait_send()


def reduce_shapes(order, q, n):
    full = {"x": 2, "y": 4, "z": 4}
    left, width, out = ["x", "y", "z"], n, []
    for i, ax in enumerate(order):
        left.remove(ax)
        if ax == "x":
            width = n // 2
        s = tuple(full[a] for a in left) + (q, width)
        out.append((3,) + s)
        if i < 2:
            out.append(s)
    return out


def run_pipe(steps, offsets, count):
    for t in range(count + max(offsets)):
        for step, d in zip(steps, offsets):
            if 0 <= t - d < count:
                step(t - d)


ROWS = {"small": 16, "out": 64, "up": 64, "down": 256}
COLS = {"small": 256, "out": 1024, "up": 4096, "down": 1024}
GATHER_NAMES = ("small", "out", "up", "down")
GATHER_PARTS = (
    ("small", 0, 256, False),
    ("out", 0, 1024, False),
    ("up", 0, 1024, True),
    ("up", 1024, 1024, False),
    ("up", 2048, 1024, True),
    ("up", 3072, 1024, False),
    ("down", 0, 512, False),
    ("down", 512, 512, False),
)
ANYWHERE = pl.BlockSpec(memory_space=pl.ANY)
INSIDE = pl.BlockSpec(memory_space=pltpu.VMEM)


def quarters_of(m):
    return 1 if m == "small" else 4


def flat_pipe(steps, offsets, count):
    out = []
    for t in range(count + max(offsets)):
        for step, d in zip(steps, offsets):
            if 0 <= t - d < count:
                out.append(functools.partial(step, t - d))
    return out


def advance(queue, n):
    for _ in range(min(n, len(queue))):
        queue.pop(0)()


def sp_peers(p):
    out = []
    for dx, dz in ((0, 1), (0, 3), (2, 0), (2, 1), (2, 3), (0, 2), (2, 2)):
        xh = p.xh if dx == 0 else 1 - p.xh
        out.append((p.to(dx=dx, dz=dz), xh * 4 + lax.rem(p.z + dz, 4)))
    return out


def nt(a, b):
    return lax.dot_general(a, b, (((1,), (1,)), ((), ())), preferred_element_type=F32)


def nn(a, b):
    return jnp.dot(a, b, preferred_element_type=F32)


def forward_kernel(*refs):
    refs = list(refs)

    def take(n):
        head = refs[:n]
        del refs[:n]
        return head

    k = len(GATHER_NAMES)
    tok, wq = take(2)
    ins = dict(zip(GATHER_NAMES, take(k)))
    outs = dict(zip(GATHER_NAMES, take(k)))
    tall, wsel, qkv, lse, ctx = take(5)
    small_v, vt, ct, ch, cr = take(5)
    p, s = Place(), Copies(*refs)
    me = p.xh * 4 + p.z
    peers = sp_peers(p)
    greet(
        [p.to(dy=1), p.to(dy=2), p.to(dy=3), p.to(dx=1), p.to(dx=3), p.to(dc=1)]
        + [d for d, _ in peers]
    )
    sent = []

    def go(src, dst, dev):
        cp = s.remote(src, dst, dev)
        sent.append(cp)
        return cp

    pick = [
        s.local(
            wq.at[:, pl.ds(pl.multiple_of(j * 1024 + me * 128, 128), 128)],
            wsel.at[p.xl, p.y, p.c, :, pl.ds(j * 128, 128)],
        )
        for j in range(3)
    ]
    own_tok = s.local(tok, tall.at[me])
    tok_cps = [go(tok, tall.at[me], d) for d, _ in peers]
    parts = [Gather(p, s, ins[m], outs[m], lo, n, quarters) for m, lo, n, quarters in GATHER_PARTS]
    parts[0].start()
    for cp in pick:
        cp.wait()
    mine = wsel.at[p.xl, p.y, p.c]
    wy = [go(mine, mine, p.to(dy=d)) for d in (1, 3, 2)]
    queue = flat_pipe(
        (
            lambda i: parts[i + 1].start(),
            lambda i: parts[i + 1].stage_x(),
            lambda i: parts[i + 1].stage_z(),
            lambda i: parts[i + 1].stage_core(),
        ),
        (0, 3, 5, 6),
        len(parts) - 1,
    )
    advance(queue, 2)
    for cp in wy:
        cp.wait_recv()
    column = wsel.at[p.xl, :, p.c]
    wx = go(column, column, p.to(dx=1 - 2 * p.xl))
    parts[0].stage_x()
    advance(queue, 1)
    wx.wait_recv()
    plane = wsel.at[:, :, p.c]
    wc = go(plane, plane, p.to(dc=1))
    parts[0].stage_core()
    advance(queue, 1)
    parts[0].arrived()
    small_cp = s.local(outs["small"], small_v)
    advance(queue, 2)
    wc.wait_recv()
    small_cp.wait()
    own_tok.wait()
    for cp in tok_cps:
        cp.wait_recv()

    even, odd = 2 * me, 2 * me + 1
    qv = (
        small_v[even // 8, (even // 2) % 4, even % 2, 0, 3:4, :].astype(F32)
        + small_v[odd // 8, (odd // 2) % 4, odd % 2, 0, 4:5, :].astype(F32)
    )
    bias = jnp.concatenate([qv[:, :128], jnp.zeros((1, 128), F32), qv[:, 128:]], axis=1)

    def project(i, _):
        x = tall[pl.ds(2 * i, 2)].reshape(256, 1024)
        v = nn(x, wsel[...].reshape(1024, 384)) + bias
        qkv[pl.ds(pl.multiple_of(i * 256, 256), 256), :] = v.astype(BF)
        return 0

    lax.fori_loop(0, 4, project, 0)
    vt[...] = qkv[:, 256:384].astype(F32).T.astype(BF)
    per = max(1, (len(queue) - 4) // 4)
    for b in range(4):
        rows = pl.ds(b * 256, 256)
        for h in range(2):
            keys = qkv[:, 128 + 64 * h : 192 + 64 * h]
            st = nt(keys, qkv[rows, 64 * h : 64 * h + 64]) * 0.125
            peak = jnp.max(st, axis=0, keepdims=True)
            e = jnp.exp(st - peak)
            total = jnp.sum(e, axis=0, keepdims=True)
            c = nn(vt[64 * h : 64 * h + 64, :], e.astype(BF))
            ct[64 * h : 64 * h + 64, rows] = c / total
            lse[h : h + 1, rows] = peak + jnp.log(total)
        advance(queue, per)
    for t in range(8):
        ch[t] = ct[:, t * 128 : (t + 1) * 128].T.astype(BF)
    ctx_cps = [go(ch.at[t], cr.at[me], d) for d, t in peers]
    cr[me] = ch[me]
    advance(queue, len(queue))
    for cp in ctx_cps:
        cp.wait_recv()
    for t in range(8):
        ctx[:, t * 128 : (t + 1) * 128] = cr[t]
    for g in parts:
        g.finish()
    for cp in sent:
        cp.wait_send()


def attend_forward(tokens, w_qkv, arrays):
    ins, shapes = [], []
    for m, a in zip(GATHER_NAMES, arrays):
        q = quarters_of(m)
        a = a.reshape(q, ROWS[m] // q, COLS[m])
        ins.append(a)
        shapes.append(jax.ShapeDtypeStruct((2, 4, 2) + a.shape, BF))
    k = len(ins)
    shapes += [
        jax.ShapeDtypeStruct((8, 128, 1024), BF),
        jax.ShapeDtypeStruct((2, 4, 2, 64, 384), BF),
        jax.ShapeDtypeStruct((1024, 384), BF),
        jax.ShapeDtypeStruct((8, 1024), F32),
        jax.ShapeDtypeStruct((128, 1024), BF),
    ]
    out = pl.pallas_call(
        forward_kernel,
        out_shape=shapes,
        in_specs=[ANYWHERE] * (2 + k),
        out_specs=[ANYWHERE] * k + [INSIDE] * 5,
        scratch_shapes=[
            pltpu.VMEM((2, 4, 2, 1, 16, 256), BF),
            pltpu.VMEM((128, 1024), BF),
            pltpu.VMEM((128, 1024), F32),
            pltpu.VMEM((8, 128, 128), BF),
            pltpu.VMEM((8, 128, 128), BF),
            pltpu.SemaphoreType.DMA((200,)),
            pltpu.SemaphoreType.DMA((200,)),
        ],
        compiler_params=pltpu.CompilerParams(
            collective_id=1, has_side_effects=True, vmem_limit_bytes=40 * 2**20
        ),
        name="attend_forward",
    )(tokens, w_qkv, *ins)
    return [o.reshape(16 * ROWS[m], COLS[m]) for m, o in zip(GATHER_NAMES, out)] + list(out[k:])


SMALL_SHAPE = (2, 4, 4, 8, 256)


class Products:
    def __init__(self, place, copies, left, right, both_left, both_right, totals, pieces, g, bufs):
        self.p, self.s = place, copies
        self.left, self.right = left, right
        self.both_left, self.both_right = both_left, both_right
        self.pieces, self.g = pieces, g
        self.swaps, self.ready = {}, set()
        self.red = [
            Reduce(place, copies, o, gi, b, totals[m].at[:, :, pl.ds(lo, n)])
            for (m, lo, n, o), gi, b in zip(pieces, g, bufs)
        ]

    def swap(self, m):
        p, s = self.p, self.s
        here = [
            s.local(self.left[m].at[:, :, p.c], self.both_left[m].at[:, :, :, pl.ds(0, 128)]),
            s.local(self.right[m], self.both_right[m].at[pl.ds(0, 128)]),
        ]
        there = [
            s.remote(
                self.left[m].at[:, :, 1 - p.c],
                self.both_left[m].at[:, :, :, pl.ds(128, 128)],
                p.to(dc=1),
            ),
            s.remote(self.right[m], self.both_right[m].at[pl.ds(128, 128)], p.to(dc=1)),
        ]
        self.swaps[m] = (here, there)

    def begin(self, i):
        m, lo, n, _ = self.pieces[i]
        if m not in self.ready:
            for cp in self.swaps[m][0]:
                cp.wait()
            for cp in self.swaps[m][1]:
                cp.wait_recv()
            self.ready.add(m)
        left, right, g = self.both_left[m], self.both_right[m], self.g[i]
        rows = left.shape[2]
        tile = min(512, n)

        def body(j, _):
            b, t = j // (n // tile), lax.rem(j, n // tile)
            c0 = pl.multiple_of(lo + t * tile, tile)
            v = jnp.dot(
                left[b].reshape(4 * rows, 256),
                right[:, pl.ds(c0, tile)],
                preferred_element_type=F32,
            ).astype(BF)
            g[b, :, :, :, pl.ds(pl.multiple_of(t * tile, tile), tile)] = v.reshape(
                4, 4, rows // 4, tile
            )
            return 0

        lax.fori_loop(0, 2 * (n // tile), body, 0)
        self.red[i].first()

    def finish(self):
        for r in self.red:
            r.finish()
        for m in self.swaps:
            for cp in self.swaps[m][1]:
                cp.wait_send()


def piece_scratch(pieces):
    sc = []
    for m, _, n, o in pieces:
        q = ROWS[m] // 4
        sc.append(pltpu.VMEM((2, 4, 4, q, n), BF))
        sc += [pltpu.VMEM(x, BF) for x in reduce_shapes(o, q, n)]
    return sc


PIECES = (
    ("down", 0, 512, "yzx"),
    ("up", 0, 1024, "xyz"),
    ("down", 512, 512, "zxy"),
    ("up", 1024, 1024, "yzx"),
    ("up", 2048, 1024, "zxy"),
    ("up", 3072, 1024, "xyz"),
    ("out", 0, 1024, "yzx"),
)
GRAD_NAMES = ("down", "up", "out")


def backward_kernel(*refs):
    refs = list(refs)

    def take(n):
        head = refs[:n]
        del refs[:n]
        return head

    k = len(GRAD_NAMES)
    left = dict(zip(GRAD_NAMES, take(k)))
    right = dict(zip(GRAD_NAMES, take(k)))
    small, gctx, gsum, tall_t, wsel, qkv, lse = take(7)
    totals = dict(zip(GRAD_NAMES, take(k)))
    small_total, grad_tok, gw = take(3)
    both_left = dict(zip(GRAD_NAMES, take(k)))
    both_right = dict(zip(GRAD_NAMES, take(k)))
    small_src, small_in, small_g = take(3)
    small_bufs = take(5)
    g, bufs = [], []
    for _ in PIECES:
        g += take(1)
        bufs.append(take(5))
    do, kt, dqt, dkv, dqkv, gq, gq_c, gq_x, gq_y, dts, dtr = take(11)
    p, s = Place(), Copies(*refs)
    me = p.xh * 4 + p.z
    peers = sp_peers(p)
    greet(
        [p.to(dy=1), p.to(dy=2), p.to(dy=3), p.to(dx=1), p.to(dx=3), p.to(dc=1)]
        + [d for d, _ in peers]
    )
    sent = []

    def go(src, dst, dev):
        cp = s.remote(src, dst, dev)
        sent.append(cp)
        return cp

    do_cps = [
        go(gctx.at[:, pl.ds(pl.multiple_of(t * 128, 128), 128)], do.at[me], d) for d, t in peers
    ]
    do_own = s.local(gctx.at[:, pl.ds(pl.multiple_of(me * 128, 128), 128)], do.at[me])
    prod = Products(p, s, left, right, both_left, both_right, totals, PIECES, g, bufs)
    for m in GRAD_NAMES:
        prod.swap(m)
    kt[...] = qkv[:, 128:256].astype(F32).T.astype(BF)
    red = prod.red
    n = len(PIECES)
    for i in range(n):
        prod.begin(i)
    queue = flat_pipe(
        (
            lambda i: red[i].second(),
            lambda i: red[i].third(),
            lambda i: red[i].share(),
            lambda i: red[i].spread(),
            lambda i: red[i].done(),
        ),
        (0, 2, 4, 5, 6),
        n,
    )
    do_own.wait()
    for cp in do_cps:
        cp.wait_recv()
    dkv[...] = jnp.zeros_like(dkv)
    for b in range(4):
        rows = pl.ds(b * 256, 256)
        for h in range(2):
            lanes = slice(64 * h, 64 * h + 64)
            keys = qkv[:, 128 + 64 * h : 192 + 64 * h]
            vals = qkv[:, 256 + 64 * h : 320 + 64 * h]
            q = qkv[rows, lanes]
            dob = do[2 * b : 2 * b + 2].reshape(256, 128)[:, lanes]
            probs = jnp.exp(nt(keys, q) * 0.125 - lse[h : h + 1, rows])
            dp = nt(vals, dob)
            inner = jnp.sum(probs * dp, axis=0, keepdims=True)
            ds = (probs * (dp - inner)).astype(BF)
            dqt[lanes, rows] = nn(kt[lanes, :], ds) * 0.125
            dkv[:, lanes] += nn(ds, q) * 0.125
            dkv[:, 128 + 64 * h : 192 + 64 * h] += nn(probs.astype(BF), dob)
        if b >= 1:
            advance(queue, 1)
    dqkv[:, :128] = dqt[...].T.astype(BF)
    dqkv[:, 128:] = dkv[...].astype(BF)

    def part(i, _):
        rows = pl.ds(pl.multiple_of(i * 256, 256), 256)
        v = nt(dqkv[rows, :], wsel[...].reshape(1024, 384)).astype(BF)
        dts[pl.ds(2 * i, 2)] = v.reshape(2, 128, 1024)
        return 0

    lax.fori_loop(0, 4, part, 0)
    dt_cps = [go(dts.at[t], dtr.at[me], d) for d, t in peers]

    def rows_of(i, _):
        v = nn(tall_t[pl.ds(pl.multiple_of(i * 256, 256), 256), :], dqkv[...])
        gq[pl.ds(2 * i, 2)] = v.astype(BF).reshape(2, 2, 64, 384)
        return 0

    lax.fori_loop(0, 4, rows_of, 0)
    c_cp = go(gq.at[:, 1 - p.c], gq_c, p.to(dc=1))

    cols = jnp.sum(dqkv[...].astype(F32), axis=0, keepdims=True)
    both = jnp.broadcast_to(jnp.concatenate([cols[:, :128], cols[:, 256:]], axis=1), (8, 256))
    low = lax.broadcasted_iota(jnp.int32, (8, 256), 1) % 128 < 64
    small_src[...] = small[...]
    for c, v in ((0, both), (1, pltpu.roll(both, 192, 1))):
        at = (me // 4, me % 4, c, 0)
        small_src[at] = small_src[at] + jnp.where(low, v, 0.0)
    small_swap = s.remote(small_src.at[:, :, 1 - p.c], small_in, p.to(dc=1))
    small_red = Reduce(p, s, "xyz", small_g, small_bufs, small_total)
    advance(queue, 2)
    small_swap.wait_recv()
    for i in range(2):
        for j in range(4):
            small_g[i, j] = small_src[i, j, p.c] + small_in[i, j]
    small_red.first()

    c_cp.wait_recv()

    def add_core(i, _):
        gq_c[i] = (gq_c[i].astype(F32) + gq[i, p.c].astype(F32)).astype(BF)
        return 0

    lax.fori_loop(0, 8, add_core, 0)
    x_cp = go(gq_c.at[pl.ds((1 - p.xl) * 4, 4)], gq_x, p.to(dx=1 - 2 * p.xl))
    advance(queue, 3)
    small_red.second()
    x_cp.wait_recv()

    def add_x(i, _):
        gq_x[i] = (gq_x[i].astype(F32) + gq_c[p.xl * 4 + i].astype(F32)).astype(BF)
        return 0

    lax.fori_loop(0, 4, add_x, 0)
    y_cps = [go(gq_x.at[lax.rem(p.y + d, 4)], gq_y.at[d - 1], p.to(dy=d)) for d in (1, 3, 2)]
    advance(queue, 3)
    small_red.third()
    for cp in y_cps:
        cp.wait_recv()
    acc = gq_x[p.y].astype(F32)
    for i in range(3):
        acc = acc + gq_y[i].astype(F32)
    gw[me] = acc.astype(BF)
    gw_cps = [go(gw.at[me], gw.at[me], d) for d, _ in peers]
    advance(queue, 3)
    small_red.share()
    for cp in dt_cps:
        cp.wait_recv()
    dtr[me] = dts[me]
    acc = gsum[...]
    for t in range(8):
        acc = acc + dtr[t].astype(F32)
    grad_tok[...] = acc.astype(BF)
    small_red.spread()
    advance(queue, len(queue))
    for cp in gw_cps:
        cp.wait_recv()
    small_red.done()
    prod.finish()
    small_red.finish()
    small_swap.wait_send()
    for cp in sent:
        cp.wait_send()


SMALL = (
    ("bias_q", 64),
    ("bias_v", 64),
    ("bias_out", 64),
    ("gain_one", 64),
    ("shift_one", 64),
    ("bias_up", 256),
    ("bias_down", 64),
    ("gain_two", 64),
    ("shift_two", 64),
)
SMALL_LAYOUT = ("bias_q", "bias_out", "bias_v", "gain_one", "bias_up", "shift_one", "bias_down")
SMALL_LAYOUT += ("gain_two", "shift_two")


def pack_small(sums):
    width = dict(SMALL)
    cols = [
        sums[k].reshape(16, width[k]) if k in sums else jnp.zeros((16, width[k]), F32)
        for k in SMALL_LAYOUT
    ]
    v = jnp.concatenate(cols + [jnp.zeros((16, 256), F32)], axis=1)
    return jnp.pad(v.reshape(2, 4, 2, 4, 1, 256), ((0, 0),) * 4 + ((0, 7), (0, 0)))


def unpack_small(total):
    flat, at, out = total[:, 0].reshape(1024), 0, {}
    for k in SMALL_LAYOUT:
        out[k] = flat[at : at + dict(SMALL)[k]]
        at += dict(SMALL)[k]
    return out


def attend_backward(pairs, small, gctx, gsum, tall_t, wsel, qkv, lse):
    lefts = [pairs[m][0].T.reshape(2, 4, 2, ROWS[m], 128) for m in GRAD_NAMES]
    rights = [pairs[m][1] for m in GRAD_NAMES]
    packed = pack_small(small)
    scratch = [pltpu.VMEM((2, 4, ROWS[m], 256), BF) for m in GRAD_NAMES]
    scratch += [pltpu.VMEM((256, COLS[m]), BF) for m in GRAD_NAMES]
    scratch += [pltpu.VMEM((2, 4, 2, 4, 8, 256), F32)]
    scratch += [pltpu.VMEM(SMALL_SHAPE, F32)] * 2
    scratch += [pltpu.VMEM(x, F32) for x in reduce_shapes("xyz", 8, 256)]
    scratch += piece_scratch(PIECES)
    scratch += [
        pltpu.VMEM((8, 128, 128), BF),
        pltpu.VMEM((128, 1024), BF),
        pltpu.VMEM((128, 1024), F32),
        pltpu.VMEM((1024, 256), F32),
        pltpu.VMEM((1024, 384), BF),
        pltpu.VMEM((8, 2, 64, 384), BF),
        pltpu.VMEM((8, 64, 384), BF),
        pltpu.VMEM((4, 64, 384), BF),
        pltpu.VMEM((3, 64, 384), BF),
        pltpu.VMEM((8, 128, 1024), BF),
        pltpu.VMEM((8, 128, 1024), BF),
    ]
    scratch += [pltpu.SemaphoreType.DMA((250,)), pltpu.SemaphoreType.DMA((250,))]
    k = len(GRAD_NAMES)
    out = pl.pallas_call(
        backward_kernel,
        out_shape=[jax.ShapeDtypeStruct((4, ROWS[m] // 4, COLS[m]), BF) for m in GRAD_NAMES]
        + [
            jax.ShapeDtypeStruct((4, 8, 256), F32),
            jax.ShapeDtypeStruct((128, 1024), BF),
            jax.ShapeDtypeStruct((8, 64, 384), BF),
        ],
        in_specs=[ANYWHERE] * (2 * k) + [INSIDE, ANYWHERE] + [INSIDE] * 5,
        out_specs=[INSIDE] * (k + 3),
        scratch_shapes=scratch,
        compiler_params=pltpu.CompilerParams(
            collective_id=2, has_side_effects=True, vmem_limit_bytes=63 * 2**20
        ),
        name="attend_backward",
    )(*lefts, *rights, packed, gctx, gsum, tall_t, wsel, qkv, lse)
    grads = {m: o.reshape(ROWS[m], COLS[m]).astype(F32) for m, o in zip(GRAD_NAMES, out)}
    gw = out[k + 2].reshape(8, 64, 3, 128).transpose(1, 2, 0, 3)
    grads["qkv"] = gw.reshape(64, 3072).astype(F32)
    return grads, unpack_small(out[k]), out[k + 1]


def norm_rows(values, scale_vec, shift_vec):
    center = values - jnp.mean(values, axis=-1, keepdims=True)
    spread = jnp.mean(center * center, axis=-1, keepdims=True)
    inverse = lax.rsqrt(spread + epsilon)
    normed = center * inverse
    return (normed * scale_vec + shift_vec, normed, inverse)


def norm_back(grad_out, normed, inverse, scale_vec):
    scaled = grad_out * scale_vec
    centered = scaled - jnp.mean(scaled, axis=-1, keepdims=True)
    return inverse * (centered - normed * jnp.mean(scaled * normed, axis=-1, keepdims=True))


def right_product(left_op, right_op):
    return lax.dot_general(
        left_op, right_op, (((1,), (1,)), ((), ())), preferred_element_type=jnp.float32
    )


def on_device(
    tokens,
    cotangent,
    w_qkv,
    bias_q,
    bias_v,
    w_out,
    bias_out,
    gain_one,
    shift_one,
    w_up,
    bias_up,
    w_down,
    bias_down,
    gain_two,
    shift_two,
):
    num_seqs, slice_len, model_width = tokens.shape
    row_count = num_seqs * slice_len
    inputs = tokens.reshape(row_count, model_width)
    own = dict(
        bias_q=bias_q,
        bias_v=bias_v,
        bias_out=bias_out,
        gain_one=gain_one,
        shift_one=shift_one,
        bias_up=bias_up,
        bias_down=bias_down,
        gain_two=gain_two,
        shift_two=shift_two,
    )
    zero = jnp.zeros((64,), BF)
    packed = jnp.concatenate(
        [own[k] for k, _ in SMALL]
        + [bias_q, zero, bias_v, zero, zero, bias_q, zero, bias_v, jnp.zeros((11 * 256,), BF)]
    ).reshape(16, 256)
    small, full_out, full_up, full_down, tall, wsel, qkv, lse, context_tokens = attend_forward(
        inputs, w_qkv, [packed, w_out, w_up, w_down]
    )
    small = small.reshape(16, 16, 256)[:, :3].reshape(16, 768).astype(F32)
    vec, at = {}, 0
    for k, n in SMALL:
        vec[k] = small[:, at : at + n].reshape(16 * n)
        at += n
    branch = jnp.dot(context_tokens, full_out, preferred_element_type=F32) + vec["bias_out"]
    normed_one, hat_one, inv_one = norm_rows(
        inputs.astype(F32) + branch, vec["gain_one"], vec["shift_one"]
    )
    normed_low = normed_one.astype(BF)
    pre_act = jnp.dot(normed_low, full_up, preferred_element_type=F32) + vec["bias_up"]
    act_low = jax.nn.gelu(pre_act, approximate=False).astype(BF)
    ffn_out = jnp.dot(act_low, full_down, preferred_element_type=F32) + vec["bias_down"]
    normed_two, hat_two, inv_two = norm_rows(
        normed_one + ffn_out, vec["gain_two"], vec["shift_two"]
    )
    output = normed_two.astype(BF).reshape(tokens.shape)
    grad_out = cotangent.reshape(row_count, model_width).astype(F32)
    gs = {}
    gs["gain_two"] = jnp.sum(grad_out * hat_two, axis=0)
    gs["shift_two"] = jnp.sum(grad_out, axis=0)
    grad_sum_two = norm_back(grad_out, hat_two, inv_two, vec["gain_two"])
    grad_ffn_low = grad_sum_two.astype(BF)
    gs["bias_down"] = jnp.sum(grad_ffn_low.astype(F32), axis=0)
    grad_act = right_product(grad_ffn_low, full_down)
    cdf_part = 0.5 * (1.0 + lax.erf(pre_act * root_half))
    slope = cdf_part + pre_act * jnp.exp(-0.5 * pre_act * pre_act) * inv_root_two_pi
    grad_pre_low = (grad_act * slope).astype(BF)
    gs["bias_up"] = jnp.sum(grad_pre_low.astype(F32), axis=0)
    grad_normed_one = grad_sum_two + right_product(grad_pre_low, full_up)
    gs["gain_one"] = jnp.sum(grad_normed_one * hat_one, axis=0)
    gs["shift_one"] = jnp.sum(grad_normed_one, axis=0)
    grad_sum_one = norm_back(grad_normed_one, hat_one, inv_one, vec["gain_one"])
    grad_branch_low = grad_sum_one.astype(BF)
    gs["bias_out"] = jnp.sum(grad_branch_low.astype(F32), axis=0)
    grad_context = right_product(grad_branch_low, full_out).astype(BF)
    grads, res, grad_inputs = attend_backward(
        {
            "down": (act_low, grad_ffn_low),
            "up": (normed_low, grad_pre_low),
            "out": (context_tokens, grad_branch_low),
        },
        gs,
        grad_context,
        grad_sum_one,
        tall.reshape(1024, model_width).T,
        wsel,
        qkv,
        lse,
    )
    return (
        output,
        grad_inputs.reshape(tokens.shape),
        grads["qkv"],
        res["bias_q"],
        res["bias_v"],
        grads["out"],
        res["bias_out"],
        res["gain_one"],
        res["shift_one"],
        grads["up"],
        res["bias_up"],
        grads["down"],
        res["bias_down"],
        res["gain_two"],
        res["shift_two"],
    )


def solution(mesh):
    rows, vector = P("fsdp", None), P("fsdp")
    block = P("fsdp", "sp", None)
    params = (rows, vector, vector, rows, vector, vector, vector)
    params += (rows, vector, rows, vector, vector, vector)
    return jax.shard_map(
        on_device,
        mesh=mesh,
        in_specs=(block, block) + params,
        out_specs=(block, block) + params,
        check_vma=False,
    )
```

```python
import functools
import math

import jax
import jax.numpy as jnp
from jax import lax
from jax.experimental import pallas as pl
from jax.experimental.pallas import tpu as pltpu
from jax.sharding import PartitionSpec as P

HD = 64
MESH = pl.DeviceIdType.MESH
BF = jnp.bfloat16
F32 = jnp.float32

epsilon = 1e-05
root_half = 0.7071067811865476
inv_root_two_pi = 0.3989422804014327


class Place:
    def __init__(self):
        f = lax.axis_index("fsdp")
        s = lax.axis_index("sp")
        self.xh, self.xl, self.y, self.z, self.c = s // 4, f // 8, (f // 2) % 4, s % 4, f % 2
        self.x = 2 * self.xh + self.xl

    def to(self, dx=0, dy=0, dz=0, dc=0):
        x = lax.rem(self.x + dx + 4, 4)
        y = lax.rem(self.y + dy + 4, 4)
        z = lax.rem(self.z + dz + 4, 4)
        c = self.c if dc == 0 else 1 - self.c
        return ((x % 2) * 8 + y * 2 + c, (x // 2) * 4 + z)


class Copies:
    def __init__(self, send, recv):
        self.send, self.recv, self.n = send, recv, 0

    def remote(self, src, dst, dev):
        i = self.n
        self.n += 1
        cp = pltpu.make_async_remote_copy(
            src_ref=src,
            dst_ref=dst,
            send_sem=self.send.at[i],
            recv_sem=self.recv.at[i],
            device_id=dev,
            device_id_type=MESH,
        )
        cp.start()
        return cp

    def local(self, src, dst):
        i = self.n
        self.n += 1
        cp = pltpu.make_async_copy(src, dst, self.recv.at[i])
        cp.start()
        return cp


def greet(targets):
    bar = pltpu.get_barrier_semaphore()
    for t in targets:
        pl.semaphore_signal(bar, inc=1, device_id=t, device_id_type=MESH)
    pl.semaphore_wait(bar, len(targets))


class Gather:
    def __init__(self, place, copies, src, out, lo, n, quarters):
        self.p, self.s, self.src, self.out = place, copies, src, out
        self.lo, self.n, self.quarters = lo, n, quarters
        self.sent, self.core = [], []

    def cols(self, half=None):
        if half is None:
            return pl.ds(self.lo, self.n)
        return pl.ds(self.lo + half * (self.n // 2), self.n // 2)

    def go(self, src, dst, **k):
        cp = self.s.remote(src, dst, self.p.to(**k))
        self.sent.append(cp)
        return cp

    def q(self):
        return self.p.z if self.quarters else slice(None)

    def start(self):
        p, o, q = self.p, self.out, self.q()
        self.own = self.s.local(
            self.src.at[:, :, self.cols()], o.at[p.xl, p.y, p.c, :, :, self.cols()]
        )
        self.ycp = [
            self.go(
                self.src.at[q, :, self.cols()], o.at[p.xl, p.y, p.c, q, :, self.cols()], dy=k
            )
            for k in (1, 3, 2)
        ]
        self.xcp = [
            self.go(
                self.src.at[q, :, self.cols(h)], o.at[p.xl, p.y, p.c, q, :, self.cols(h)], dx=dx
            )
            for h, dx in ((0, 1), (1, -1))
        ]

    def stage_x(self):
        p, o, q = self.p, self.out, self.q()
        for k, cp in zip((3, 1, 2), self.ycp):
            cp.wait_recv()
            for h, dx in ((0, 1), (1, -1)):
                r = o.at[p.xl, lax.rem(p.y + k, 4), p.c, q, :, self.cols(h)]
                self.xcp.append(self.go(r, r, dx=dx))
        if self.quarters:
            self.zcp = []
            for dz in (1, 3, 2):
                for k in (1, 2, 3):
                    r = o.at[p.xl, lax.rem(p.y + k, 4), p.c, q, :, self.cols()]
                    self.zcp.append(self.go(r, r, dz=dz))
        else:
            self.own.wait()
            r = o.at[p.xl, :, p.c, :, :, self.cols()]
            self.core.append(self.go(r, r, dc=1))

    def stage_z(self):
        if not self.quarters:
            return
        p, o, q = self.p, self.out, self.q()
        for cp in self.xcp:
            cp.wait_recv()
        for dz in (1, 3, 2):
            r = o.at[1 - p.xl, :, p.c, q, :, self.cols()]
            self.zcp.append(self.go(r, r, dz=dz))

    def stage_core(self):
        p, o = self.p, self.out
        if self.quarters:
            for cp in self.zcp:
                cp.wait_recv()
            self.own.wait()
            r = o.at[p.xl, :, p.c, :, :, self.cols()]
            self.core.append(self.go(r, r, dc=1))
        else:
            for cp in self.xcp:
                cp.wait_recv()
        r = o.at[1 - p.xl, :, p.c, :, :, self.cols()]
        self.core.append(self.go(r, r, dc=1))

    def arrived(self):
        for cp in self.core:
            cp.wait_recv()
        self.core = []

    def finish(self):
        self.arrived()
        for cp in self.sent:
            cp.wait_send()


class Reduce:
    def __init__(self, place, copies, order, g, bufs, total):
        self.p, self.s, self.order, self.g = place, copies, order, g
        self.r1, self.s1, self.r2, self.s2, self.r3 = bufs
        self.tot = total
        self.n = g.shape[-1]
        self.sent = []

    def go(self, src, dst, **k):
        cp = self.s.remote(src, dst, self.p.to(**k))
        self.sent.append(cp)
        return cp

    def half(self, xh):
        m = self.n // 2
        return pl.ds(pl.multiple_of(xh * m, 128), m)

    def me(self, i):
        return {"x": self.p.x, "y": self.p.y, "z": self.p.z}[self.order[i]]

    def pick(self, ref, i, v):
        o, ax = self.order, self.order[i]
        if ax == "x":
            rest = [slice(None)] * (len(ref.shape) - 2)
            return ref.at[(lax.rem(v, 2),) + tuple(rest) + (self.half(v // 2),)]
        lead = 0 if "x" in o[:i] else 1
        if ax == "z" and "y" not in o[:i]:
            lead += 1
        return ref.at[(slice(None),) * lead + (v,)]

    def scatter(self, i, src, recv):
        me = self.me(i)
        return [
            self.go(
                self.pick(src, i, lax.rem(me + k, 4)), recv.at[k - 1], **{"d" + self.order[i]: k}
            )
            for k in (1, 3, 2)
        ]

    def add(self, i, src, recv, out, cps):
        for cp in cps:
            cp.wait_recv()
        own = self.pick(src, i, self.me(i))
        shape = out.shape
        rows = (slice(None), slice(None))

        def one(idx):
            acc = own[idx].astype(F32)
            for k in range(3):
                acc = acc + recv[(k,) + idx].astype(F32)
            out[idx] = acc.astype(out.dtype)

        if len(shape) == 2:
            one(rows)
            return

        def body(j, _):
            idx = []
            for d in reversed(shape[:-2]):
                idx.insert(0, lax.rem(j, d))
                j = j // d
            one(tuple(idx) + rows)
            return 0

        lax.fori_loop(0, math.prod(shape[:-2]), body, 0)

    def first(self):
        self.c1 = self.scatter(0, self.g, self.r1)

    def second(self):
        self.add(0, self.g, self.r1, self.s1, self.c1)
        self.c2 = self.scatter(1, self.s1, self.r2)

    def third(self):
        self.add(1, self.s1, self.r2, self.s2, self.c2)
        self.c3 = self.scatter(2, self.s2, self.r3)

    def share(self):
        p = self.p
        mine = self.tot.at[p.z, :, self.half(p.xh)]
        self.add(2, self.s2, self.r3, mine, self.c3)
        self.c4 = self.go(mine, mine, dx=2)

    def spread(self):
        self.c4.wait_recv()
        r = self.tot.at[self.p.z]
        self.c5 = [self.go(r, r, dz=k) for k in (1, 3, 2)]

    def done(self):
        for cp in self.c5:
            cp.wait_recv()

    def finish(self):
        for cp in self.sent:
            cp.wait_send()


def reduce_shapes(order, q, n):
    full = {"x": 2, "y": 4, "z": 4}
    left, width, out = ["x", "y", "z"], n, []
    for i, ax in enumerate(order):
        left.remove(ax)
        if ax == "x":
            width = n // 2
        s = tuple(full[a] for a in left) + (q, width)
        out.append((3,) + s)
        if i < 2:
            out.append(s)
    return out


def run_pipe(steps, offsets, count):
    for t in range(count + max(offsets)):
        for step, d in zip(steps, offsets):
            if 0 <= t - d < count:
                step(t - d)


ROWS = {"small": 16, "out": 64, "up": 64, "down": 256}
COLS = {"small": 256, "out": 1024, "up": 4096, "down": 1024}
GATHER_NAMES = ("small", "out", "up", "down")
GATHER_PARTS = (
    ("small", 0, 256, False),
    ("out", 0, 1024, False),
    ("up", 0, 1024, True),
    ("up", 1024, 1024, False),
    ("up", 2048, 1024, True),
    ("up", 3072, 1024, False),
    ("down", 0, 512, False),
    ("down", 512, 512, False),
)
ANYWHERE = pl.BlockSpec(memory_space=pl.ANY)
INSIDE = pl.BlockSpec(memory_space=pltpu.VMEM)


def flat_pipe(steps, offsets, count):
    out = []
    for t in range(count + max(offsets)):
        for step, d in zip(steps, offsets):
            if 0 <= t - d < count:
                out.append(functools.partial(step, t - d))
    return out


def advance(queue, n):
    for _ in range(min(n, len(queue))):
        queue.pop(0)()


def sp_peers(p):
    out = []
    for dx, dz in ((0, 1), (0, 3), (2, 0), (2, 1), (2, 3), (0, 2), (2, 2)):
        xh = p.xh if dx == 0 else 1 - p.xh
        out.append((p.to(dx=dx, dz=dz), xh * 4 + lax.rem(p.z + dz, 4)))
    return out


def nt(a, b):
    return lax.dot_general(a, b, (((1,), (1,)), ((), ())), preferred_element_type=F32)


def nn(a, b):
    return jnp.dot(a, b, preferred_element_type=F32)


def forward_kernel(*refs):
    refs = list(refs)

    def take(n):
        head = refs[:n]
        del refs[:n]
        return head

    k = len(GATHER_NAMES)
    tok, wq = take(2)
    vectors, bias_up = take(2)
    ins = dict(zip(GATHER_NAMES[1:], take(k - 1)))
    outs = dict(zip(GATHER_NAMES, take(k)))
    tall, wsel, qkv, lse, ctx = take(5)
    small_v, pack, vt, ct, ch, cr = take(6)
    p, s = Place(), Copies(*refs)
    me = p.xh * 4 + p.z
    peers = sp_peers(p)
    pack[...] = jnp.zeros_like(pack)
    pack[0, 0:8, 0:64] = vectors[...]
    pack[0, 0:8, 192:256] = vectors[...]
    pack[0, 8:9, :] = bias_up[...]
    ins["small"] = pack
    greet(
        [p.to(dy=1), p.to(dy=2), p.to(dy=3), p.to(dx=1), p.to(dx=3), p.to(dc=1)]
        + [d for d, _ in peers]
    )
    sent = []

    def go(src, dst, dev):
        cp = s.remote(src, dst, dev)
        sent.append(cp)
        return cp

    pick = [
        s.local(
            wq.at[:, pl.ds(pl.multiple_of(j * 1024 + me * 128, 128), 128)],
            wsel.at[p.xl, p.y, p.c, :, pl.ds(j * 128, 128)],
        )
        for j in range(3)
    ]
    own_tok = s.local(tok, tall.at[me])
    tok_cps = [go(tok, tall.at[me], d) for d, _ in peers]
    parts = [Gather(p, s, ins[m], outs[m], lo, n, quarters) for m, lo, n, quarters in GATHER_PARTS]
    parts[0].start()
    for cp in pick:
        cp.wait()
    mine = wsel.at[p.xl, p.y, p.c]
    wy = [go(mine, mine, p.to(dy=d)) for d in (1, 3, 2)]
    queue = flat_pipe(
        (
            lambda i: parts[i + 1].start(),
            lambda i: parts[i + 1].stage_x(),
            lambda i: parts[i + 1].stage_z(),
            lambda i: parts[i + 1].stage_core(),
        ),
        (0, 3, 5, 6),
        len(parts) - 1,
    )
    advance(queue, 2)
    for cp in wy:
        cp.wait_recv()
    column = wsel.at[p.xl, :, p.c]
    wx = go(column, column, p.to(dx=1 - 2 * p.xl))
    parts[0].stage_x()
    advance(queue, 1)
    wx.wait_recv()
    plane = wsel.at[:, :, p.c]
    wc = go(plane, plane, p.to(dc=1))
    parts[0].stage_core()
    advance(queue, 1)
    parts[0].arrived()
    small_cp = s.local(outs["small"], small_v)
    advance(queue, 2)
    wc.wait_recv()
    small_cp.wait()
    own_tok.wait()
    for cp in tok_cps:
        cp.wait_recv()

    b, y = me // 4, me % 4
    qv = [
        small_v[b, y, 0, 0, r : r + 1, 0:128] + small_v[b, y, 1, 0, r : r + 1, 128:256]
        for r in range(2)
    ]
    bias = jnp.concatenate([qv[0], jnp.zeros((1, 128), F32), qv[1]], axis=1)

    def project(i, _):
        x = tall[pl.ds(2 * i, 2)].reshape(256, 1024)
        v = nn(x, wsel[...].reshape(1024, 384)) + bias
        qkv[pl.ds(pl.multiple_of(i * 256, 256), 256), :] = v.astype(BF)
        return 0

    lax.fori_loop(0, 4, project, 0)
    vt[...] = qkv[:, 256:384].astype(F32).T.astype(BF)
    per = max(1, (len(queue) - 4) // 4)
    for b in range(4):
        rows = pl.ds(b * 256, 256)
        for h in range(2):
            keys = qkv[:, 128 + 64 * h : 192 + 64 * h]
            st = nt(keys, qkv[rows, 64 * h : 64 * h + 64]) * 0.125
            peak = jnp.max(st, axis=0, keepdims=True)
            e = jnp.exp(st - peak)
            total = jnp.sum(e, axis=0, keepdims=True)
            c = nn(vt[64 * h : 64 * h + 64, :], e.astype(BF))
            ct[64 * h : 64 * h + 64, rows] = c / total
            lse[h : h + 1, rows] = peak + jnp.log(total)
        advance(queue, per)
    for t in range(8):
        ch[t] = ct[:, t * 128 : (t + 1) * 128].T.astype(BF)
    ctx_cps = [go(ch.at[t], cr.at[me], d) for d, t in peers]
    cr[me] = ch[me]
    advance(queue, len(queue))
    for cp in ctx_cps:
        cp.wait_recv()
    for t in range(8):
        ctx[:, t * 128 : (t + 1) * 128] = cr[t]
    for g in parts:
        g.finish()
    for cp in sent:
        cp.wait_send()


def attend_forward(tokens, w_qkv, vectors, bias_up, arrays):
    ins = []
    shapes = [jax.ShapeDtypeStruct((2, 4, 2, 1, 16, 256), F32)]
    for m, a in zip(GATHER_NAMES[1:], arrays):
        ins.append(a.reshape(4, ROWS[m] // 4, COLS[m]))
        shapes.append(jax.ShapeDtypeStruct((2, 4, 2) + ins[-1].shape, BF))
    k = len(shapes)
    shapes += [
        jax.ShapeDtypeStruct((8, 128, 1024), BF),
        jax.ShapeDtypeStruct((2, 4, 2, 64, 384), BF),
        jax.ShapeDtypeStruct((1024, 384), BF),
        jax.ShapeDtypeStruct((8, 1024), F32),
        jax.ShapeDtypeStruct((128, 1024), BF),
    ]
    out = pl.pallas_call(
        forward_kernel,
        out_shape=shapes,
        in_specs=[ANYWHERE] * 2 + [INSIDE] * 2 + [ANYWHERE] * (k - 1),
        out_specs=[ANYWHERE] * k + [INSIDE] * 5,
        scratch_shapes=[
            pltpu.VMEM((2, 4, 2, 1, 16, 256), F32),
            pltpu.VMEM((1, 16, 256), F32),
            pltpu.VMEM((128, 1024), BF),
            pltpu.VMEM((128, 1024), F32),
            pltpu.VMEM((8, 128, 128), BF),
            pltpu.VMEM((8, 128, 128), BF),
            pltpu.SemaphoreType.DMA((200,)),
            pltpu.SemaphoreType.DMA((200,)),
        ],
        compiler_params=pltpu.CompilerParams(
            collective_id=1, has_side_effects=True, vmem_limit_bytes=40 * 2**20
        ),
        name="attend_forward",
    )(tokens, w_qkv, vectors, bias_up, *ins)
    whole = [o.reshape(16 * ROWS[m], COLS[m]) for m, o in zip(GATHER_NAMES[1:], out[1:k])]
    return [out[0]] + whole + list(out[k:])


SMALL_SHAPE = (2, 4, 4, 8, 256)


class Products:
    def __init__(self, place, copies, left, right, both_left, both_right, totals, pieces, g, bufs):
        self.p, self.s = place, copies
        self.left, self.right = left, right
        self.both_left, self.both_right = both_left, both_right
        self.pieces, self.g = pieces, g
        self.swaps, self.ready = {}, set()
        self.red = [
            Reduce(place, copies, o, gi, b, totals[m].at[:, :, pl.ds(lo, n)])
            for (m, lo, n, o), gi, b in zip(pieces, g, bufs)
        ]

    def swap(self, m):
        p, s = self.p, self.s
        here = [
            s.local(self.left[m].at[:, :, p.c], self.both_left[m].at[:, :, :, pl.ds(0, 128)]),
            s.local(self.right[m], self.both_right[m].at[pl.ds(0, 128)]),
        ]
        there = [
            s.remote(
                self.left[m].at[:, :, 1 - p.c],
                self.both_left[m].at[:, :, :, pl.ds(128, 128)],
                p.to(dc=1),
            ),
            s.remote(self.right[m], self.both_right[m].at[pl.ds(128, 128)], p.to(dc=1)),
        ]
        self.swaps[m] = (here, there)

    def begin(self, i):
        m, lo, n, _ = self.pieces[i]
        if m not in self.ready:
            for cp in self.swaps[m][0]:
                cp.wait()
            for cp in self.swaps[m][1]:
                cp.wait_recv()
            self.ready.add(m)
        left, right, g = self.both_left[m], self.both_right[m], self.g[i]
        rows = left.shape[2]
        tile = min(512, n)

        def body(j, _):
            b, t = j // (n // tile), lax.rem(j, n // tile)
            c0 = pl.multiple_of(lo + t * tile, tile)
            v = jnp.dot(
                left[b].reshape(4 * rows, 256),
                right[:, pl.ds(c0, tile)],
                preferred_element_type=F32,
            ).astype(BF)
            g[b, :, :, :, pl.ds(pl.multiple_of(t * tile, tile), tile)] = v.reshape(
                4, 4, rows // 4, tile
            )
            return 0

        lax.fori_loop(0, 2 * (n // tile), body, 0)
        self.red[i].first()

    def finish(self):
        for r in self.red:
            r.finish()
        for m in self.swaps:
            for cp in self.swaps[m][1]:
                cp.wait_send()


def piece_scratch(pieces):
    sc = []
    for m, _, n, o in pieces:
        q = ROWS[m] // 4
        sc.append(pltpu.VMEM((2, 4, 4, q, n), BF))
        sc += [pltpu.VMEM(x, BF) for x in reduce_shapes(o, q, n)]
    return sc


VECTORS = (
    "bias_q",
    "bias_v",
    "bias_out",
    "gain_one",
    "shift_one",
    "bias_down",
    "gain_two",
    "shift_two",
)


def ln_rows(u):
    center = u - jnp.mean(u, axis=-1, keepdims=True)
    spread = jnp.mean(center * center, axis=-1, keepdims=True)
    inverse = lax.rsqrt(spread + epsilon)
    return center * inverse, inverse


def ln_back(e, hat, inverse, gain):
    scaled = e * gain
    centered = scaled - jnp.mean(scaled, axis=-1, keepdims=True)
    return inverse * (centered - hat * jnp.mean(scaled * hat, axis=-1, keepdims=True))


def col_sum(v):
    return jnp.sum(v, axis=0, keepdims=True)


def middle(
    tok,
    ctx,
    cot,
    small_v,
    wait_out,
    wait_up,
    wait_down,
    w_out,
    w_up,
    w_down,
    output,
    gctx,
    gsum,
    lefts,
    rights,
    small,
    vec,
    bup,
    slope,
    hat1,
    base,
    acc,
):
    for r, name in enumerate(VECTORS):
        for j in range(8):
            a = small_v[j // 4, j % 4, 0, 0, r : r + 1, 0:128]
            b = small_v[j // 4, j % 4, 1, 0, r : r + 1, 128:256]
            vec[r : r + 1, j * 128 : (j + 1) * 128] = a + b
    for f in range(16):
        bup[0:1, f * 256 : (f + 1) * 256] = small_v[f // 8, (f // 2) % 4, f % 2, 0, 8:9, :]
    row = {n: vec[r : r + 1, :] for r, n in enumerate(VECTORS)}

    def put(name, v):
        r = VECTORS.index(name)
        for j in range(8):
            small[j // 4, j % 4, 0, r : r + 1, 0:128] = v[:, j * 128 : (j + 1) * 128]

    small[...] = jnp.zeros_like(small)
    x = tok[...].astype(F32)
    wait_out()
    branch = nn(ctx[...], w_out[...]) + row["bias_out"]
    hat, inv1 = ln_rows(x + branch)
    hat1[...] = hat
    normed = hat * row["gain_one"] + row["shift_one"]
    base[...] = normed
    low = normed.astype(BF)
    rights["low"][...] = low
    lefts["up"][...] = normed.T.astype(BF).reshape(8, 2, 64, 128)
    lefts["out"][...] = ctx[...].astype(F32).T.astype(BF).reshape(8, 2, 64, 128)
    acc[...] = jnp.zeros_like(acc)

    def up(t, _):
        cols = pl.ds(pl.multiple_of(t * 512, 512), 512)
        wait_up(t)
        pre = nn(rights["low"][...], w_up[t]) + bup[0:1, cols]
        cdf = 0.5 * (1.0 + lax.erf(pre * root_half))
        slope[:, cols] = cdf + pre * jnp.exp(-0.5 * pre * pre) * inv_root_two_pi
        act = pre * cdf
        lefts["down"][t] = act.T.astype(BF).reshape(2, 256, 128)
        wait_down(t)
        acc[...] += nn(act.astype(BF), w_down[t])
        return 0

    lax.fori_loop(0, 8, up, 0)
    hat2, inv2 = ln_rows(base[...] + acc[...] + row["bias_down"])
    output[...] = (hat2 * row["gain_two"] + row["shift_two"]).astype(BF)
    dy = cot[...].astype(F32)
    put("gain_two", col_sum(dy * hat2))
    put("shift_two", col_sum(dy))
    gs2 = ln_back(dy, hat2, inv2, row["gain_two"])
    acc[...] = gs2
    ffn = gs2.astype(BF)
    rights["down"][...] = ffn
    put("bias_down", col_sum(ffn.astype(F32)))

    def back(t, _):
        cols = pl.ds(pl.multiple_of(t * 512, 512), 512)
        pre = (nt(rights["down"][...], w_down[t]) * slope[:, cols]).astype(BF)
        rights["up"][:, cols] = pre
        s = col_sum(pre.astype(F32))
        small[t // 4, lax.rem(t, 4), 1, 0:1, :] = s[:, :256]
        small[t // 4, lax.rem(t, 4), 1, 1:2, :] = s[:, 256:]
        acc[...] += nt(pre, w_up[t])
        return 0

    lax.fori_loop(0, 8, back, 0)
    gn = acc[...]
    hat = hat1[...]
    put("gain_one", col_sum(gn * hat))
    put("shift_one", col_sum(gn))
    gs1 = ln_back(gn, hat, inv1, row["gain_one"])
    gsum[...] = gs1
    gb = gs1.astype(BF)
    rights["out"][...] = gb
    put("bias_out", col_sum(gb.astype(F32)))
    gctx[...] = nt(gb, w_out[...]).astype(BF)


def middle_kernel(
    tok, ctx, cot, small_h, out_h, up_h, down_h,
    output, gctx, gsum, l_down, l_up, l_out, r_down, r_up, r_out, small,
    small_v, w_out, w_up, w_down, low, vec, bup, slope, hat1, base, acc, sem,
):
    cps = [pltpu.make_async_copy(small_h, small_v, sem.at[0])]
    cps += [pltpu.make_async_copy(out_h, w_out, sem.at[1])]
    ups = [
        pltpu.make_async_copy(up_h.at[:, pl.ds(t * 512, 512)], w_up.at[t], sem.at[2 + t])
        for t in range(8)
    ]
    downs = [
        pltpu.make_async_copy(down_h.at[pl.ds(t * 512, 512)], w_down.at[t], sem.at[10 + t])
        for t in range(8)
    ]
    for cp in cps:
        cp.start()
    for a, b in zip(ups, downs):
        a.start()
        b.start()
    cps[0].wait()

    def wait_up(t):
        pltpu.make_async_copy(up_h.at[:, pl.ds(0, 512)], w_up.at[t], sem.at[2 + t]).wait()

    def wait_down(t):
        pltpu.make_async_copy(down_h.at[pl.ds(0, 512)], w_down.at[t], sem.at[10 + t]).wait()

    middle(
        tok, ctx, cot, small_v, cps[1].wait, wait_up, wait_down, w_out, w_up, w_down,
        output, gctx, gsum,
        {"down": l_down, "up": l_up, "out": l_out},
        {"down": r_down, "up": r_up, "out": r_out, "low": low},
        small, vec, bup, slope, hat1, base, acc,
    )


def run_middle(tok, ctx, cot, small_full, full_out, full_up, full_down):
    def b(*s):
        return jax.ShapeDtypeStruct(s, BF)

    def f(*s):
        return jax.ShapeDtypeStruct(s, F32)

    return pl.pallas_call(
        middle_kernel,
        out_shape=[b(128, 1024), b(128, 1024), f(128, 1024)]
        + [b(8, 2, 256, 128), b(8, 2, 64, 128), b(8, 2, 64, 128)]
        + [b(128, 1024), b(128, 4096), b(128, 1024), f(2, 4, 4, 8, 256)],
        in_specs=[INSIDE] * 3 + [ANYWHERE] * 4,
        out_specs=[INSIDE] * 10,
        scratch_shapes=[
            pltpu.VMEM((2, 4, 2, 1, 16, 256), F32),
            pltpu.VMEM((1024, 1024), BF),
            pltpu.VMEM((8, 1024, 512), BF),
            pltpu.VMEM((8, 512, 1024), BF),
            pltpu.VMEM((128, 1024), BF),
            pltpu.VMEM((8, 1024), F32),
            pltpu.VMEM((8, 4096), F32),
            pltpu.VMEM((128, 4096), F32),
            pltpu.VMEM((128, 1024), F32),
            pltpu.VMEM((128, 1024), F32),
            pltpu.VMEM((128, 1024), F32),
            pltpu.SemaphoreType.DMA((18,)),
        ],
        compiler_params=pltpu.CompilerParams(vmem_limit_bytes=56 * 2**20),
        name="middle",
    )(tok, ctx, cot, small_full, full_out, full_up, full_down)


PIECES = (
    ("down", 0, 512, "yzx"),
    ("up", 0, 1024, "xyz"),
    ("down", 512, 512, "zxy"),
    ("up", 1024, 1024, "yzx"),
    ("up", 2048, 1024, "zxy"),
    ("up", 3072, 1024, "xyz"),
    ("out", 0, 1024, "yzx"),
)
GRAD_NAMES = ("down", "up", "out")


def backward_kernel(*refs):
    refs = list(refs)

    def take(n):
        head = refs[:n]
        del refs[:n]
        return head

    k = len(GRAD_NAMES)
    left = dict(zip(GRAD_NAMES, take(k)))
    right = dict(zip(GRAD_NAMES, take(k)))
    small, gctx, gsum, tall_t, wsel, qkv, lse = take(7)
    totals = dict(zip(GRAD_NAMES, take(k)))
    small_total, grad_tok, gw = take(3)
    both_left = dict(zip(GRAD_NAMES, take(k)))
    both_right = dict(zip(GRAD_NAMES, take(k)))
    small_src, small_in, small_g = take(3)
    small_bufs = take(5)
    g, bufs = [], []
    for _ in PIECES:
        g += take(1)
        bufs.append(take(5))
    do, kt, dqt, dkv, dqkv, gq, gq_c, gq_x, gq_y, dts, dtr = take(11)
    p, s = Place(), Copies(*refs)
    me = p.xh * 4 + p.z
    peers = sp_peers(p)
    greet(
        [p.to(dy=1), p.to(dy=2), p.to(dy=3), p.to(dx=1), p.to(dx=3), p.to(dc=1)]
        + [d for d, _ in peers]
    )
    sent = []

    def go(src, dst, dev):
        cp = s.remote(src, dst, dev)
        sent.append(cp)
        return cp

    do_cps = [
        go(gctx.at[:, pl.ds(pl.multiple_of(t * 128, 128), 128)], do.at[me], d) for d, t in peers
    ]
    do_own = s.local(gctx.at[:, pl.ds(pl.multiple_of(me * 128, 128), 128)], do.at[me])
    prod = Products(p, s, left, right, both_left, both_right, totals, PIECES, g, bufs)
    for m in GRAD_NAMES:
        prod.swap(m)
    kt[...] = qkv[:, 128:256].astype(F32).T.astype(BF)
    red = prod.red
    n = len(PIECES)
    for i in range(n):
        prod.begin(i)
    queue = flat_pipe(
        (
            lambda i: red[i].second(),
            lambda i: red[i].third(),
            lambda i: red[i].share(),
            lambda i: red[i].spread(),
            lambda i: red[i].done(),
        ),
        (0, 2, 4, 5, 6),
        n,
    )
    do_own.wait()
    for cp in do_cps:
        cp.wait_recv()
    dkv[...] = jnp.zeros_like(dkv)
    for b in range(4):
        rows = pl.ds(b * 256, 256)
        for h in range(2):
            lanes = slice(64 * h, 64 * h + 64)
            keys = qkv[:, 128 + 64 * h : 192 + 64 * h]
            vals = qkv[:, 256 + 64 * h : 320 + 64 * h]
            q = qkv[rows, lanes]
            dob = do[2 * b : 2 * b + 2].reshape(256, 128)[:, lanes]
            probs = jnp.exp(nt(keys, q) * 0.125 - lse[h : h + 1, rows])
            dp = nt(vals, dob)
            inner = jnp.sum(probs * dp, axis=0, keepdims=True)
            ds = (probs * (dp - inner)).astype(BF)
            dqt[lanes, rows] = nn(kt[lanes, :], ds) * 0.125
            dkv[:, lanes] += nn(ds, q) * 0.125
            dkv[:, 128 + 64 * h : 192 + 64 * h] += nn(probs.astype(BF), dob)
        if b >= 1:
            advance(queue, 1)
    dqkv[:, :128] = dqt[...].T.astype(BF)
    dqkv[:, 128:] = dkv[...].astype(BF)

    def part(i, _):
        rows = pl.ds(pl.multiple_of(i * 256, 256), 256)
        v = nt(dqkv[rows, :], wsel[...].reshape(1024, 384)).astype(BF)
        dts[pl.ds(2 * i, 2)] = v.reshape(2, 128, 1024)
        return 0

    lax.fori_loop(0, 4, part, 0)
    dt_cps = [go(dts.at[t], dtr.at[me], d) for d, t in peers]

    def rows_of(i, _):
        v = nn(tall_t[pl.ds(pl.multiple_of(i * 256, 256), 256), :], dqkv[...])
        gq[pl.ds(2 * i, 2)] = v.astype(BF).reshape(2, 2, 64, 384)
        return 0

    lax.fori_loop(0, 4, rows_of, 0)
    c_cp = go(gq.at[:, 1 - p.c], gq_c, p.to(dc=1))

    cols = jnp.sum(dqkv[...].astype(F32), axis=0, keepdims=True)
    small_src[...] = small[...]
    small_src[me // 4, me % 4, 0, 0:1, 0:128] = cols[:, :128]
    small_src[me // 4, me % 4, 0, 1:2, 0:128] = cols[:, 256:]
    small_swap = s.remote(small_src, small_in, p.to(dc=1))
    small_red = Reduce(p, s, "xyz", small_g, small_bufs, small_total)
    advance(queue, 2)
    small_swap.wait_recv()
    small_g[...] = small_src[...] + small_in[...]
    small_red.first()

    c_cp.wait_recv()

    def add_core(i, _):
        gq_c[i] = (gq_c[i].astype(F32) + gq[i, p.c].astype(F32)).astype(BF)
        return 0

    lax.fori_loop(0, 8, add_core, 0)
    x_cp = go(gq_c.at[pl.ds((1 - p.xl) * 4, 4)], gq_x, p.to(dx=1 - 2 * p.xl))
    advance(queue, 3)
    small_red.second()
    x_cp.wait_recv()

    def add_x(i, _):
        gq_x[i] = (gq_x[i].astype(F32) + gq_c[p.xl * 4 + i].astype(F32)).astype(BF)
        return 0

    lax.fori_loop(0, 4, add_x, 0)
    y_cps = [go(gq_x.at[lax.rem(p.y + d, 4)], gq_y.at[d - 1], p.to(dy=d)) for d in (1, 3, 2)]
    advance(queue, 3)
    small_red.third()
    for cp in y_cps:
        cp.wait_recv()
    acc = gq_x[p.y].astype(F32)
    for i in range(3):
        acc = acc + gq_y[i].astype(F32)
    gw[me] = acc.astype(BF)
    gw_cps = [go(gw.at[me], gw.at[me], d) for d, _ in peers]
    advance(queue, 3)
    small_red.share()
    for cp in dt_cps:
        cp.wait_recv()
    dtr[me] = dts[me]
    acc = gsum[...]
    for t in range(8):
        acc = acc + dtr[t].astype(F32)
    grad_tok[...] = acc.astype(BF)
    small_red.spread()
    advance(queue, len(queue))
    for cp in gw_cps:
        cp.wait_recv()
    small_red.done()
    prod.finish()
    small_red.finish()
    small_swap.wait_send()
    for cp in sent:
        cp.wait_send()


def attend_backward(pairs, small, gctx, gsum, tall_t, wsel, qkv, lse):
    lefts = [pairs[m][0].reshape(2, 4, 2, ROWS[m], 128) for m in GRAD_NAMES]
    rights = [pairs[m][1] for m in GRAD_NAMES]
    scratch = [pltpu.VMEM((2, 4, ROWS[m], 256), BF) for m in GRAD_NAMES]
    scratch += [pltpu.VMEM((256, COLS[m]), BF) for m in GRAD_NAMES]
    scratch += [pltpu.VMEM(SMALL_SHAPE, F32)] * 3
    scratch += [pltpu.VMEM(x, F32) for x in reduce_shapes("xyz", 8, 256)]
    scratch += piece_scratch(PIECES)
    scratch += [
        pltpu.VMEM((8, 128, 128), BF),
        pltpu.VMEM((128, 1024), BF),
        pltpu.VMEM((128, 1024), F32),
        pltpu.VMEM((1024, 256), F32),
        pltpu.VMEM((1024, 384), BF),
        pltpu.VMEM((8, 2, 64, 384), BF),
        pltpu.VMEM((8, 64, 384), BF),
        pltpu.VMEM((4, 64, 384), BF),
        pltpu.VMEM((3, 64, 384), BF),
        pltpu.VMEM((8, 128, 1024), BF),
        pltpu.VMEM((8, 128, 1024), BF),
    ]
    scratch += [pltpu.SemaphoreType.DMA((250,)), pltpu.SemaphoreType.DMA((250,))]
    k = len(GRAD_NAMES)
    out = pl.pallas_call(
        backward_kernel,
        out_shape=[jax.ShapeDtypeStruct((4, ROWS[m] // 4, COLS[m]), BF) for m in GRAD_NAMES]
        + [
            jax.ShapeDtypeStruct((4, 8, 256), F32),
            jax.ShapeDtypeStruct((128, 1024), BF),
            jax.ShapeDtypeStruct((8, 64, 384), BF),
        ],
        in_specs=[ANYWHERE] * (2 * k) + [INSIDE, ANYWHERE] + [INSIDE] * 5,
        out_specs=[INSIDE] * (k + 3),
        scratch_shapes=scratch,
        compiler_params=pltpu.CompilerParams(
            collective_id=2, has_side_effects=True, vmem_limit_bytes=63 * 2**20
        ),
        name="attend_backward",
    )(*lefts, *rights, small, gctx, gsum, tall_t, wsel, qkv, lse)
    grads = {m: o.reshape(ROWS[m], COLS[m]).astype(F32) for m, o in zip(GRAD_NAMES, out)}
    gw = out[k + 2].reshape(8, 64, 3, 128).transpose(1, 2, 0, 3)
    grads["qkv"] = gw.reshape(64, 3072).astype(F32)
    return grads, out[k], out[k + 1]


def on_device(
    tokens,
    cotangent,
    w_qkv,
    bias_q,
    bias_v,
    w_out,
    bias_out,
    gain_one,
    shift_one,
    w_up,
    bias_up,
    w_down,
    bias_down,
    gain_two,
    shift_two,
):
    num_seqs, slice_len, model_width = tokens.shape
    row_count = num_seqs * slice_len
    inputs = tokens.reshape(row_count, model_width)
    own = dict(
        bias_q=bias_q,
        bias_v=bias_v,
        bias_out=bias_out,
        gain_one=gain_one,
        shift_one=shift_one,
        bias_down=bias_down,
        gain_two=gain_two,
        shift_two=shift_two,
    )
    vectors = jnp.stack([own[k] for k in VECTORS]).astype(F32)
    small, full_out, full_up, full_down, tall, wsel, qkv, lse, context_tokens = attend_forward(
        inputs, w_qkv, vectors, bias_up.astype(F32).reshape(1, 256), [w_out, w_up, w_down]
    )
    output, grad_context, grad_sum_one, l_down, l_up, l_out, r_down, r_up, r_out, sums = run_middle(
        inputs,
        context_tokens,
        cotangent.reshape(row_count, model_width),
        small,
        full_out,
        full_up,
        full_down,
    )
    grads, total, grad_inputs = attend_backward(
        {
            "down": (l_down, r_down),
            "up": (l_up, r_up),
            "out": (l_out, r_out),
        },
        sums,
        grad_context,
        grad_sum_one,
        tall.reshape(1024, model_width).T,
        wsel,
        qkv,
        lse,
    )
    core = lax.axis_index("fsdp") % 2
    mine = lax.dynamic_slice(total, (0, 0, core * 64), (1, 8, 64))
    res = {k: mine[0, r] for r, k in enumerate(VECTORS)}
    res["bias_up"] = lax.dynamic_slice(total, (1, core, 0), (1, 1, 256)).reshape(256)
    return (
        output.reshape(tokens.shape),
        grad_inputs.reshape(tokens.shape),
        grads["qkv"],
        res["bias_q"],
        res["bias_v"],
        grads["out"],
        res["bias_out"],
        res["gain_one"],
        res["shift_one"],
        grads["up"],
        res["bias_up"],
        grads["down"],
        res["bias_down"],
        res["gain_two"],
        res["shift_two"],
    )


def solution(mesh):
    rows, vector = P("fsdp", None), P("fsdp")
    block = P("fsdp", "sp", None)
    params = (rows, vector, vector, rows, vector, vector, vector)
    params += (rows, vector, rows, vector, vector, vector)
    return jax.shard_map(
        on_device,
        mesh=mesh,
        in_specs=(block, block) + params,
        out_specs=(block, block) + params,
        check_vma=False,
    )
```

```python
import functools
import math

import jax
import jax.numpy as jnp
from jax import lax
from jax.experimental import pallas as pl
from jax.experimental.pallas import tpu as pltpu
from jax.sharding import PartitionSpec as P

HD = 64
MESH = pl.DeviceIdType.MESH
BF = jnp.bfloat16
F32 = jnp.float32

epsilon = 1e-05
root_half = 0.7071067811865476
inv_root_two_pi = 0.3989422804014327


class Place:
    def __init__(self):
        f = lax.axis_index("fsdp")
        s = lax.axis_index("sp")
        self.xh, self.xl, self.y, self.z, self.c = s // 4, f // 8, (f // 2) % 4, s % 4, f % 2
        self.x = 2 * self.xh + self.xl

    def to(self, dx=0, dy=0, dz=0, dc=0):
        x = lax.rem(self.x + dx + 4, 4)
        y = lax.rem(self.y + dy + 4, 4)
        z = lax.rem(self.z + dz + 4, 4)
        c = self.c if dc == 0 else 1 - self.c
        return ((x % 2) * 8 + y * 2 + c, (x // 2) * 4 + z)


class Copies:
    def __init__(self, send, recv):
        self.send, self.recv, self.n = send, recv, 0

    def remote(self, src, dst, dev):
        i = self.n
        self.n += 1
        cp = pltpu.make_async_remote_copy(
            src_ref=src,
            dst_ref=dst,
            send_sem=self.send.at[i],
            recv_sem=self.recv.at[i],
            device_id=dev,
            device_id_type=MESH,
        )
        cp.start()
        return cp

    def local(self, src, dst):
        i = self.n
        self.n += 1
        cp = pltpu.make_async_copy(src, dst, self.recv.at[i])
        cp.start()
        return cp


def greet(targets):
    bar = pltpu.get_barrier_semaphore()
    for t in targets:
        pl.semaphore_signal(bar, inc=1, device_id=t, device_id_type=MESH)
    pl.semaphore_wait(bar, len(targets))


class Gather:
    def __init__(self, place, copies, src, out, lo, n, quarters):
        self.p, self.s, self.src, self.out = place, copies, src, out
        self.lo, self.n, self.quarters = lo, n, quarters
        self.sent, self.core = [], []

    def cols(self, half=None):
        if half is None:
            return pl.ds(self.lo, self.n)
        return pl.ds(self.lo + half * (self.n // 2), self.n // 2)

    def go(self, src, dst, **k):
        cp = self.s.remote(src, dst, self.p.to(**k))
        self.sent.append(cp)
        return cp

    def q(self):
        return self.p.z if self.quarters else slice(None)

    def start(self):
        p, o, q = self.p, self.out, self.q()
        self.own = self.s.local(
            self.src.at[:, :, self.cols()], o.at[p.xl, p.y, p.c, :, :, self.cols()]
        )
        self.ycp = [
            self.go(
                self.src.at[q, :, self.cols()], o.at[p.xl, p.y, p.c, q, :, self.cols()], dy=k
            )
            for k in (1, 3, 2)
        ]
        self.xcp = [
            self.go(
                self.src.at[q, :, self.cols(h)], o.at[p.xl, p.y, p.c, q, :, self.cols(h)], dx=dx
            )
            for h, dx in ((0, 1), (1, -1))
        ]

    def stage_x(self):
        p, o, q = self.p, self.out, self.q()
        for k, cp in zip((3, 1, 2), self.ycp):
            cp.wait_recv()
            for h, dx in ((0, 1), (1, -1)):
                r = o.at[p.xl, lax.rem(p.y + k, 4), p.c, q, :, self.cols(h)]
                self.xcp.append(self.go(r, r, dx=dx))
        if self.quarters:
            self.zcp = []
            for dz in (1, 3, 2):
                for k in (1, 2, 3):
                    r = o.at[p.xl, lax.rem(p.y + k, 4), p.c, q, :, self.cols()]
                    self.zcp.append(self.go(r, r, dz=dz))
        else:
            self.own.wait()
            r = o.at[p.xl, :, p.c, :, :, self.cols()]
            self.core.append(self.go(r, r, dc=1))

    def stage_z(self):
        if not self.quarters:
            return
        p, o, q = self.p, self.out, self.q()
        for cp in self.xcp:
            cp.wait_recv()
        for dz in (1, 3, 2):
            r = o.at[1 - p.xl, :, p.c, q, :, self.cols()]
            self.zcp.append(self.go(r, r, dz=dz))

    def stage_core(self):
        p, o = self.p, self.out
        if self.quarters:
            for cp in self.zcp:
                cp.wait_recv()
            self.own.wait()
            r = o.at[p.xl, :, p.c, :, :, self.cols()]
            self.core.append(self.go(r, r, dc=1))
        else:
            for cp in self.xcp:
                cp.wait_recv()
        r = o.at[1 - p.xl, :, p.c, :, :, self.cols()]
        self.core.append(self.go(r, r, dc=1))

    def arrived(self):
        for cp in self.core:
            cp.wait_recv()
        self.core = []

    def finish(self):
        self.arrived()
        for cp in self.sent:
            cp.wait_send()


class Reduce:
    def __init__(self, place, copies, order, g, bufs, total):
        self.p, self.s, self.order, self.g = place, copies, order, g
        self.r1, self.s1, self.r2, self.s2, self.r3 = bufs
        self.tot = total
        self.n = g.shape[-1]
        self.sent = []

    def go(self, src, dst, **k):
        cp = self.s.remote(src, dst, self.p.to(**k))
        self.sent.append(cp)
        return cp

    def half(self, xh):
        m = self.n // 2
        return pl.ds(pl.multiple_of(xh * m, 128), m)

    def me(self, i):
        return {"x": self.p.x, "y": self.p.y, "z": self.p.z}[self.order[i]]

    def pick(self, ref, i, v):
        o, ax = self.order, self.order[i]
        if ax == "x":
            rest = [slice(None)] * (len(ref.shape) - 2)
            return ref.at[(lax.rem(v, 2),) + tuple(rest) + (self.half(v // 2),)]
        lead = 0 if "x" in o[:i] else 1
        if ax == "z" and "y" not in o[:i]:
            lead += 1
        return ref.at[(slice(None),) * lead + (v,)]

    def scatter(self, i, src, recv):
        me = self.me(i)
        return [
            self.go(
                self.pick(src, i, lax.rem(me + k, 4)), recv.at[k - 1], **{"d" + self.order[i]: k}
            )
            for k in (1, 3, 2)
        ]

    def add(self, i, src, recv, out, cps):
        for cp in cps:
            cp.wait_recv()
        own = self.pick(src, i, self.me(i))
        shape = out.shape
        rows = (slice(None), slice(None))

        def one(idx):
            acc = own[idx].astype(F32)
            for k in range(3):
                acc = acc + recv[(k,) + idx].astype(F32)
            out[idx] = acc.astype(out.dtype)

        if len(shape) == 2:
            one(rows)
            return

        def body(j, _):
            idx = []
            for d in reversed(shape[:-2]):
                idx.insert(0, lax.rem(j, d))
                j = j // d
            one(tuple(idx) + rows)
            return 0

        lax.fori_loop(0, math.prod(shape[:-2]), body, 0)

    def first(self):
        self.c1 = self.scatter(0, self.g, self.r1)

    def second(self):
        self.add(0, self.g, self.r1, self.s1, self.c1)
        self.c2 = self.scatter(1, self.s1, self.r2)

    def third(self):
        self.add(1, self.s1, self.r2, self.s2, self.c2)
        self.c3 = self.scatter(2, self.s2, self.r3)

    def share(self):
        p = self.p
        mine = self.tot.at[p.z, :, self.half(p.xh)]
        self.add(2, self.s2, self.r3, mine, self.c3)
        self.c4 = self.go(mine, mine, dx=2)

    def spread(self):
        self.c4.wait_recv()
        r = self.tot.at[self.p.z]
        self.c5 = [self.go(r, r, dz=k) for k in (1, 3, 2)]

    def done(self):
        for cp in self.c5:
            cp.wait_recv()

    def finish(self):
        for cp in self.sent:
            cp.wait_send()


def reduce_shapes(order, q, n):
    full = {"x": 2, "y": 4, "z": 4}
    left, width, out = ["x", "y", "z"], n, []
    for i, ax in enumerate(order):
        left.remove(ax)
        if ax == "x":
            width = n // 2
        s = tuple(full[a] for a in left) + (q, width)
        out.append((3,) + s)
        if i < 2:
            out.append(s)
    return out


ROWS = {"small": 16, "out": 64, "up": 64, "down": 256}
COLS = {"small": 256, "out": 1024, "up": 4096, "down": 1024}
GATHER_NAMES = ("small", "out", "up", "down")
GATHER_PARTS = (
    ("small", 0, 256, False),
    ("out", 0, 1024, False),
    ("up", 0, 2048, False),
    ("up", 2048, 1024, True),
    ("up", 3072, 1024, True),
    ("down", 0, 512, False),
    ("down", 512, 512, False),
)
ANYWHERE = pl.BlockSpec(memory_space=pl.ANY)
INSIDE = pl.BlockSpec(memory_space=pltpu.VMEM)


def flat_pipe(steps, offsets, count):
    out = []
    for t in range(count + max(offsets)):
        for step, d in zip(steps, offsets):
            if 0 <= t - d < count:
                out.append(functools.partial(step, t - d))
    return out


def advance(queue, n):
    for _ in range(min(n, len(queue))):
        queue.pop(0)()


def sp_peers(p):
    out = []
    for dx, dz in ((0, 1), (0, 3), (2, 0), (2, 1), (2, 3), (0, 2), (2, 2)):
        xh = p.xh if dx == 0 else 1 - p.xh
        out.append((p.to(dx=dx, dz=dz), xh * 4 + lax.rem(p.z + dz, 4)))
    return out


def nt(a, b):
    return lax.dot_general(a, b, (((1,), (1,)), ((), ())), preferred_element_type=F32)


def nn(a, b):
    return jnp.dot(a, b, preferred_element_type=F32)


def forward_kernel(*refs):
    refs = list(refs)

    def take(n):
        head = refs[:n]
        del refs[:n]
        return head

    k = len(GATHER_NAMES)
    tok, wq = take(2)
    vectors, bias_up = take(2)
    ins = dict(zip(GATHER_NAMES[1:], take(k - 1)))
    outs = dict(zip(GATHER_NAMES, take(k)))
    tall, wsel, qkv, lse, ctx = take(5)
    small_v, pack, vt, ct, ch, cr = take(6)
    p, s = Place(), Copies(*refs)
    me = p.xh * 4 + p.z
    peers = sp_peers(p)
    pack[...] = jnp.zeros_like(pack)
    pack[0, 0:8, 0:64] = vectors[...]
    pack[0, 0:8, 192:256] = vectors[...]
    pack[0, 8:9, :] = bias_up[...]
    ins["small"] = pack
    greet(
        [p.to(dy=1), p.to(dy=2), p.to(dy=3), p.to(dx=1), p.to(dx=3), p.to(dc=1)]
        + [d for d, _ in peers]
    )
    sent = []

    def go(src, dst, dev):
        cp = s.remote(src, dst, dev)
        sent.append(cp)
        return cp

    pick = [
        s.local(
            wq.at[:, pl.ds(pl.multiple_of(j * 1024 + me * 128, 128), 128)],
            wsel.at[p.xl, p.y, p.c, :, pl.ds(j * 128, 128)],
        )
        for j in range(3)
    ]
    own_tok = s.local(tok, tall.at[me])
    across = go(tok, tall.at[me], p.to(dx=2))
    tok_cps = [go(tok, tall.at[me], p.to(dz=d)) for d in (1, 3, 2)]
    parts = [Gather(p, s, ins[m], outs[m], lo, n, quarters) for m, lo, n, quarters in GATHER_PARTS]
    parts[0].start()
    for cp in pick:
        cp.wait()
    mine = wsel.at[p.xl, p.y, p.c]
    wy = [go(mine, mine, p.to(dy=d)) for d in (1, 3, 2)]
    queue = flat_pipe(
        (
            lambda i: parts[i + 1].start(),
            lambda i: parts[i + 1].stage_x(),
            lambda i: parts[i + 1].stage_z(),
            lambda i: parts[i + 1].stage_core(),
        ),
        (0, 3, 5, 6),
        len(parts) - 1,
    )
    advance(queue, 2)
    for cp in wy:
        cp.wait_recv()
    column = wsel.at[p.xl, :, p.c]
    wx = go(column, column, p.to(dx=1 - 2 * p.xl))
    across.wait_recv()
    far = tall.at[(1 - p.xh) * 4 + p.z]
    tok_cps += [go(far, far, p.to(dz=d)) for d in (1, 3, 2)]
    parts[0].stage_x()
    advance(queue, 1)
    wx.wait_recv()
    plane = wsel.at[:, :, p.c]
    wc = go(plane, plane, p.to(dc=1))
    parts[0].stage_core()
    advance(queue, 1)
    parts[0].arrived()
    small_cp = s.local(outs["small"], small_v)
    advance(queue, 2)
    wc.wait_recv()
    small_cp.wait()
    own_tok.wait()
    for cp in tok_cps:
        cp.wait_recv()

    b, y = me // 4, me % 4
    qv = [
        small_v[b, y, 0, 0, r : r + 1, 0:128] + small_v[b, y, 1, 0, r : r + 1, 128:256]
        for r in range(2)
    ]
    bias = jnp.concatenate([qv[0], jnp.zeros((1, 128), F32), qv[1]], axis=1)

    def project(i, _):
        x = tall[pl.ds(2 * i, 2)].reshape(256, 1024)
        v = nn(x, wsel[...].reshape(1024, 384)) + bias
        qkv[pl.ds(pl.multiple_of(i * 256, 256), 256), :] = v.astype(BF)
        return 0

    lax.fori_loop(0, 4, project, 0)
    vt[...] = qkv[:, 256:384].astype(F32).T.astype(BF)
    per = max(1, (len(queue) - 4) // 4)
    for b in range(4):
        rows = pl.ds(b * 256, 256)
        for h in range(2):
            keys = qkv[:, 128 + 64 * h : 192 + 64 * h]
            st = nt(keys, qkv[rows, 64 * h : 64 * h + 64]) * 0.125
            peak = jnp.max(st, axis=0, keepdims=True)
            e = jnp.exp(st - peak)
            total = jnp.sum(e, axis=0, keepdims=True)
            c = nn(vt[64 * h : 64 * h + 64, :], e.astype(BF))
            ct[64 * h : 64 * h + 64, rows] = c / total
            lse[h : h + 1, rows] = peak + jnp.log(total)
        advance(queue, per)
    for t in range(8):
        ch[t] = ct[:, t * 128 : (t + 1) * 128].T.astype(BF)
    ctx_cps = [go(ch.at[t], cr.at[me], d) for d, t in peers]
    cr[me] = ch[me]
    advance(queue, len(queue))
    for cp in ctx_cps:
        cp.wait_recv()
    for t in range(8):
        ctx[:, t * 128 : (t + 1) * 128] = cr[t]
    for g in parts:
        g.finish()
    for cp in sent:
        cp.wait_send()


def attend_forward(tokens, w_qkv, vectors, bias_up, arrays):
    ins = []
    shapes = [jax.ShapeDtypeStruct((2, 4, 2, 1, 16, 256), F32)]
    for m, a in zip(GATHER_NAMES[1:], arrays):
        ins.append(a.reshape(4, ROWS[m] // 4, COLS[m]))
        shapes.append(jax.ShapeDtypeStruct((2, 4, 2) + ins[-1].shape, BF))
    k = len(shapes)
    shapes += [
        jax.ShapeDtypeStruct((8, 128, 1024), BF),
        jax.ShapeDtypeStruct((2, 4, 2, 64, 384), BF),
        jax.ShapeDtypeStruct((1024, 384), BF),
        jax.ShapeDtypeStruct((8, 1024), F32),
        jax.ShapeDtypeStruct((128, 1024), BF),
    ]
    out = pl.pallas_call(
        forward_kernel,
        out_shape=shapes,
        in_specs=[ANYWHERE] * 2 + [INSIDE] * 2 + [ANYWHERE] * (k - 1),
        out_specs=[ANYWHERE] * k + [INSIDE] * 5,
        scratch_shapes=[
            pltpu.VMEM((2, 4, 2, 1, 16, 256), F32),
            pltpu.VMEM((1, 16, 256), F32),
            pltpu.VMEM((128, 1024), BF),
            pltpu.VMEM((128, 1024), F32),
            pltpu.VMEM((8, 128, 128), BF),
            pltpu.VMEM((8, 128, 128), BF),
            pltpu.SemaphoreType.DMA((200,)),
            pltpu.SemaphoreType.DMA((200,)),
        ],
        compiler_params=pltpu.CompilerParams(
            collective_id=1, has_side_effects=True, vmem_limit_bytes=62 * 2**20
        ),
        name="attend_forward",
    )(tokens, w_qkv, vectors, bias_up, *ins)
    whole = [o.reshape(16 * ROWS[m], COLS[m]) for m, o in zip(GATHER_NAMES[1:], out[1:k])]
    return [out[0]] + whole + list(out[k:])


SMALL_SHAPE = (2, 4, 4, 8, 256)


class ReduceTwo(Reduce):
    def __init__(self, place, copies, order, g, bufs, total):
        self.p, self.s, self.order, self.g = place, copies, order, g
        self.r1, self.s1, self.r2 = bufs
        self.tot = total
        self.n = g.shape[-1]
        self.sent = []

    def pick(self, ref, i, v):
        if self.order[i] == "x":
            rest = [slice(None)] * (len(ref.shape) - 2)
            return ref.at[(lax.rem(v, 2),) + tuple(rest) + (self.half(v // 2),)]
        return ref.at[:, v] if i == 0 else ref.at[v]

    def share(self):
        mine = self.tot.at[self.p.z, :, self.half(self.p.xh)]
        self.add(1, self.s1, self.r2, mine, self.c2)
        self.c4 = self.go(mine, mine, dx=2)


def reduce_two_shapes(order, rows, n):
    if order[0] == "x":
        return [(3, 4, rows, n // 2), (4, rows, n // 2), (3, rows, n // 2)]
    return [(3, 2, rows, n), (2, rows, n), (3, rows, n // 2)]


class Tokens:
    def __init__(self, place, copies, axis, left, right, both_left, both_right):
        self.p, self.s, self.axis = place, copies, axis
        self.left, self.right, self.bl, self.br = left, right, both_left, both_right
        self.sent, self.cps, self.own = [], [], []

    def lanes(self, ref, at, n):
        return ref.at[(slice(None),) * (len(ref.shape) - 1) + (pl.ds(at, n),)]

    def sources(self, t):
        if self.axis == "y":
            return self.left.at[:, t], self.right
        return self.left, self.right.at[:, pl.ds(pl.multiple_of(t * 1024, 128), 1024)]

    def place(self):
        me = self.p.y if self.axis == "y" else self.p.z
        return me, pl.multiple_of(me * 128, 128)

    def send(self, side, steps=(1, 3, 2, 0)):
        me, slot = self.place()
        dst = self.lanes(self.bl, slot, 128) if side == 0 else self.br.at[pl.ds(slot, 128)]
        for k in steps:
            src = self.sources(lax.rem(me + k, 4))[side]
            if k == 0:
                self.own.append(self.s.local(src, dst))
                continue
            cp = self.s.remote(src, dst, self.p.to(**{"d" + self.axis: k}))
            self.cps.append(cp)
            self.sent.append(cp)

    def rows_of(self, ref, c):
        return ref.at[:, c] if self.axis == "y" else ref.at[:, :, c]

    def swap(self):
        p, s = self.p, self.s
        for cp in self.own:
            cp.wait()
        for cp in self.cps:
            cp.wait_recv()
        far = self.rows_of(self.bl, 1 - p.c)
        self.cores = [
            s.remote(self.lanes(far, 0, 512), self.lanes(far, 512, 512), p.to(dc=1)),
            s.remote(self.br.at[pl.ds(0, 512)], self.br.at[pl.ds(512, 512)], p.to(dc=1)),
        ]
        self.sent += self.cores

    def ready(self):
        for cp in self.cores:
            cp.wait_recv()

    def multiply(self, lo, g):
        n = g.shape[-1]

        def body(b, _):
            left = self.bl[b, self.p.c] if self.axis == "y" else self.bl[b, :, self.p.c]
            v = nn(left.reshape(4 * g.shape[2], 1024), self.br[:, lo : lo + n])
            g[b] = v.astype(BF).reshape(4, g.shape[2], n)
            return 0

        lax.fori_loop(0, 2, body, 0)

    def finish(self):
        for cp in self.sent:
            cp.wait_send()


VECTORS = (
    "bias_q",
    "bias_v",
    "bias_out",
    "gain_one",
    "shift_one",
    "bias_down",
    "gain_two",
    "shift_two",
)


def ln_rows(u):
    center = u - jnp.mean(u, axis=-1, keepdims=True)
    spread = jnp.mean(center * center, axis=-1, keepdims=True)
    inverse = lax.rsqrt(spread + epsilon)
    return center * inverse, inverse


def ln_back(e, hat, inverse, gain):
    scaled = e * gain
    centered = scaled - jnp.mean(scaled, axis=-1, keepdims=True)
    return inverse * (centered - hat * jnp.mean(scaled * hat, axis=-1, keepdims=True))


def col_sum(v):
    return jnp.sum(v, axis=0, keepdims=True)


def middle(
    tok,
    ctx,
    cot,
    small_v,
    wait_out,
    wait_up,
    wait_down,
    w_out,
    w_up,
    w_down,
    output,
    gctx,
    gsum,
    lefts,
    rights,
    small,
    vec,
    bup,
    slope,
    hat1,
    base,
    acc,
    toks,
    place,
):
    for r, name in enumerate(VECTORS):
        for j in range(8):
            a = small_v[j // 4, j % 4, 0, 0, r : r + 1, 0:128]
            b = small_v[j // 4, j % 4, 1, 0, r : r + 1, 128:256]
            vec[r : r + 1, j * 128 : (j + 1) * 128] = a + b
    for f in range(16):
        bup[0:1, f * 256 : (f + 1) * 256] = small_v[f // 8, (f // 2) % 4, f % 2, 0, 8:9, :]
    row = {n: vec[r : r + 1, :] for r, n in enumerate(VECTORS)}

    def put(name, v):
        r = VECTORS.index(name)
        for j in range(8):
            small[j // 4, j % 4, 0, r : r + 1, 0:128] = v[:, j * 128 : (j + 1) * 128]

    small[...] = jnp.zeros_like(small)
    x = tok[...].astype(F32)
    wait_out()
    branch = nn(ctx[...], w_out[...]) + row["bias_out"]
    hat, inv1 = ln_rows(x + branch)
    hat1[...] = hat
    normed = hat * row["gain_one"] + row["shift_one"]
    base[...] = normed
    low = normed.astype(BF)
    rights["low"][...] = low
    lefts["up"][...] = normed.T.astype(BF).reshape(2, 4, 2, 64, 128)
    lefts["out"][...] = ctx[...].astype(F32).T.astype(BF).reshape(2, 4, 2, 64, 128)
    toks["up"].send(0)
    toks["out"].send(0)
    acc[...] = jnp.zeros_like(acc)

    def up(t, _):
        cols = pl.ds(pl.multiple_of(t * 512, 512), 512)
        wait_up(t)
        pre = nn(rights["low"][...], w_up[t]) + bup[0:1, cols]
        cdf = 0.5 * (1.0 + lax.erf(pre * root_half))
        slope[:, cols] = cdf + pre * jnp.exp(-0.5 * pre * pre) * inv_root_two_pi
        act = pre * cdf
        lefts["down"][t // 4, lax.rem(t, 4)] = act.T.astype(BF).reshape(2, 256, 128)
        wait_down(t)
        acc[...] += nn(act.astype(BF), w_down[t])
        return 0

    lax.fori_loop(0, 8, up, 0)
    toks["down"].send(0)
    hat2, inv2 = ln_rows(base[...] + acc[...] + row["bias_down"])
    output[...] = (hat2 * row["gain_two"] + row["shift_two"]).astype(BF)
    dy = cot[...].astype(F32)
    put("gain_two", col_sum(dy * hat2))
    put("shift_two", col_sum(dy))
    gs2 = ln_back(dy, hat2, inv2, row["gain_two"])
    acc[...] = gs2
    ffn = gs2.astype(BF)
    rights["down"][...] = ffn
    toks["down"].send(1)
    put("bias_down", col_sum(ffn.astype(F32)))

    def back(k, j, _):
        t = 2 * lax.rem(place.z + k, 4) + j
        cols = pl.ds(pl.multiple_of(t * 512, 512), 512)
        pre = (nt(rights["down"][...], w_down[t]) * slope[:, cols]).astype(BF)
        rights["up"][:, cols] = pre
        s = col_sum(pre.astype(F32))
        small[t // 4, lax.rem(t, 4), 1, 0:1, :] = s[:, :256]
        small[t // 4, lax.rem(t, 4), 1, 1:2, :] = s[:, 256:]
        acc[...] += nt(pre, w_up[t])
        return 0

    for k in (1, 3, 2, 0):
        lax.fori_loop(0, 2, functools.partial(back, k), 0)
        toks["up"].send(1, (k,))
    gn = acc[...]
    hat = hat1[...]
    put("gain_one", col_sum(gn * hat))
    put("shift_one", col_sum(gn))
    gs1 = ln_back(gn, hat, inv1, row["gain_one"])
    gsum[...] = gs1
    gb = gs1.astype(BF)
    rights["out"][...] = gb
    toks["out"].send(1)
    put("bias_out", col_sum(gb.astype(F32)))
    gctx[...] = nt(gb, w_out[...]).astype(BF)


GRAD_NAMES = ("down", "up", "out")
GRAD_AXIS = {"down": "y", "up": "z", "out": "y"}
PIECE_ROWS = {"down": 64, "up": 64, "out": 16}
PIECES = (
    ("down", 0, 512, "xz"),
    ("down", 512, 512, "zx"),
    ("up", 0, 512, "yx"),
    ("up", 512, 512, "xy"),
    ("out", 0, 1024, "zx"),
)


def backward_kernel(*refs):
    refs = list(refs)

    def take(n):
        head = refs[:n]
        del refs[:n]
        return head

    k = len(GRAD_NAMES)
    tok, ctx, cot, small_h, out_h, up_h, down_h, tall_t, wsel, qkv, lse = take(11)
    totals = dict(zip(GRAD_NAMES, take(k)))
    small_total, grad_tok, gw, output = take(4)
    small_v, w_out, w_up, w_down, low, vec, bup, slope, hat1, base, acc, sem = take(12)
    gctx, gsum = take(2)
    left = dict(zip(GRAD_NAMES, take(k)))
    right = dict(zip(GRAD_NAMES, take(k)))
    both_left = dict(zip(GRAD_NAMES, take(k)))
    both_right = dict(zip(GRAD_NAMES, take(k)))
    small_src, small_in, small_g = take(3)
    small_bufs = take(5)
    g, bufs = [], []
    for _ in PIECES:
        g += take(1)
        bufs.append(take(3))
    do, kt, dqt, dkv, dqkv, gq, gq_c, gq_x, gq_y = take(9)
    dts, dtx, dtxr, dtz, dtz_s, dtzr = take(6)
    vec_cp = pltpu.make_async_copy(small_h, small_v, sem.at[0])
    out_cp = pltpu.make_async_copy(out_h, w_out, sem.at[1])
    vec_cp.start()
    out_cp.start()
    for t in range(8):
        pltpu.make_async_copy(up_h.at[:, pl.ds(t * 512, 512)], w_up.at[t], sem.at[2 + t]).start()
        pltpu.make_async_copy(down_h.at[pl.ds(t * 512, 512)], w_down.at[t], sem.at[10 + t]).start()

    def wait_up(t):
        pltpu.make_async_copy(up_h.at[:, pl.ds(0, 512)], w_up.at[t], sem.at[2 + t]).wait()

    def wait_down(t):
        pltpu.make_async_copy(down_h.at[pl.ds(0, 512)], w_down.at[t], sem.at[10 + t]).wait()

    p, s = Place(), Copies(*refs)
    me = p.xh * 4 + p.z
    peers = sp_peers(p)
    greet(
        [p.to(dy=1), p.to(dy=2), p.to(dy=3), p.to(dx=1), p.to(dx=3), p.to(dc=1)]
        + [d for d, _ in peers]
    )
    sent = []

    def go(src, dst, dev):
        cp = s.remote(src, dst, dev)
        sent.append(cp)
        return cp

    toks = {
        m: Tokens(p, s, GRAD_AXIS[m], left[m], right[m], both_left[m], both_right[m])
        for m in GRAD_NAMES
    }
    vec_cp.wait()
    middle(
        tok,
        ctx,
        cot,
        small_v,
        out_cp.wait,
        wait_up,
        wait_down,
        w_out,
        w_up,
        w_down,
        output,
        gctx,
        gsum,
        left,
        dict(right, low=low),
        small_src,
        vec,
        bup,
        slope,
        hat1,
        base,
        acc,
        toks,
        p,
    )
    do_cps = [
        go(gctx.at[:, pl.ds(pl.multiple_of(t * 128, 128), 128)], do.at[me], d) for d, t in peers
    ]
    do_own = s.local(gctx.at[:, pl.ds(pl.multiple_of(me * 128, 128), 128)], do.at[me])
    toks["down"].swap()
    red = [
        ReduceTwo(p, s, o, gi, b, totals[m].at[:, :, pl.ds(lo, n)])
        for (m, lo, n, o), gi, b in zip(PIECES, g, bufs)
    ]
    kt[...] = qkv[:, 128:256].astype(F32).T.astype(BF)
    toks["up"].swap()
    ready = set()

    def begin(i):
        m, lo, _, _ = PIECES[i]
        if m not in ready:
            toks[m].ready()
            ready.add(m)
        toks[m].multiply(lo, g[i])
        red[i].first()

    begin(0)
    begin(1)
    do_own.wait()
    for cp in do_cps:
        cp.wait_recv()
    dkv[...] = jnp.zeros_like(dkv)

    def head_block(b, h):
        rows = pl.ds(b * 256, 256)
        lanes = slice(64 * h, 64 * h + 64)
        keys = qkv[:, 128 + 64 * h : 192 + 64 * h]
        vals = qkv[:, 256 + 64 * h : 320 + 64 * h]
        q = qkv[rows, lanes]
        dob = do[2 * b : 2 * b + 2].reshape(256, 128)[:, lanes]
        probs = jnp.exp(nt(keys, q) * 0.125 - lse[h : h + 1, rows])
        dp = nt(vals, dob)
        inner = jnp.sum(probs * dp, axis=0, keepdims=True)
        ds = (probs * (dp - inner)).astype(BF)
        dqt[lanes, rows] = nn(kt[lanes, :], ds) * 0.125
        dkv[:, lanes] += nn(ds, q) * 0.125
        dkv[:, 128 + 64 * h : 192 + 64 * h] += nn(probs.astype(BF), dob)

    for b in range(4):
        for h in range(2):
            head_block(b, h)
        if b == 0:
            begin(2)
            toks["out"].swap()
        if b == 1:
            begin(3)
        if b == 2:
            begin(4)
    dqkv[:, :128] = dqt[...].T.astype(BF)
    dqkv[:, 128:] = dkv[...].astype(BF)

    def part(i, _):
        rows = pl.ds(pl.multiple_of(i * 256, 256), 256)
        v = nt(dqkv[rows, :], wsel[...].reshape(1024, 384)).astype(BF)
        dts[i // 2, pl.ds(2 * lax.rem(i, 2), 2)] = v.reshape(2, 128, 1024)
        return 0

    lax.fori_loop(0, 4, part, 0)
    first, second = pl.ds(0, 512), pl.ds(512, 512)
    dx_cp = go(dts.at[1 - p.xh, :, :, first], dtx, p.to(dx=2))
    dz_cps = [
        go(dts.at[:, lax.rem(p.z + d, 4), :, second], dtz.at[d - 1], p.to(dz=d)) for d in (1, 3, 2)
    ]

    def rows_of(i, _):
        v = nn(tall_t[pl.ds(pl.multiple_of(i * 256, 256), 256), :], dqkv[...])
        gq[pl.ds(2 * i, 2)] = v.astype(BF).reshape(2, 2, 64, 384)
        return 0

    lax.fori_loop(0, 4, rows_of, 0)
    c_cp = go(gq.at[:, 1 - p.c], gq_c, p.to(dc=1))
    cols = jnp.sum(dqkv[...].astype(F32), axis=0, keepdims=True)
    small_src[me // 4, me % 4, 0, 0:1, 0:128] = cols[:, :128]
    small_src[me // 4, me % 4, 0, 1:2, 0:128] = cols[:, 256:]
    small_swap = s.remote(small_src, small_in, p.to(dc=1))
    small_red = Reduce(p, s, "xyz", small_g, small_bufs, small_total)

    c_cp.wait_recv()

    def add_core(i, _):
        gq_c[i] = (gq_c[i].astype(F32) + gq[i, p.c].astype(F32)).astype(BF)
        return 0

    lax.fori_loop(0, 8, add_core, 0)
    x_cp = go(gq_c.at[pl.ds((1 - p.xl) * 4, 4)], gq_x, p.to(dx=1 - 2 * p.xl))
    small_swap.wait_recv()
    small_g[...] = small_src[...] + small_in[...]
    small_red.first()
    dx_cp.wait_recv()

    def add_far(i, _):
        dtx[i] = (dtx[i].astype(F32) + dts[p.xh, i, :, 0:512].astype(F32)).astype(BF)
        return 0

    lax.fori_loop(0, 4, add_far, 0)
    dz2_cps = [go(dtx.at[lax.rem(p.z + d, 4)], dtxr.at[d - 1], p.to(dz=d)) for d in (1, 3, 2)]
    for cp in dz_cps:
        cp.wait_recv()

    def add_round(i, _):
        v = dts[i, p.z, :, 512:1024].astype(F32)
        for d in range(3):
            v = v + dtz[d, i].astype(F32)
        dtz_s[i] = v.astype(BF)
        return 0

    lax.fori_loop(0, 2, add_round, 0)
    dx2_cp = go(dtz_s.at[1 - p.xh], dtzr, p.to(dx=2))
    x_cp.wait_recv()

    def add_x(i, _):
        gq_x[i] = (gq_x[i].astype(F32) + gq_c[p.xl * 4 + i].astype(F32)).astype(BF)
        return 0

    lax.fori_loop(0, 4, add_x, 0)
    y_cps = [go(gq_x.at[lax.rem(p.y + d, 4)], gq_y.at[d - 1], p.to(dy=d)) for d in (1, 3, 2)]
    for i in range(2):
        red[i].second()
    small_red.second()
    for i in range(2, len(PIECES)):
        red[i].second()
    for cp in y_cps:
        cp.wait_recv()
    acc = gq_x[p.y].astype(F32)
    for i in range(3):
        acc = acc + gq_y[i].astype(F32)
    gw[me] = acc.astype(BF)
    gw_cps = [go(gw.at[me], gw.at[me], d) for d, _ in peers]
    small_red.third()
    for r in red:
        r.share()
    small_red.share()
    for r in red:
        r.spread()
    small_red.spread()
    for cp in dz2_cps:
        cp.wait_recv()
    dx2_cp.wait_recv()
    acc = gsum[:, 0:512] + dtx[p.z].astype(F32)
    for t in range(3):
        acc = acc + dtxr[t].astype(F32)
    grad_tok[:, 0:512] = acc.astype(BF)
    acc = gsum[:, 512:1024] + dtz_s[p.xh].astype(F32) + dtzr[...].astype(F32)
    grad_tok[:, 512:1024] = acc.astype(BF)
    for cp in gw_cps:
        cp.wait_recv()
    for r in red:
        r.done()
    small_red.done()
    for r in red:
        r.finish()
    for m in GRAD_NAMES:
        toks[m].finish()
    small_red.finish()
    small_swap.wait_send()
    for cp in sent:
        cp.wait_send()


def finish_layer(tok, ctx, cot, small_h, out_h, up_h, down_h, tall_t, wsel, qkv, lse):
    scratch = [
        pltpu.VMEM((2, 4, 2, 1, 16, 256), F32),
        pltpu.VMEM((1024, 1024), BF),
        pltpu.VMEM((8, 1024, 512), BF),
        pltpu.VMEM((8, 512, 1024), BF),
        pltpu.VMEM((128, 1024), BF),
        pltpu.VMEM((8, 1024), F32),
        pltpu.VMEM((8, 4096), F32),
        pltpu.VMEM((128, 4096), F32),
        pltpu.VMEM((128, 1024), F32),
        pltpu.VMEM((128, 1024), F32),
        pltpu.VMEM((128, 1024), F32),
        pltpu.SemaphoreType.DMA((18,)),
        pltpu.VMEM((128, 1024), BF),
        pltpu.VMEM((128, 1024), F32),
    ]
    scratch += [pltpu.VMEM((2, 4, 2, ROWS[m], 128), BF) for m in GRAD_NAMES]
    scratch += [pltpu.VMEM((128, COLS[m]), BF) for m in GRAD_NAMES]
    scratch += [
        pltpu.VMEM((2, 2, ROWS[m], 1024) if GRAD_AXIS[m] == "y" else (2, 4, 2, ROWS[m], 1024), BF)
        for m in GRAD_NAMES
    ]
    scratch += [pltpu.VMEM((1024, 1024), BF) for m in GRAD_NAMES]
    scratch += [pltpu.VMEM(SMALL_SHAPE, F32)] * 3
    scratch += [pltpu.VMEM(x, F32) for x in reduce_shapes("xyz", 8, 256)]
    for m, _, n, o in PIECES:
        scratch.append(pltpu.VMEM((2, 4, PIECE_ROWS[m], n), BF))
        scratch += [pltpu.VMEM(x, BF) for x in reduce_two_shapes(o, PIECE_ROWS[m], n)]
    scratch += [
        pltpu.VMEM((8, 128, 128), BF),
        pltpu.VMEM((128, 1024), BF),
        pltpu.VMEM((128, 1024), F32),
        pltpu.VMEM((1024, 256), F32),
        pltpu.VMEM((1024, 384), BF),
        pltpu.VMEM((8, 2, 64, 384), BF),
        pltpu.VMEM((8, 64, 384), BF),
        pltpu.VMEM((4, 64, 384), BF),
        pltpu.VMEM((3, 64, 384), BF),
        pltpu.VMEM((2, 4, 128, 1024), BF),
        pltpu.VMEM((4, 128, 512), BF),
        pltpu.VMEM((3, 128, 512), BF),
        pltpu.VMEM((3, 2, 128, 512), BF),
        pltpu.VMEM((2, 128, 512), BF),
        pltpu.VMEM((128, 512), BF),
    ]
    scratch += [pltpu.SemaphoreType.DMA((250,)), pltpu.SemaphoreType.DMA((250,))]
    k = len(GRAD_NAMES)
    out = pl.pallas_call(
        backward_kernel,
        out_shape=[jax.ShapeDtypeStruct((4, PIECE_ROWS[m], 1024), BF) for m in GRAD_NAMES]
        + [
            jax.ShapeDtypeStruct((4, 8, 256), F32),
            jax.ShapeDtypeStruct((128, 1024), BF),
            jax.ShapeDtypeStruct((8, 64, 384), BF),
            jax.ShapeDtypeStruct((128, 1024), BF),
        ],
        in_specs=[INSIDE] * 3 + [ANYWHERE] * 4 + [INSIDE] * 4,
        out_specs=[INSIDE] * (k + 4),
        scratch_shapes=scratch,
        compiler_params=pltpu.CompilerParams(
            collective_id=2, has_side_effects=True, vmem_limit_bytes=62 * 2**20
        ),
        name="layer_back",
    )(tok, ctx, cot, small_h, out_h, up_h, down_h, tall_t, wsel, qkv, lse)
    grads = {
        "down": out[0].reshape(256, 1024).astype(F32),
        "up": out[1].transpose(1, 0, 2).reshape(64, 4096).astype(F32),
        "out": out[2].reshape(64, 1024).astype(F32),
    }
    gw = out[k + 2].reshape(8, 64, 3, 128).transpose(1, 2, 0, 3)
    grads["qkv"] = gw.reshape(64, 3072).astype(F32)
    return grads, out[k], out[k + 1], out[k + 3]


def on_device(
    tokens,
    cotangent,
    w_qkv,
    bias_q,
    bias_v,
    w_out,
    bias_out,
    gain_one,
    shift_one,
    w_up,
    bias_up,
    w_down,
    bias_down,
    gain_two,
    shift_two,
):
    num_seqs, slice_len, model_width = tokens.shape
    row_count = num_seqs * slice_len
    inputs = tokens.reshape(row_count, model_width)
    own = dict(
        bias_q=bias_q,
        bias_v=bias_v,
        bias_out=bias_out,
        gain_one=gain_one,
        shift_one=shift_one,
        bias_down=bias_down,
        gain_two=gain_two,
        shift_two=shift_two,
    )
    vectors = jnp.stack([own[k] for k in VECTORS]).astype(F32)
    small, full_out, full_up, full_down, tall, wsel, qkv, lse, context_tokens = attend_forward(
        inputs, w_qkv, vectors, bias_up.astype(F32).reshape(1, 256), [w_out, w_up, w_down]
    )
    grads, total, grad_inputs, output = finish_layer(
        inputs,
        context_tokens,
        cotangent.reshape(row_count, model_width),
        small,
        full_out,
        full_up,
        full_down,
        tall.reshape(1024, model_width).T,
        wsel,
        qkv,
        lse,
    )
    core = lax.axis_index("fsdp") % 2
    mine = lax.dynamic_slice(total, (0, 0, core * 64), (1, 8, 64))
    res = {k: mine[0, r] for r, k in enumerate(VECTORS)}
    res["bias_up"] = lax.dynamic_slice(total, (1, core, 0), (1, 1, 256)).reshape(256)
    return (
        output.reshape(tokens.shape),
        grad_inputs.reshape(tokens.shape),
        grads["qkv"],
        res["bias_q"],
        res["bias_v"],
        grads["out"],
        res["bias_out"],
        res["gain_one"],
        res["shift_one"],
        grads["up"],
        res["bias_up"],
        grads["down"],
        res["bias_down"],
        res["gain_two"],
        res["shift_two"],
    )


def solution(mesh):
    rows, vector = P("fsdp", None), P("fsdp")
    block = P("fsdp", "sp", None)
    params = (rows, vector, vector, rows, vector, vector, vector)
    params += (rows, vector, rows, vector, vector, vector)
    return jax.shard_map(
        on_device,
        mesh=mesh,
        in_specs=(block, block) + params,
        out_specs=(block, block) + params,
        check_vma=False,
    )
```

```python
import functools
import math

import jax
import jax.numpy as jnp
from jax import lax
from jax.experimental import pallas as pl
from jax.experimental.pallas import tpu as pltpu
from jax.sharding import PartitionSpec as P

HD = 64
MESH = pl.DeviceIdType.MESH
BF = jnp.bfloat16
F32 = jnp.float32

epsilon = 1e-05
root_half = 0.7071067811865476
inv_root_two_pi = 0.3989422804014327


class Place:
    def __init__(self):
        f = lax.axis_index("fsdp")
        s = lax.axis_index("sp")
        self.xh, self.xl, self.y, self.z, self.c = s // 4, f // 8, (f // 2) % 4, s % 4, f % 2
        self.x = 2 * self.xh + self.xl

    def to(self, dx=0, dy=0, dz=0, dc=0):
        x = lax.rem(self.x + dx + 4, 4)
        y = lax.rem(self.y + dy + 4, 4)
        z = lax.rem(self.z + dz + 4, 4)
        c = self.c if dc == 0 else 1 - self.c
        return ((x % 2) * 8 + y * 2 + c, (x // 2) * 4 + z)


class Copies:
    def __init__(self, send, recv):
        self.send, self.recv, self.n = send, recv, 0

    def remote(self, src, dst, dev):
        i = self.n
        self.n += 1
        cp = pltpu.make_async_remote_copy(
            src_ref=src,
            dst_ref=dst,
            send_sem=self.send.at[i],
            recv_sem=self.recv.at[i],
            device_id=dev,
            device_id_type=MESH,
        )
        cp.start()
        return cp

    def local(self, src, dst):
        i = self.n
        self.n += 1
        cp = pltpu.make_async_copy(src, dst, self.recv.at[i])
        cp.start()
        return cp


def greet(targets):
    bar = pltpu.get_barrier_semaphore()
    for t in targets:
        pl.semaphore_signal(bar, inc=1, device_id=t, device_id_type=MESH)
    pl.semaphore_wait(bar, len(targets))


class Gather:
    def __init__(self, place, copies, src, out, lo, n, quarters):
        self.p, self.s, self.src, self.out = place, copies, src, out
        self.lo, self.n, self.quarters = lo, n, quarters
        self.sent, self.core = [], []

    def cols(self, half=None):
        if half is None:
            return pl.ds(self.lo, self.n)
        return pl.ds(self.lo + half * (self.n // 2), self.n // 2)

    def go(self, src, dst, **k):
        cp = self.s.remote(src, dst, self.p.to(**k))
        self.sent.append(cp)
        return cp

    def q(self):
        return self.p.z if self.quarters else slice(None)

    def start(self):
        p, o, q = self.p, self.out, self.q()
        self.own = self.s.local(
            self.src.at[:, :, self.cols()], o.at[p.xl, p.y, p.c, :, :, self.cols()]
        )
        self.ycp = [
            self.go(
                self.src.at[q, :, self.cols()], o.at[p.xl, p.y, p.c, q, :, self.cols()], dy=k
            )
            for k in (1, 3, 2)
        ]
        self.xcp = [
            self.go(
                self.src.at[q, :, self.cols(h)], o.at[p.xl, p.y, p.c, q, :, self.cols(h)], dx=dx
            )
            for h, dx in ((0, 1), (1, -1))
        ]

    def stage_x(self):
        p, o, q = self.p, self.out, self.q()
        for k, cp in zip((3, 1, 2), self.ycp):
            cp.wait_recv()
            for h, dx in ((0, 1), (1, -1)):
                r = o.at[p.xl, lax.rem(p.y + k, 4), p.c, q, :, self.cols(h)]
                self.xcp.append(self.go(r, r, dx=dx))
        if self.quarters:
            self.zcp = []
            for dz in (1, 3, 2):
                for k in (1, 2, 3):
                    r = o.at[p.xl, lax.rem(p.y + k, 4), p.c, q, :, self.cols()]
                    self.zcp.append(self.go(r, r, dz=dz))
        else:
            self.own.wait()
            r = o.at[p.xl, :, p.c, :, :, self.cols()]
            self.core.append(self.go(r, r, dc=1))

    def stage_z(self):
        if not self.quarters:
            return
        p, o, q = self.p, self.out, self.q()
        for cp in self.xcp:
            cp.wait_recv()
        for dz in (1, 3, 2):
            r = o.at[1 - p.xl, :, p.c, q, :, self.cols()]
            self.zcp.append(self.go(r, r, dz=dz))

    def stage_core(self):
        p, o = self.p, self.out
        if self.quarters:
            for cp in self.zcp:
                cp.wait_recv()
            self.own.wait()
            r = o.at[p.xl, :, p.c, :, :, self.cols()]
            self.core.append(self.go(r, r, dc=1))
        else:
            for cp in self.xcp:
                cp.wait_recv()
        r = o.at[1 - p.xl, :, p.c, :, :, self.cols()]
        self.core.append(self.go(r, r, dc=1))

    def arrived(self):
        for cp in self.core:
            cp.wait_recv()
        self.core = []

    def finish(self):
        self.arrived()
        for cp in self.sent:
            cp.wait_send()


class Reduce:
    def __init__(self, place, copies, order, g, bufs, total):
        self.p, self.s, self.order, self.g = place, copies, order, g
        self.r1, self.s1, self.r2, self.s2, self.r3 = bufs
        self.tot = total
        self.n = g.shape[-1]
        self.sent = []

    def go(self, src, dst, **k):
        cp = self.s.remote(src, dst, self.p.to(**k))
        self.sent.append(cp)
        return cp

    def half(self, xh):
        m = self.n // 2
        return pl.ds(pl.multiple_of(xh * m, 128), m)

    def me(self, i):
        return {"x": self.p.x, "y": self.p.y, "z": self.p.z}[self.order[i]]

    def pick(self, ref, i, v):
        o, ax = self.order, self.order[i]
        if ax == "x":
            rest = [slice(None)] * (len(ref.shape) - 2)
            return ref.at[(lax.rem(v, 2),) + tuple(rest) + (self.half(v // 2),)]
        lead = 0 if "x" in o[:i] else 1
        if ax == "z" and "y" not in o[:i]:
            lead += 1
        return ref.at[(slice(None),) * lead + (v,)]

    def scatter(self, i, src, recv):
        me = self.me(i)
        return [
            self.go(
                self.pick(src, i, lax.rem(me + k, 4)), recv.at[k - 1], **{"d" + self.order[i]: k}
            )
            for k in (1, 3, 2)
        ]

    def add(self, i, src, recv, out, cps):
        for cp in cps:
            cp.wait_recv()
        own = self.pick(src, i, self.me(i))
        shape = out.shape
        rows = (slice(None), slice(None))

        def one(idx):
            acc = own[idx].astype(F32)
            for k in range(3):
                acc = acc + recv[(k,) + idx].astype(F32)
            out[idx] = acc.astype(out.dtype)

        if len(shape) == 2:
            one(rows)
            return

        def body(j, _):
            idx = []
            for d in reversed(shape[:-2]):
                idx.insert(0, lax.rem(j, d))
                j = j // d
            one(tuple(idx) + rows)
            return 0

        lax.fori_loop(0, math.prod(shape[:-2]), body, 0)

    def first(self):
        self.c1 = self.scatter(0, self.g, self.r1)

    def second(self):
        self.add(0, self.g, self.r1, self.s1, self.c1)
        self.c2 = self.scatter(1, self.s1, self.r2)

    def third(self):
        self.add(1, self.s1, self.r2, self.s2, self.c2)
        self.c3 = self.scatter(2, self.s2, self.r3)

    def share(self):
        p = self.p
        mine = self.tot.at[p.z, :, self.half(p.xh)]
        self.add(2, self.s2, self.r3, mine, self.c3)
        self.c4 = self.go(mine, mine, dx=2)

    def spread(self):
        self.c4.wait_recv()
        r = self.tot.at[self.p.z]
        self.c5 = [self.go(r, r, dz=k) for k in (1, 3, 2)]

    def done(self):
        for cp in self.c5:
            cp.wait_recv()

    def finish(self):
        for cp in self.sent:
            cp.wait_send()


def reduce_shapes(order, q, n):
    full = {"x": 2, "y": 4, "z": 4}
    left, width, out = ["x", "y", "z"], n, []
    for i, ax in enumerate(order):
        left.remove(ax)
        if ax == "x":
            width = n // 2
        s = tuple(full[a] for a in left) + (q, width)
        out.append((3,) + s)
        if i < 2:
            out.append(s)
    return out


ROWS = {"small": 16, "out": 64, "up": 64, "down": 256}
COLS = {"small": 256, "out": 1024, "up": 4096, "down": 1024}
GATHER_NAMES = ("small", "out", "up", "down")
GATHER_PARTS = (
    ("small", 0, 256, False),
    ("out", 0, 1024, False),
    ("up", 0, 2048, False),
    ("up", 2048, 1024, True),
    ("up", 3072, 1024, True),
    ("down", 0, 512, False),
    ("down", 512, 256, False),
    ("down", 768, 256, False),
)
ANYWHERE = pl.BlockSpec(memory_space=pl.ANY)
INSIDE = pl.BlockSpec(memory_space=pltpu.VMEM)


def flat_pipe(steps, offsets, count):
    out = []
    for t in range(count + max(offsets)):
        for step, d in zip(steps, offsets):
            if 0 <= t - d < count:
                out.append(functools.partial(step, t - d))
    return out


def advance(queue, n):
    for _ in range(min(n, len(queue))):
        queue.pop(0)()


def sp_peers(p):
    out = []
    for dx, dz in ((0, 1), (0, 3), (2, 0), (2, 1), (2, 3), (0, 2), (2, 2)):
        xh = p.xh if dx == 0 else 1 - p.xh
        out.append((p.to(dx=dx, dz=dz), xh * 4 + lax.rem(p.z + dz, 4)))
    return out


def nt(a, b):
    return lax.dot_general(a, b, (((1,), (1,)), ((), ())), preferred_element_type=F32)


def nn(a, b):
    return jnp.dot(a, b, preferred_element_type=F32)


def forward_kernel(*refs):
    refs = list(refs)

    def take(n):
        head = refs[:n]
        del refs[:n]
        return head

    k = len(GATHER_NAMES)
    tok, wq = take(2)
    vectors, bias_up = take(2)
    ins = dict(zip(GATHER_NAMES[1:], take(k - 1)))
    outs = dict(zip(GATHER_NAMES, take(k)))
    tall_t, wsel, qkv, lse, ctx = take(5)
    tall, small_v, pack, vt, ct, ch, cr = take(7)
    p, s = Place(), Copies(*refs)
    me = p.xh * 4 + p.z
    peers = sp_peers(p)
    pack[...] = jnp.zeros_like(pack)
    pack[0, 0:8, 0:64] = vectors[...]
    pack[0, 0:8, 192:256] = vectors[...]
    pack[0, 8:9, :] = bias_up[...]
    ins["small"] = pack
    greet(
        [p.to(dy=1), p.to(dy=2), p.to(dy=3), p.to(dx=1), p.to(dx=3), p.to(dc=1)]
        + [d for d, _ in peers]
    )
    sent = []

    def go(src, dst, dev):
        cp = s.remote(src, dst, dev)
        sent.append(cp)
        return cp

    pick = [
        s.local(
            wq.at[:, pl.ds(pl.multiple_of(j * 1024 + me * 128, 128), 128)],
            wsel.at[p.xl, p.y, p.c, :, pl.ds(j * 128, 128)],
        )
        for j in range(3)
    ]
    own_tok = s.local(tok, tall.at[me])
    across = go(tok, tall.at[me], p.to(dx=2))
    tok_cps = [go(tok, tall.at[me], p.to(dz=d)) for d in (1, 3, 2)]
    parts = [Gather(p, s, ins[m], outs[m], lo, n, quarters) for m, lo, n, quarters in GATHER_PARTS]
    parts[0].start()
    for cp in pick:
        cp.wait()
    mine = wsel.at[p.xl, p.y, p.c]
    wy = [go(mine, mine, p.to(dy=d)) for d in (1, 3, 2)]
    queue = flat_pipe(
        (
            lambda i: parts[i + 1].start(),
            lambda i: parts[i + 1].stage_x(),
            lambda i: parts[i + 1].stage_z(),
            lambda i: parts[i + 1].stage_core(),
        ),
        (0, 3, 5, 6),
        len(parts) - 1,
    )
    advance(queue, 2)
    for cp in wy:
        cp.wait_recv()
    column = wsel.at[p.xl, :, p.c]
    wx = go(column, column, p.to(dx=1 - 2 * p.xl))
    across.wait_recv()
    far = tall.at[(1 - p.xh) * 4 + p.z]
    tok_cps += [go(far, far, p.to(dz=d)) for d in (1, 3, 2)]
    parts[0].stage_x()
    advance(queue, 1)
    wx.wait_recv()
    plane = wsel.at[:, :, p.c]
    wc = go(plane, plane, p.to(dc=1))
    parts[0].stage_core()
    advance(queue, 1)
    parts[0].arrived()
    small_cp = s.local(outs["small"], small_v)
    advance(queue, 2)
    wc.wait_recv()
    small_cp.wait()
    own_tok.wait()
    for cp in tok_cps:
        cp.wait_recv()

    b, y = me // 4, me % 4
    qv = [
        small_v[b, y, 0, 0, r : r + 1, 0:128] + small_v[b, y, 1, 0, r : r + 1, 128:256]
        for r in range(2)
    ]
    bias = jnp.concatenate([qv[0], jnp.zeros((1, 128), F32), qv[1]], axis=1)

    def project(i, _):
        x = tall[pl.ds(2 * i, 2)].reshape(256, 1024)
        v = nn(x, wsel[...].reshape(1024, 384)) + bias
        qkv[pl.ds(pl.multiple_of(i * 256, 256), 256), :] = v.astype(BF)
        return 0

    lax.fori_loop(0, 4, project, 0)
    vt[...] = qkv[:, 256:384].astype(F32).T.astype(BF)
    per = max(1, (len(queue) - 4) // 4)
    for b in range(4):
        rows = pl.ds(b * 256, 256)
        for h in range(2):
            keys = qkv[:, 128 + 64 * h : 192 + 64 * h]
            st = nt(keys, qkv[rows, 64 * h : 64 * h + 64]) * 0.125
            peak = jnp.max(st, axis=0, keepdims=True)
            e = jnp.exp(st - peak)
            total = jnp.sum(e, axis=0, keepdims=True)
            c = nn(vt[64 * h : 64 * h + 64, :], e.astype(BF))
            ct[64 * h : 64 * h + 64, rows] = c / total
            lse[h : h + 1, rows] = peak + jnp.log(total)
        advance(queue, per)
    for t in range(8):
        ch[t] = ct[:, t * 128 : (t + 1) * 128].T.astype(BF)
    ctx_cps = [go(ch.at[t], cr.at[me], d) for d, t in peers]
    cr[me] = ch[me]

    def turn(t, _):
        tall_t[:, pl.ds(pl.multiple_of(t * 128, 128), 128)] = tall[t].astype(F32).T.astype(BF)
        return 0

    for t in range(4):
        lax.fori_loop(2 * t, 2 * t + 2, turn, 0)
        advance(queue, 2)
    advance(queue, len(queue))
    for cp in ctx_cps:
        cp.wait_recv()
    for t in range(8):
        ctx[:, t * 128 : (t + 1) * 128] = cr[t]
    for g in parts:
        g.finish()
    for cp in sent:
        cp.wait_send()


def attend_forward(tokens, w_qkv, vectors, bias_up, arrays):
    ins = []
    shapes = [jax.ShapeDtypeStruct((2, 4, 2, 1, 16, 256), F32)]
    for m, a in zip(GATHER_NAMES[1:], arrays):
        ins.append(a.reshape(4, ROWS[m] // 4, COLS[m]))
        shapes.append(jax.ShapeDtypeStruct((2, 4, 2) + ins[-1].shape, BF))
    k = len(shapes)
    shapes += [
        jax.ShapeDtypeStruct((1024, 1024), BF),
        jax.ShapeDtypeStruct((2, 4, 2, 64, 384), BF),
        jax.ShapeDtypeStruct((1024, 384), BF),
        jax.ShapeDtypeStruct((8, 1024), F32),
        jax.ShapeDtypeStruct((128, 1024), BF),
    ]
    out = pl.pallas_call(
        forward_kernel,
        out_shape=shapes,
        in_specs=[ANYWHERE] * 2 + [INSIDE] * 2 + [ANYWHERE] * (k - 1),
        out_specs=[ANYWHERE] * k + [INSIDE] * 5,
        scratch_shapes=[
            pltpu.VMEM((8, 128, 1024), BF),
            pltpu.VMEM((2, 4, 2, 1, 16, 256), F32),
            pltpu.VMEM((1, 16, 256), F32),
            pltpu.VMEM((128, 1024), BF),
            pltpu.VMEM((128, 1024), F32),
            pltpu.VMEM((8, 128, 128), BF),
            pltpu.VMEM((8, 128, 128), BF),
            pltpu.SemaphoreType.DMA((200,)),
            pltpu.SemaphoreType.DMA((200,)),
        ],
        compiler_params=pltpu.CompilerParams(
            collective_id=1, has_side_effects=True, vmem_limit_bytes=62 * 2**20
        ),
        name="attend_forward",
    )(tokens, w_qkv, vectors, bias_up, *ins)
    whole = [o.reshape(16 * ROWS[m], COLS[m]) for m, o in zip(GATHER_NAMES[1:], out[1:k])]
    return [out[0]] + whole + list(out[k:])


SMALL_SHAPE = (2, 4, 4, 8, 256)


class ReduceTwo(Reduce):
    def __init__(self, place, copies, order, g, bufs, total):
        self.p, self.s, self.order, self.g = place, copies, order, g
        self.r1, self.s1, self.r2 = bufs
        self.tot = total
        self.n = g.shape[-1]
        self.sent = []

    def pick(self, ref, i, v):
        if self.order[i] == "x":
            rest = [slice(None)] * (len(ref.shape) - 2)
            return ref.at[(lax.rem(v, 2),) + tuple(rest) + (self.half(v // 2),)]
        return ref.at[:, v] if i == 0 else ref.at[v]

    def share(self):
        mine = self.tot.at[self.p.z, :, self.half(self.p.xh)]
        self.add(1, self.s1, self.r2, mine, self.c2)
        self.c4 = self.go(mine, mine, dx=2)


def reduce_two_shapes(order, rows, n):
    if order[0] == "x":
        return [(3, 4, rows, n // 2), (4, rows, n // 2), (3, rows, n // 2)]
    return [(3, 2, rows, n), (2, rows, n), (3, rows, n // 2)]


class Tokens:
    def __init__(self, place, copies, axis, left, right, both_left, both_right):
        self.p, self.s, self.axis = place, copies, axis
        self.left, self.right, self.bl, self.br = left, right, both_left, both_right
        self.sent, self.cps, self.own = [], [], []

    def sources(self, t):
        if self.axis == "y":
            return self.left.at[:, t], self.right
        return self.left, self.right.at[:, pl.ds(pl.multiple_of(t * 1024, 128), 1024)]

    def send(self, side, steps=(1, 3, 2, 0)):
        me = self.p.y if self.axis == "y" else self.p.z
        slot = pl.multiple_of(me * 128, 128)
        dst = self.bl.at[me] if side == 0 else self.br.at[pl.ds(slot, 128)]
        for k in steps:
            src = self.sources(lax.rem(me + k, 4))[side]
            if k == 0:
                self.own.append(self.s.local(src, dst))
                continue
            cp = self.s.remote(src, dst, self.p.to(**{"d" + self.axis: k}))
            self.cps.append(cp)
            self.sent.append(cp)

    def swap(self):
        p, s = self.p, self.s
        for cp in self.own:
            cp.wait()
        for cp in self.cps:
            cp.wait_recv()
        lead = (slice(None),) * (1 if self.axis == "y" else 2)
        near, far = [self.bl.at[(pl.ds(k, 4),) + lead + (1 - p.c,)] for k in (0, 4)]
        self.cores = [
            s.remote(near, far, p.to(dc=1)),
            s.remote(self.br.at[pl.ds(0, 512)], self.br.at[pl.ds(512, 512)], p.to(dc=1)),
        ]
        self.sent += self.cores

    def ready(self):
        for cp in self.cores:
            cp.wait_recv()

    def multiply(self, lo, g):
        n = g.shape[-1]

        def body(b, _):
            at = (b, self.p.c) if self.axis == "y" else (b, slice(None), self.p.c)
            left = [self.bl[(k,) + at].reshape(4 * g.shape[2], 128) for k in range(8)]
            v = nn(jnp.concatenate(left, axis=1), self.br[:, lo : lo + n])
            g[b] = v.astype(BF).reshape(4, g.shape[2], n)
            return 0

        lax.fori_loop(0, 2, body, 0)

    def finish(self):
        for cp in self.sent:
            cp.wait_send()


VECTORS = (
    "bias_q",
    "bias_v",
    "bias_out",
    "gain_one",
    "shift_one",
    "bias_down",
    "gain_two",
    "shift_two",
)


def ln_rows(u):
    center = u - jnp.mean(u, axis=-1, keepdims=True)
    spread = jnp.mean(center * center, axis=-1, keepdims=True)
    inverse = lax.rsqrt(spread + epsilon)
    return center * inverse, inverse


def ln_back(e, hat, inverse, gain):
    scaled = e * gain
    centered = scaled - jnp.mean(scaled, axis=-1, keepdims=True)
    return inverse * (centered - hat * jnp.mean(scaled * hat, axis=-1, keepdims=True))


def col_sum(v):
    return jnp.sum(v, axis=0, keepdims=True)


def middle(
    tok,
    ctx,
    cot,
    small_v,
    wait_out,
    wait_up,
    wait_down,
    w_out,
    w_up,
    w_down,
    output,
    gctx,
    gsum,
    lefts,
    rights,
    small,
    vec,
    bup,
    slope,
    hat1,
    base,
    acc,
    toks,
    place,
):
    for r, name in enumerate(VECTORS):
        for j in range(8):
            a = small_v[j // 4, j % 4, 0, 0, r : r + 1, 0:128]
            b = small_v[j // 4, j % 4, 1, 0, r : r + 1, 128:256]
            vec[r : r + 1, j * 128 : (j + 1) * 128] = a + b
    for f in range(16):
        bup[0:1, f * 256 : (f + 1) * 256] = small_v[f // 8, (f // 2) % 4, f % 2, 0, 8:9, :]
    row = {n: vec[r : r + 1, :] for r, n in enumerate(VECTORS)}

    def put(name, v):
        r = VECTORS.index(name)
        for j in range(8):
            small[j // 4, j % 4, 0, r : r + 1, 0:128] = v[:, j * 128 : (j + 1) * 128]

    small[...] = jnp.zeros_like(small)
    x = tok[...].astype(F32)
    wait_out()
    branch = nn(ctx[...], w_out[...]) + row["bias_out"]
    hat, inv1 = ln_rows(x + branch)
    hat1[...] = hat
    normed = hat * row["gain_one"] + row["shift_one"]
    base[...] = normed
    low = normed.astype(BF)
    rights["low"][...] = low
    lefts["up"][...] = normed.T.astype(BF).reshape(2, 4, 2, 64, 128)
    lefts["out"][...] = ctx[...].astype(F32).T.astype(BF).reshape(2, 4, 2, 64, 128)
    toks["up"].send(0)
    toks["out"].send(0)
    acc[...] = jnp.zeros_like(acc)

    def up(t, _):
        cols = pl.ds(pl.multiple_of(t * 512, 512), 512)
        wait_up(t)
        pre = nn(rights["low"][...], w_up[t]) + bup[0:1, cols]
        cdf = 0.5 * (1.0 + lax.erf(pre * root_half))
        slope[:, cols] = cdf + pre * jnp.exp(-0.5 * pre * pre) * inv_root_two_pi
        act = pre * cdf
        lefts["down"][t // 4, lax.rem(t, 4)] = act.T.astype(BF).reshape(2, 256, 128)
        wait_down(t)
        acc[...] += nn(act.astype(BF), w_down[t])
        return 0

    lax.fori_loop(0, 8, up, 0)
    toks["down"].send(0)
    hat2, inv2 = ln_rows(base[...] + acc[...] + row["bias_down"])
    output[...] = (hat2 * row["gain_two"] + row["shift_two"]).astype(BF)
    dy = cot[...].astype(F32)
    put("gain_two", col_sum(dy * hat2))
    put("shift_two", col_sum(dy))
    gs2 = ln_back(dy, hat2, inv2, row["gain_two"])
    acc[...] = gs2
    ffn = gs2.astype(BF)
    rights["down"][...] = ffn
    toks["down"].send(1)
    put("bias_down", col_sum(ffn.astype(F32)))

    def back(k, j, _):
        t = 2 * lax.rem(place.z + k, 4) + j
        cols = pl.ds(pl.multiple_of(t * 512, 512), 512)
        pre = (nt(rights["down"][...], w_down[t]) * slope[:, cols]).astype(BF)
        rights["up"][:, cols] = pre
        s = col_sum(pre.astype(F32))
        small[t // 4, lax.rem(t, 4), 1, 0:1, :] = s[:, :256]
        small[t // 4, lax.rem(t, 4), 1, 1:2, :] = s[:, 256:]
        acc[...] += nt(pre, w_up[t])
        return 0

    for k in (1, 3, 2, 0):
        lax.fori_loop(0, 2, functools.partial(back, k), 0)
        toks["up"].send(1, (k,))
    gn = acc[...]
    hat = hat1[...]
    put("gain_one", col_sum(gn * hat))
    put("shift_one", col_sum(gn))
    gs1 = ln_back(gn, hat, inv1, row["gain_one"])
    gsum[...] = gs1
    gb = gs1.astype(BF)
    rights["out"][...] = gb
    toks["out"].send(1)
    put("bias_out", col_sum(gb.astype(F32)))
    gctx[...] = nt(gb, w_out[...]).astype(BF)


GRAD_NAMES = ("down", "up", "out")
GRAD_AXIS = {"down": "y", "up": "z", "out": "y"}
PIECE_ROWS = {"down": 64, "up": 64, "out": 16}
PIECES = (
    ("down", 0, 512, "xz"),
    ("down", 512, 512, "zx"),
    ("up", 0, 512, "yx"),
    ("up", 512, 512, "xy"),
    ("out", 0, 1024, "zx"),
)


def backward_kernel(*refs):
    refs = list(refs)

    def take(n):
        head = refs[:n]
        del refs[:n]
        return head

    k = len(GRAD_NAMES)
    tok, ctx, cot, small_h, out_h, up_h, down_h, tall_t, wsel, qkv, lse = take(11)
    totals = dict(zip(GRAD_NAMES, take(k)))
    small_total, grad_tok, gw, output = take(4)
    small_v, w_out, w_up, w_down, low, vec, bup, slope, hat1, base, acc, sem = take(12)
    gctx, gsum = take(2)
    left = dict(zip(GRAD_NAMES, take(k)))
    right = dict(zip(GRAD_NAMES, take(k)))
    both_left = dict(zip(GRAD_NAMES, take(k)))
    both_right = dict(zip(GRAD_NAMES, take(k)))
    small_src, small_in, small_g = take(3)
    small_bufs = take(5)
    g, bufs = [], []
    for _ in PIECES:
        g += take(1)
        bufs.append(take(3))
    do, kt, dqt, dkv, dqkv, gq, gq_c, gq_x, gq_y = take(9)
    dts, dtx, dtxr, dtz, dtz_s, dtzr = take(6)
    bq, bq_c, bq_s, bq_x, bq_y, bw = take(6)
    vec_cp = pltpu.make_async_copy(small_h, small_v, sem.at[0])
    out_cp = pltpu.make_async_copy(out_h, w_out, sem.at[1])
    vec_cp.start()
    out_cp.start()
    for t in range(8):
        pltpu.make_async_copy(up_h.at[:, pl.ds(t * 512, 512)], w_up.at[t], sem.at[2 + t]).start()
        pltpu.make_async_copy(down_h.at[pl.ds(t * 512, 512)], w_down.at[t], sem.at[10 + t]).start()

    def wait_up(t):
        pltpu.make_async_copy(up_h.at[:, pl.ds(0, 512)], w_up.at[t], sem.at[2 + t]).wait()

    def wait_down(t):
        pltpu.make_async_copy(down_h.at[pl.ds(0, 512)], w_down.at[t], sem.at[10 + t]).wait()

    p, s = Place(), Copies(*refs)
    me = p.xh * 4 + p.z
    peers = sp_peers(p)
    greet(
        [p.to(dy=1), p.to(dy=2), p.to(dy=3), p.to(dx=1), p.to(dx=3), p.to(dc=1)]
        + [d for d, _ in peers]
    )
    sent = []

    def go(src, dst, dev):
        cp = s.remote(src, dst, dev)
        sent.append(cp)
        return cp

    toks = {
        m: Tokens(p, s, GRAD_AXIS[m], left[m], right[m], both_left[m], both_right[m])
        for m in GRAD_NAMES
    }
    vec_cp.wait()
    middle(
        tok,
        ctx,
        cot,
        small_v,
        out_cp.wait,
        wait_up,
        wait_down,
        w_out,
        w_up,
        w_down,
        output,
        gctx,
        gsum,
        left,
        dict(right, low=low),
        small_src,
        vec,
        bup,
        slope,
        hat1,
        base,
        acc,
        toks,
        p,
    )
    do_cps = [
        go(gctx.at[:, pl.ds(pl.multiple_of(t * 128, 128), 128)], do.at[me], d) for d, t in peers
    ]
    do_own = s.local(gctx.at[:, pl.ds(pl.multiple_of(me * 128, 128), 128)], do.at[me])
    small_swap = s.remote(small_src, small_in, p.to(dc=1))
    small_red = Reduce(p, s, "xyz", small_g, small_bufs, small_total)
    toks["down"].swap()
    red = [
        ReduceTwo(p, s, o, gi, b, totals[m].at[:, :, pl.ds(lo, n)])
        for (m, lo, n, o), gi, b in zip(PIECES, g, bufs)
    ]
    kt[...] = qkv[:, 128:256].astype(F32).T.astype(BF)
    toks["up"].swap()
    ready = set()

    def begin(i):
        m, lo, _, _ = PIECES[i]
        if m not in ready:
            toks[m].ready()
            ready.add(m)
        toks[m].multiply(lo, g[i])
        red[i].first()

    begin(0)
    begin(1)
    small_swap.wait_recv()
    small_g[...] = small_src[...] + small_in[...]
    small_red.first()
    do_own.wait()
    for cp in do_cps:
        cp.wait_recv()
    dkv[...] = jnp.zeros_like(dkv)

    def head_block(b, h):
        rows = pl.ds(b * 256, 256)
        lanes = slice(64 * h, 64 * h + 64)
        keys = qkv[:, 128 + 64 * h : 192 + 64 * h]
        vals = qkv[:, 256 + 64 * h : 320 + 64 * h]
        q = qkv[rows, lanes]
        dob = do[2 * b : 2 * b + 2].reshape(256, 128)[:, lanes]
        probs = jnp.exp(nt(keys, q) * 0.125 - lse[h : h + 1, rows])
        dp = nt(vals, dob)
        inner = jnp.sum(probs * dp, axis=0, keepdims=True)
        ds = (probs * (dp - inner)).astype(BF)
        dqt[lanes, rows] = nn(kt[lanes, :], ds) * 0.125
        dkv[:, lanes] += nn(ds, q) * 0.125
        dkv[:, 128 + 64 * h : 192 + 64 * h] += nn(probs.astype(BF), dob)

    for b in range(4):
        for h in range(2):
            head_block(b, h)
        if b == 0:
            begin(2)
            toks["out"].swap()
        if b == 1:
            begin(3)
            red[0].second()
        if b == 2:
            begin(4)
            red[1].second()
    dqkv[:, :128] = dqt[...].T.astype(BF)
    dqkv[:, 128:] = dkv[...].astype(BF)

    def part(i, _):
        rows = pl.ds(pl.multiple_of(i * 256, 256), 256)
        v = nt(dqkv[rows, :], wsel[...].reshape(1024, 384)).astype(BF)
        dts[i // 2, pl.ds(2 * lax.rem(i, 2), 2)] = v.reshape(2, 128, 1024)
        return 0

    lax.fori_loop(0, 4, part, 0)
    first, second = pl.ds(0, 512), pl.ds(512, 512)
    dx_cp = go(dts.at[1 - p.xh, :, :, first], dtx, p.to(dx=2))
    dz_cps = [
        go(dts.at[:, lax.rem(p.z + d, 4), :, second], dtz.at[d - 1], p.to(dz=d)) for d in (1, 3, 2)
    ]

    def rows_of(i, _):
        v = nn(tall_t[pl.ds(pl.multiple_of(i * 256, 256), 256), :], dqkv[...])
        gq[pl.ds(2 * i, 2)] = v.astype(BF).reshape(2, 2, 64, 384)
        return 0

    lax.fori_loop(0, 4, rows_of, 0)
    c_cp = go(gq.at[:, 1 - p.c], gq_c, p.to(dc=1))
    cols = jnp.sum(dqkv[...].astype(F32), axis=0, keepdims=True)
    bq[...] = jnp.zeros_like(bq)
    bq[0:1, :] = cols[:, :128]
    bq[1:2, :] = cols[:, 256:]
    bc_cp = go(bq, bq_c, p.to(dc=1))
    small_red.second()
    red[2].second()
    red[3].second()
    c_cp.wait_recv()

    def add_core(i, _):
        gq_c[i] = (gq_c[i].astype(F32) + gq[i, p.c].astype(F32)).astype(BF)
        return 0

    lax.fori_loop(0, 8, add_core, 0)
    x_cp = go(gq_c.at[pl.ds((1 - p.xl) * 4, 4)], gq_x, p.to(dx=1 - 2 * p.xl))
    bc_cp.wait_recv()
    bq_s[0] = bq[...] + bq_c[...]
    bx_cp = go(bq_s.at[0], bq_x, p.to(dx=1 - 2 * p.xl))
    red[4].second()
    small_red.third()
    red[0].share()
    red[1].share()
    x_cp.wait_recv()

    def add_x(i, _):
        gq_x[i] = (gq_x[i].astype(F32) + gq_c[p.xl * 4 + i].astype(F32)).astype(BF)
        return 0

    lax.fori_loop(0, 4, add_x, 0)
    y_cps = [go(gq_x.at[lax.rem(p.y + d, 4)], gq_y.at[d - 1], p.to(dy=d)) for d in (1, 3, 2)]
    bx_cp.wait_recv()
    bq_s[1] = bq_s[0] + bq_x[...]
    by_cps = [go(bq_s.at[1], bq_y.at[d - 1], p.to(dy=d)) for d in (1, 3, 2)]
    dx_cp.wait_recv()

    def add_far(i, _):
        dtx[i] = (dtx[i].astype(F32) + dts[p.xh, i, :, 0:512].astype(F32)).astype(BF)
        return 0

    lax.fori_loop(0, 4, add_far, 0)
    dz2_cps = [go(dtx.at[lax.rem(p.z + d, 4)], dtxr.at[d - 1], p.to(dz=d)) for d in (1, 3, 2)]
    for cp in dz_cps:
        cp.wait_recv()

    def add_round(i, _):
        v = dts[i, p.z, :, 512:1024].astype(F32)
        for d in range(3):
            v = v + dtz[d, i].astype(F32)
        dtz_s[i] = v.astype(BF)
        return 0

    lax.fori_loop(0, 2, add_round, 0)
    dx2_cp = go(dtz_s.at[1 - p.xh], dtzr, p.to(dx=2))
    red[2].share()
    red[3].share()
    red[4].share()
    small_red.share()
    red[0].spread()
    red[1].spread()
    for cp in y_cps:
        cp.wait_recv()
    acc = gq_x[p.y].astype(F32)
    for i in range(3):
        acc = acc + gq_y[i].astype(F32)
    gw[me] = acc.astype(BF)
    for cp in by_cps:
        cp.wait_recv()
    bw[me] = ((bq_s[1] + bq_y[0]) + (bq_y[1] + bq_y[2]))[0:8, :]
    gw_cps = [go(gw.at[me], gw.at[me], d) for d, _ in peers]
    gw_cps += [go(bw.at[me], bw.at[me], d) for d, _ in peers]
    red[2].spread()
    red[3].spread()
    red[4].spread()
    small_red.spread()
    for cp in dz2_cps:
        cp.wait_recv()
    dx2_cp.wait_recv()
    acc = gsum[:, 0:512] + dtx[p.z].astype(F32)
    for t in range(3):
        acc = acc + dtxr[t].astype(F32)
    grad_tok[:, 0:512] = acc.astype(BF)
    acc = gsum[:, 512:1024] + dtz_s[p.xh].astype(F32) + dtzr[...].astype(F32)
    grad_tok[:, 512:1024] = acc.astype(BF)
    for cp in gw_cps:
        cp.wait_recv()
    for r in red:
        r.done()
    small_red.done()
    for r in red:
        r.finish()
    for m in GRAD_NAMES:
        toks[m].finish()
    small_red.finish()
    small_swap.wait_send()
    small_total[0, 0:2, 0:128] = bw[p.xl * 4 + p.y, 0:2, :]
    for cp in sent:
        cp.wait_send()


def finish_layer(tok, ctx, cot, small_h, out_h, up_h, down_h, tall_t, wsel, qkv, lse):
    scratch = [
        pltpu.VMEM((2, 4, 2, 1, 16, 256), F32),
        pltpu.VMEM((1024, 1024), BF),
        pltpu.VMEM((8, 1024, 512), BF),
        pltpu.VMEM((8, 512, 1024), BF),
        pltpu.VMEM((128, 1024), BF),
        pltpu.VMEM((8, 1024), F32),
        pltpu.VMEM((8, 4096), F32),
        pltpu.VMEM((128, 4096), F32),
        pltpu.VMEM((128, 1024), F32),
        pltpu.VMEM((128, 1024), F32),
        pltpu.VMEM((128, 1024), F32),
        pltpu.SemaphoreType.DMA((18,)),
        pltpu.VMEM((128, 1024), BF),
        pltpu.VMEM((128, 1024), F32),
    ]
    scratch += [pltpu.VMEM((2, 4, 2, ROWS[m], 128), BF) for m in GRAD_NAMES]
    scratch += [pltpu.VMEM((128, COLS[m]), BF) for m in GRAD_NAMES]
    scratch += [
        pltpu.VMEM((8, 2, 2, ROWS[m], 128) if GRAD_AXIS[m] == "y" else (8, 2, 4, 2, ROWS[m], 128), BF)
        for m in GRAD_NAMES
    ]
    scratch += [pltpu.VMEM((1024, 1024), BF) for m in GRAD_NAMES]
    scratch += [pltpu.VMEM(SMALL_SHAPE, F32)] * 3
    scratch += [pltpu.VMEM(x, F32) for x in reduce_shapes("xyz", 8, 256)]
    for m, _, n, o in PIECES:
        scratch.append(pltpu.VMEM((2, 4, PIECE_ROWS[m], n), BF))
        scratch += [pltpu.VMEM(x, BF) for x in reduce_two_shapes(o, PIECE_ROWS[m], n)]
    scratch += [
        pltpu.VMEM((8, 128, 128), BF),
        pltpu.VMEM((128, 1024), BF),
        pltpu.VMEM((128, 1024), F32),
        pltpu.VMEM((1024, 256), F32),
        pltpu.VMEM((1024, 384), BF),
        pltpu.VMEM((8, 2, 64, 384), BF),
        pltpu.VMEM((8, 64, 384), BF),
        pltpu.VMEM((4, 64, 384), BF),
        pltpu.VMEM((3, 64, 384), BF),
        pltpu.VMEM((2, 4, 128, 1024), BF),
        pltpu.VMEM((4, 128, 512), BF),
        pltpu.VMEM((3, 128, 512), BF),
        pltpu.VMEM((3, 2, 128, 512), BF),
        pltpu.VMEM((2, 128, 512), BF),
        pltpu.VMEM((128, 512), BF),
        pltpu.VMEM((8, 128), F32),
        pltpu.VMEM((8, 128), F32),
        pltpu.VMEM((2, 8, 128), F32),
        pltpu.VMEM((8, 128), F32),
        pltpu.VMEM((3, 8, 128), F32),
        pltpu.VMEM((8, 8, 128), F32),
    ]
    scratch += [pltpu.SemaphoreType.DMA((250,)), pltpu.SemaphoreType.DMA((250,))]
    k = len(GRAD_NAMES)
    out = pl.pallas_call(
        backward_kernel,
        out_shape=[jax.ShapeDtypeStruct((4, PIECE_ROWS[m], 1024), BF) for m in GRAD_NAMES]
        + [
            jax.ShapeDtypeStruct((4, 8, 256), F32),
            jax.ShapeDtypeStruct((128, 1024), BF),
            jax.ShapeDtypeStruct((8, 64, 384), BF),
            jax.ShapeDtypeStruct((128, 1024), BF),
        ],
        in_specs=[INSIDE] * 3 + [ANYWHERE] * 4 + [INSIDE] * 4,
        out_specs=[INSIDE] * (k + 4),
        scratch_shapes=scratch,
        compiler_params=pltpu.CompilerParams(
            collective_id=2, has_side_effects=True, vmem_limit_bytes=62 * 2**20
        ),
        name="layer_back",
    )(tok, ctx, cot, small_h, out_h, up_h, down_h, tall_t, wsel, qkv, lse)
    grads = {
        "down": out[0].reshape(256, 1024).astype(F32),
        "up": out[1].transpose(1, 0, 2).reshape(64, 4096).astype(F32),
        "out": out[2].reshape(64, 1024).astype(F32),
    }
    gw = out[k + 2].reshape(8, 64, 3, 128).transpose(1, 2, 0, 3)
    grads["qkv"] = gw.reshape(64, 3072).astype(F32)
    return grads, out[k], out[k + 1], out[k + 3]


def on_device(
    tokens,
    cotangent,
    w_qkv,
    bias_q,
    bias_v,
    w_out,
    bias_out,
    gain_one,
    shift_one,
    w_up,
    bias_up,
    w_down,
    bias_down,
    gain_two,
    shift_two,
):
    num_seqs, slice_len, model_width = tokens.shape
    row_count = num_seqs * slice_len
    inputs = tokens.reshape(row_count, model_width)
    own = dict(
        bias_q=bias_q,
        bias_v=bias_v,
        bias_out=bias_out,
        gain_one=gain_one,
        shift_one=shift_one,
        bias_down=bias_down,
        gain_two=gain_two,
        shift_two=shift_two,
    )
    vectors = jnp.stack([own[k] for k in VECTORS]).astype(F32)
    small, full_out, full_up, full_down, tall_t, wsel, qkv, lse, context_tokens = attend_forward(
        inputs, w_qkv, vectors, bias_up.astype(F32).reshape(1, 256), [w_out, w_up, w_down]
    )
    grads, total, grad_inputs, output = finish_layer(
        inputs,
        context_tokens,
        cotangent.reshape(row_count, model_width),
        small,
        full_out,
        full_up,
        full_down,
        tall_t,
        wsel,
        qkv,
        lse,
    )
    core = lax.axis_index("fsdp") % 2
    mine = lax.dynamic_slice(total, (0, 0, core * 64), (1, 8, 64))
    res = {k: mine[0, r] for r, k in enumerate(VECTORS)}
    res["bias_up"] = lax.dynamic_slice(total, (1, core, 0), (1, 1, 256)).reshape(256)
    return (
        output.reshape(tokens.shape),
        grad_inputs.reshape(tokens.shape),
        grads["qkv"],
        res["bias_q"],
        res["bias_v"],
        grads["out"],
        res["bias_out"],
        res["gain_one"],
        res["shift_one"],
        grads["up"],
        res["bias_up"],
        grads["down"],
        res["bias_down"],
        res["gain_two"],
        res["shift_two"],
    )


def solution(mesh):
    rows, vector = P("fsdp", None), P("fsdp")
    block = P("fsdp", "sp", None)
    params = (rows, vector, vector, rows, vector, vector, vector)
    params += (rows, vector, rows, vector, vector, vector)
    return jax.shard_map(
        on_device,
        mesh=mesh,
        in_specs=(block, block) + params,
        out_specs=(block, block) + params,
        check_vma=False,
    )
```

```python
import functools
import math

import jax
import jax.numpy as jnp
from jax import lax
from jax.experimental import pallas as pl
from jax.experimental.pallas import tpu as pltpu
from jax.sharding import PartitionSpec as P

HD = 64
MESH = pl.DeviceIdType.MESH
BF = jnp.bfloat16
F32 = jnp.float32

epsilon = 1e-05
root_half = 0.7071067811865476
inv_root_two_pi = 0.3989422804014327


class Place:
    def __init__(self):
        f = lax.axis_index("fsdp")
        s = lax.axis_index("sp")
        self.xh, self.xl, self.y, self.z, self.c = s // 4, f // 8, (f // 2) % 4, s % 4, f % 2
        self.x = 2 * self.xh + self.xl

    def to(self, dx=0, dy=0, dz=0, dc=0):
        x = lax.rem(self.x + dx + 4, 4)
        y = lax.rem(self.y + dy + 4, 4)
        z = lax.rem(self.z + dz + 4, 4)
        c = self.c if dc == 0 else 1 - self.c
        return ((x % 2) * 8 + y * 2 + c, (x // 2) * 4 + z)


class Copies:
    def __init__(self, send, recv):
        self.send, self.recv, self.n = send, recv, 0

    def remote(self, src, dst, dev):
        i = self.n
        self.n += 1
        cp = pltpu.make_async_remote_copy(
            src_ref=src,
            dst_ref=dst,
            send_sem=self.send.at[i],
            recv_sem=self.recv.at[i],
            device_id=dev,
            device_id_type=MESH,
        )
        cp.start()
        return cp

    def local(self, src, dst):
        i = self.n
        self.n += 1
        cp = pltpu.make_async_copy(src, dst, self.recv.at[i])
        cp.start()
        return cp


def greet(targets):
    bar = pltpu.get_barrier_semaphore()
    for t in targets:
        pl.semaphore_signal(bar, inc=1, device_id=t, device_id_type=MESH)
    pl.semaphore_wait(bar, len(targets))


class Gather:
    def __init__(self, place, copies, src, out, lo, n, quarters):
        self.p, self.s, self.src, self.out = place, copies, src, out
        self.lo, self.n, self.quarters = lo, n, quarters
        self.sent, self.core = [], []

    def cols(self, half=None):
        if half is None:
            return pl.ds(self.lo, self.n)
        return pl.ds(self.lo + half * (self.n // 2), self.n // 2)

    def go(self, src, dst, **k):
        cp = self.s.remote(src, dst, self.p.to(**k))
        self.sent.append(cp)
        return cp

    def q(self):
        return self.p.z if self.quarters else slice(None)

    def start(self):
        p, o, q = self.p, self.out, self.q()
        self.own = self.s.local(
            self.src.at[:, :, self.cols()], o.at[p.xl, p.y, p.c, :, :, self.cols()]
        )
        self.ycp = [
            self.go(
                self.src.at[q, :, self.cols()], o.at[p.xl, p.y, p.c, q, :, self.cols()], dy=k
            )
            for k in (1, 3, 2)
        ]
        self.xcp = [
            self.go(
                self.src.at[q, :, self.cols(h)], o.at[p.xl, p.y, p.c, q, :, self.cols(h)], dx=dx
            )
            for h, dx in ((0, 1), (1, -1))
        ]

    def stage_x(self):
        p, o, q = self.p, self.out, self.q()
        for k, cp in zip((3, 1, 2), self.ycp):
            cp.wait_recv()
            for h, dx in ((0, 1), (1, -1)):
                r = o.at[p.xl, lax.rem(p.y + k, 4), p.c, q, :, self.cols(h)]
                self.xcp.append(self.go(r, r, dx=dx))
        if self.quarters:
            self.zcp = []
            for dz in (1, 3, 2):
                for k in (1, 2, 3):
                    r = o.at[p.xl, lax.rem(p.y + k, 4), p.c, q, :, self.cols()]
                    self.zcp.append(self.go(r, r, dz=dz))
        else:
            self.own.wait()
            r = o.at[p.xl, :, p.c, :, :, self.cols()]
            self.core.append(self.go(r, r, dc=1))

    def stage_z(self):
        if not self.quarters:
            return
        p, o, q = self.p, self.out, self.q()
        for cp in self.xcp:
            cp.wait_recv()
        for dz in (1, 3, 2):
            r = o.at[1 - p.xl, :, p.c, q, :, self.cols()]
            self.zcp.append(self.go(r, r, dz=dz))

    def stage_core(self):
        p, o = self.p, self.out
        if self.quarters:
            for cp in self.zcp:
                cp.wait_recv()
            self.own.wait()
            r = o.at[p.xl, :, p.c, :, :, self.cols()]
            self.core.append(self.go(r, r, dc=1))
        else:
            for cp in self.xcp:
                cp.wait_recv()
        r = o.at[1 - p.xl, :, p.c, :, :, self.cols()]
        self.core.append(self.go(r, r, dc=1))

    def arrived(self):
        for cp in self.core:
            cp.wait_recv()
        self.core = []

    def finish(self):
        self.arrived()
        for cp in self.sent:
            cp.wait_send()


class Reduce:
    def __init__(self, place, copies, order, g, bufs, total):
        self.p, self.s, self.order, self.g = place, copies, order, g
        self.r1, self.s1, self.r2, self.s2, self.r3 = bufs
        self.tot = total
        self.n = g.shape[-1]
        self.sent = []

    def go(self, src, dst, **k):
        cp = self.s.remote(src, dst, self.p.to(**k))
        self.sent.append(cp)
        return cp

    def half(self, xh):
        m = self.n // 2
        return pl.ds(pl.multiple_of(xh * m, 128), m)

    def me(self, i):
        return {"x": self.p.x, "y": self.p.y, "z": self.p.z}[self.order[i]]

    def pick(self, ref, i, v):
        o, ax = self.order, self.order[i]
        if ax == "x":
            rest = [slice(None)] * (len(ref.shape) - 2)
            return ref.at[(lax.rem(v, 2),) + tuple(rest) + (self.half(v // 2),)]
        lead = 0 if "x" in o[:i] else 1
        if ax == "z" and "y" not in o[:i]:
            lead += 1
        return ref.at[(slice(None),) * lead + (v,)]

    def scatter(self, i, src, recv):
        me = self.me(i)
        return [
            self.go(
                self.pick(src, i, lax.rem(me + k, 4)), recv.at[k - 1], **{"d" + self.order[i]: k}
            )
            for k in (1, 3, 2)
        ]

    def add(self, i, src, recv, out, cps):
        for cp in cps:
            cp.wait_recv()
        own = self.pick(src, i, self.me(i))
        shape = out.shape
        rows = (slice(None), slice(None))

        def one(idx):
            acc = own[idx].astype(F32)
            for k in range(3):
                acc = acc + recv[(k,) + idx].astype(F32)
            out[idx] = acc.astype(out.dtype)

        if len(shape) == 2:
            one(rows)
            return

        def body(j, _):
            idx = []
            for d in reversed(shape[:-2]):
                idx.insert(0, lax.rem(j, d))
                j = j // d
            one(tuple(idx) + rows)
            return 0

        lax.fori_loop(0, math.prod(shape[:-2]), body, 0)

    def first(self):
        self.c1 = self.scatter(0, self.g, self.r1)

    def second(self):
        self.add(0, self.g, self.r1, self.s1, self.c1)
        self.c2 = self.scatter(1, self.s1, self.r2)

    def third(self):
        self.add(1, self.s1, self.r2, self.s2, self.c2)
        self.c3 = self.scatter(2, self.s2, self.r3)

    def share(self):
        p = self.p
        mine = self.tot.at[p.z, :, self.half(p.xh)]
        self.add(2, self.s2, self.r3, mine, self.c3)
        self.c4 = self.go(mine, mine, dx=2)

    def spread(self):
        self.c4.wait_recv()
        r = self.tot.at[self.p.z]
        self.c5 = [self.go(r, r, dz=k) for k in (1, 3, 2)]

    def done(self):
        for cp in self.c5:
            cp.wait_recv()

    def finish(self):
        for cp in self.sent:
            cp.wait_send()


def reduce_shapes(order, q, n):
    full = {"x": 2, "y": 4, "z": 4}
    left, width, out = ["x", "y", "z"], n, []
    for i, ax in enumerate(order):
        left.remove(ax)
        if ax == "x":
            width = n // 2
        s = tuple(full[a] for a in left) + (q, width)
        out.append((3,) + s)
        if i < 2:
            out.append(s)
    return out


ROWS = {"small": 16, "out": 64, "up": 64, "down": 256}
COLS = {"small": 256, "out": 1024, "up": 4096, "down": 1024}
GATHER_NAMES = ("small", "out", "up", "down")
GATHER_PARTS = (
    ("small", 0, 256, False),
    ("out", 0, 1024, False),
    ("up", 0, 2048, False),
    ("up", 2048, 1024, True),
    ("up", 3072, 1024, True),
    ("down", 0, 512, False),
    ("down", 512, 256, False),
    ("down", 768, 256, False),
)
ANYWHERE = pl.BlockSpec(memory_space=pl.ANY)
INSIDE = pl.BlockSpec(memory_space=pltpu.VMEM)


def flat_pipe(steps, offsets, count):
    out = []
    for t in range(count + max(offsets)):
        for step, d in zip(steps, offsets):
            if 0 <= t - d < count:
                out.append(functools.partial(step, t - d))
    return out


def advance(queue, n):
    for _ in range(min(n, len(queue))):
        queue.pop(0)()


def sp_peers(p):
    out = []
    for dx, dz in ((0, 1), (0, 3), (2, 0), (2, 1), (2, 3), (0, 2), (2, 2)):
        xh = p.xh if dx == 0 else 1 - p.xh
        out.append((p.to(dx=dx, dz=dz), xh * 4 + lax.rem(p.z + dz, 4)))
    return out


def nt(a, b):
    return lax.dot_general(a, b, (((1,), (1,)), ((), ())), preferred_element_type=F32)


def nn(a, b):
    return jnp.dot(a, b, preferred_element_type=F32)


def forward_kernel(*refs):
    refs = list(refs)

    def take(n):
        head = refs[:n]
        del refs[:n]
        return head

    k = len(GATHER_NAMES)
    tok, wq = take(2)
    vectors, bias_up = take(2)
    ins = dict(zip(GATHER_NAMES[1:], take(k - 1)))
    outs = dict(zip(GATHER_NAMES, take(k)))
    tall_t, wsel, qkv, lse, ctx = take(5)
    tall, small_v, pack, vt, ct, ch, cr = take(7)
    p, s = Place(), Copies(*refs)
    me = p.xh * 4 + p.z
    peers = sp_peers(p)
    pack[...] = jnp.zeros_like(pack)
    pack[0, 0:8, 0:64] = vectors[...]
    pack[0, 0:8, 192:256] = vectors[...]
    pack[0, 8:9, :] = bias_up[...]
    ins["small"] = pack
    greet(
        [p.to(dy=1), p.to(dy=2), p.to(dy=3), p.to(dx=1), p.to(dx=3), p.to(dc=1)]
        + [d for d, _ in peers]
    )
    sent = []

    def go(src, dst, dev):
        cp = s.remote(src, dst, dev)
        sent.append(cp)
        return cp

    pick = [
        s.local(
            wq.at[:, pl.ds(pl.multiple_of(j * 1024 + me * 128, 128), 128)],
            wsel.at[p.xl, p.y, p.c, :, pl.ds(j * 128, 128)],
        )
        for j in range(3)
    ]
    own_tok = s.local(tok, tall.at[me])
    across = go(tok, tall.at[me], p.to(dx=2))
    tok_cps = [go(tok, tall.at[me], p.to(dz=d)) for d in (1, 3, 2)]
    parts = [Gather(p, s, ins[m], outs[m], lo, n, quarters) for m, lo, n, quarters in GATHER_PARTS]
    parts[0].start()
    for cp in pick:
        cp.wait()
    mine = wsel.at[p.xl, p.y, p.c]
    wy = [go(mine, mine, p.to(dy=d)) for d in (1, 3, 2)]
    queue = flat_pipe(
        (
            lambda i: parts[i + 1].start(),
            lambda i: parts[i + 1].stage_x(),
            lambda i: parts[i + 1].stage_z(),
            lambda i: parts[i + 1].stage_core(),
        ),
        (0, 3, 5, 6),
        len(parts) - 1,
    )
    advance(queue, 2)
    for cp in wy:
        cp.wait_recv()
    column = wsel.at[p.xl, :, p.c]
    wx = go(column, column, p.to(dx=1 - 2 * p.xl))
    across.wait_recv()
    far = tall.at[(1 - p.xh) * 4 + p.z]
    tok_cps += [go(far, far, p.to(dz=d)) for d in (1, 3, 2)]
    parts[0].stage_x()
    advance(queue, 1)
    wx.wait_recv()
    plane = wsel.at[:, :, p.c]
    wc = go(plane, plane, p.to(dc=1))
    parts[0].stage_core()
    advance(queue, 1)
    parts[0].arrived()
    small_cp = s.local(outs["small"], small_v)
    advance(queue, 2)
    wc.wait_recv()
    small_cp.wait()
    own_tok.wait()
    for cp in tok_cps:
        cp.wait_recv()

    b, y = me // 4, me % 4
    qv = [
        small_v[b, y, 0, 0, r : r + 1, 0:128] + small_v[b, y, 1, 0, r : r + 1, 128:256]
        for r in range(2)
    ]
    bias = jnp.concatenate([qv[0], jnp.zeros((1, 128), F32), qv[1]], axis=1)

    def project(i, _):
        x = tall[pl.ds(2 * i, 2)].reshape(256, 1024)
        v = nn(x, wsel[...].reshape(1024, 384)) + bias
        qkv[pl.ds(pl.multiple_of(i * 256, 256), 256), :] = v.astype(BF)
        return 0

    lax.fori_loop(0, 4, project, 0)
    vt[...] = qkv[:, 256:384].astype(F32).T.astype(BF)
    per = max(1, (len(queue) - 4) // 4)
    for b in range(4):
        rows = pl.ds(b * 256, 256)
        for h in range(2):
            keys = qkv[:, 128 + 64 * h : 192 + 64 * h]
            st = nt(keys, qkv[rows, 64 * h : 64 * h + 64]) * 0.125
            peak = jnp.max(st, axis=0, keepdims=True)
            e = jnp.exp(st - peak)
            total = jnp.sum(e, axis=0, keepdims=True)
            c = nn(vt[64 * h : 64 * h + 64, :], e.astype(BF))
            ct[64 * h : 64 * h + 64, rows] = c / total
            lse[h : h + 1, rows] = peak + jnp.log(total)
        advance(queue, per)
    for t in range(8):
        ch[t] = ct[:, t * 128 : (t + 1) * 128].T.astype(BF)
    ctx_cps = [go(ch.at[t], cr.at[me], d) for d, t in peers]
    cr[me] = ch[me]

    def turn(t, _):
        tall_t[:, pl.ds(pl.multiple_of(t * 128, 128), 128)] = tall[t].astype(F32).T.astype(BF)
        return 0

    for t in range(4):
        lax.fori_loop(2 * t, 2 * t + 2, turn, 0)
        advance(queue, 2)
    advance(queue, len(queue))
    for cp in ctx_cps:
        cp.wait_recv()
    for t in range(8):
        ctx[:, t * 128 : (t + 1) * 128] = cr[t]
    for g in parts:
        g.finish()
    for cp in sent:
        cp.wait_send()


def attend_forward(tokens, w_qkv, vectors, bias_up, arrays):
    ins = []
    shapes = [jax.ShapeDtypeStruct((2, 4, 2, 1, 16, 256), F32)]
    for m, a in zip(GATHER_NAMES[1:], arrays):
        ins.append(a.reshape(4, ROWS[m] // 4, COLS[m]))
        shapes.append(jax.ShapeDtypeStruct((2, 4, 2) + ins[-1].shape, BF))
    k = len(shapes)
    shapes += [
        jax.ShapeDtypeStruct((1024, 1024), BF),
        jax.ShapeDtypeStruct((2, 4, 2, 64, 384), BF),
        jax.ShapeDtypeStruct((1024, 384), BF),
        jax.ShapeDtypeStruct((8, 1024), F32),
        jax.ShapeDtypeStruct((128, 1024), BF),
    ]
    out = pl.pallas_call(
        forward_kernel,
        out_shape=shapes,
        in_specs=[ANYWHERE] * 2 + [INSIDE] * 2 + [ANYWHERE] * (k - 1),
        out_specs=[ANYWHERE] * k + [INSIDE] * 5,
        scratch_shapes=[
            pltpu.VMEM((8, 128, 1024), BF),
            pltpu.VMEM((2, 4, 2, 1, 16, 256), F32),
            pltpu.VMEM((1, 16, 256), F32),
            pltpu.VMEM((128, 1024), BF),
            pltpu.VMEM((128, 1024), F32),
            pltpu.VMEM((8, 128, 128), BF),
            pltpu.VMEM((8, 128, 128), BF),
            pltpu.SemaphoreType.DMA((200,)),
            pltpu.SemaphoreType.DMA((200,)),
        ],
        compiler_params=pltpu.CompilerParams(
            collective_id=1, has_side_effects=True, vmem_limit_bytes=62 * 2**20
        ),
        name="attend_forward",
    )(tokens, w_qkv, vectors, bias_up, *ins)
    whole = [o.reshape(16 * ROWS[m], COLS[m]) for m, o in zip(GATHER_NAMES[1:], out[1:k])]
    return [out[0]] + whole + list(out[k:])


SMALL_SHAPE = (2, 4, 4, 8, 256)


class ReduceTwo(Reduce):
    def __init__(self, place, copies, order, g, bufs, total):
        self.p, self.s, self.order, self.g = place, copies, order, g
        self.r1, self.s1, self.r2 = bufs
        self.tot = total
        self.n = g.shape[-1]
        self.sent = []

    def pick(self, ref, i, v):
        if self.order[i] == "x":
            rest = [slice(None)] * (len(ref.shape) - 2)
            return ref.at[(lax.rem(v, 2),) + tuple(rest) + (self.half(v // 2),)]
        return ref.at[:, v] if i == 0 else ref.at[v]

    def share(self):
        mine = self.tot.at[self.p.z, :, self.half(self.p.xh)]
        self.add(1, self.s1, self.r2, mine, self.c2)
        self.c4 = self.go(mine, mine, dx=2)


def reduce_two_shapes(order, rows, n):
    if order[0] == "x":
        return [(3, 4, rows, n // 2), (4, rows, n // 2), (3, rows, n // 2)]
    return [(3, 2, rows, n), (2, rows, n), (3, rows, n // 2)]


class Tokens:
    def __init__(self, place, copies, axis, left, right, both_left, both_right):
        self.p, self.s, self.axis = place, copies, axis
        self.left, self.right, self.bl, self.br = left, right, both_left, both_right
        self.sent, self.cps, self.own = [], [], []

    def sources(self, t):
        if self.axis == "y":
            return self.left.at[:, t], self.right
        return self.left, self.right.at[:, pl.ds(pl.multiple_of(t * 1024, 128), 1024)]

    def send(self, side, steps=(1, 3, 2, 0)):
        me = self.p.y if self.axis == "y" else self.p.z
        slot = pl.multiple_of(me * 128, 128)
        dst = self.bl.at[me] if side == 0 else self.br.at[pl.ds(slot, 128)]
        for k in steps:
            src = self.sources(lax.rem(me + k, 4))[side]
            if k == 0:
                self.own.append(self.s.local(src, dst))
                continue
            cp = self.s.remote(src, dst, self.p.to(**{"d" + self.axis: k}))
            self.cps.append(cp)
            self.sent.append(cp)

    def swap(self):
        p, s = self.p, self.s
        for cp in self.own:
            cp.wait()
        for cp in self.cps:
            cp.wait_recv()
        lead = (slice(None),) * (1 if self.axis == "y" else 2)
        near, far = [self.bl.at[(pl.ds(k, 4),) + lead + (1 - p.c,)] for k in (0, 4)]
        self.cores = [
            s.remote(near, far, p.to(dc=1)),
            s.remote(self.br.at[pl.ds(0, 512)], self.br.at[pl.ds(512, 512)], p.to(dc=1)),
        ]
        self.sent += self.cores

    def ready(self):
        for cp in self.cores:
            cp.wait_recv()

    def multiply(self, lo, g):
        n = g.shape[-1]

        def body(b, _):
            at = (b, self.p.c) if self.axis == "y" else (b, slice(None), self.p.c)
            left = [self.bl[(k,) + at].reshape(4 * g.shape[2], 128) for k in range(8)]
            v = nn(jnp.concatenate(left, axis=1), self.br[:, lo : lo + n])
            g[b] = v.astype(BF).reshape(4, g.shape[2], n)
            return 0

        lax.fori_loop(0, 2, body, 0)

    def finish(self):
        for cp in self.sent:
            cp.wait_send()


VECTORS = (
    "bias_q",
    "bias_v",
    "bias_out",
    "gain_one",
    "shift_one",
    "bias_down",
    "gain_two",
    "shift_two",
)


def ln_rows(u):
    center = u - jnp.mean(u, axis=-1, keepdims=True)
    spread = jnp.mean(center * center, axis=-1, keepdims=True)
    inverse = lax.rsqrt(spread + epsilon)
    return center * inverse, inverse


def ln_back(e, hat, inverse, gain):
    scaled = e * gain
    centered = scaled - jnp.mean(scaled, axis=-1, keepdims=True)
    return inverse * (centered - hat * jnp.mean(scaled * hat, axis=-1, keepdims=True))


def col_sum(v):
    return jnp.sum(v, axis=0, keepdims=True)


def middle(
    tok,
    ctx,
    cot,
    small_v,
    wait_out,
    wait_up,
    wait_down,
    w_out,
    w_up,
    w_down,
    output,
    gctx,
    gsum,
    lefts,
    rights,
    small,
    vec,
    bup,
    slope,
    hat1,
    base,
    acc,
    toks,
    place,
):
    for r, name in enumerate(VECTORS):
        for j in range(8):
            a = small_v[j // 4, j % 4, 0, 0, r : r + 1, 0:128]
            b = small_v[j // 4, j % 4, 1, 0, r : r + 1, 128:256]
            vec[r : r + 1, j * 128 : (j + 1) * 128] = a + b
    for f in range(16):
        bup[0:1, f * 256 : (f + 1) * 256] = small_v[f // 8, (f // 2) % 4, f % 2, 0, 8:9, :]
    row = {n: vec[r : r + 1, :] for r, n in enumerate(VECTORS)}

    def put(name, v):
        r = VECTORS.index(name)
        for j in range(8):
            small[j // 4, j % 4, 0, r : r + 1, 0:128] = v[:, j * 128 : (j + 1) * 128]

    small[...] = jnp.zeros_like(small)
    x = tok[...].astype(F32)
    wait_out()
    branch = nn(ctx[...], w_out[...]) + row["bias_out"]
    hat, inv1 = ln_rows(x + branch)
    hat1[...] = hat
    normed = hat * row["gain_one"] + row["shift_one"]
    base[...] = normed
    low = normed.astype(BF)
    rights["low"][...] = low
    lefts["up"][...] = normed.T.astype(BF).reshape(2, 4, 2, 64, 128)
    lefts["out"][...] = ctx[...].astype(F32).T.astype(BF).reshape(2, 4, 2, 64, 128)
    toks["up"].send(0)
    toks["out"].send(0)
    acc[...] = jnp.zeros_like(acc)

    def up(t, _):
        cols = pl.ds(pl.multiple_of(t * 512, 512), 512)
        wait_up(t)
        pre = nn(rights["low"][...], w_up[t]) + bup[0:1, cols]
        cdf = 0.5 * (1.0 + lax.erf(pre * root_half))
        slope[:, cols] = cdf + pre * jnp.exp(-0.5 * pre * pre) * inv_root_two_pi
        act = pre * cdf
        lefts["down"][t // 4, lax.rem(t, 4)] = act.T.astype(BF).reshape(2, 256, 128)
        wait_down(t)
        acc[...] += nn(act.astype(BF), w_down[t])
        return 0

    lax.fori_loop(0, 8, up, 0)
    toks["down"].send(0)
    hat2, inv2 = ln_rows(base[...] + acc[...] + row["bias_down"])
    output[...] = (hat2 * row["gain_two"] + row["shift_two"]).astype(BF)
    dy = cot[...].astype(F32)
    put("gain_two", col_sum(dy * hat2))
    put("shift_two", col_sum(dy))
    gs2 = ln_back(dy, hat2, inv2, row["gain_two"])
    acc[...] = gs2
    ffn = gs2.astype(BF)
    rights["down"][...] = ffn
    toks["down"].send(1)
    put("bias_down", col_sum(ffn.astype(F32)))

    def back(k, j, _):
        t = 2 * lax.rem(place.z + k, 4) + j
        cols = pl.ds(pl.multiple_of(t * 512, 512), 512)
        pre = (nt(rights["down"][...], w_down[t]) * slope[:, cols]).astype(BF)
        rights["up"][:, cols] = pre
        s = col_sum(pre.astype(F32))
        small[t // 4, lax.rem(t, 4), 1, 0:1, :] = s[:, :256]
        small[t // 4, lax.rem(t, 4), 1, 1:2, :] = s[:, 256:]
        acc[...] += nt(pre, w_up[t])
        return 0

    for k in (1, 3, 2, 0):
        lax.fori_loop(0, 2, functools.partial(back, k), 0)
        toks["up"].send(1, (k,))
    gn = acc[...]
    hat = hat1[...]
    put("gain_one", col_sum(gn * hat))
    put("shift_one", col_sum(gn))
    gs1 = ln_back(gn, hat, inv1, row["gain_one"])
    gsum[...] = gs1
    gb = gs1.astype(BF)
    rights["out"][...] = gb
    toks["out"].send(1)
    put("bias_out", col_sum(gb.astype(F32)))
    gctx[...] = nt(gb, w_out[...]).astype(BF)


GRAD_NAMES = ("down", "up", "out")
GRAD_AXIS = {"down": "y", "up": "z", "out": "y"}
PIECE_ROWS = {"down": 64, "up": 64, "out": 16}
PIECES = (
    ("down", 0, 512, "xz"),
    ("down", 512, 512, "xz"),
    ("up", 0, 512, "yx"),
    ("up", 512, 512, "xy"),
    ("out", 0, 1024, "xz"),
)


def backward_kernel(*refs):
    refs = list(refs)

    def take(n):
        head = refs[:n]
        del refs[:n]
        return head

    k = len(GRAD_NAMES)
    tok, ctx, cot, small_h, out_h, up_h, down_h, tall_t, wsel, qkv, lse = take(11)
    totals = dict(zip(GRAD_NAMES, take(k)))
    small_total, grad_tok, gw, output = take(4)
    small_v, w_out, w_up, w_down, low, vec, bup, slope, hat1, base, acc, sem = take(12)
    gctx, gsum = take(2)
    left = dict(zip(GRAD_NAMES, take(k)))
    right = dict(zip(GRAD_NAMES, take(k)))
    both_left = dict(zip(GRAD_NAMES, take(k)))
    both_right = dict(zip(GRAD_NAMES, take(k)))
    small_src, small_in, small_g = take(3)
    small_bufs = take(5)
    g, bufs = [], []
    for _ in PIECES:
        g += take(1)
        bufs.append(take(3))
    do, kt, dqt, dkv, dqkv, gq, gq_c, gq_x, gq_y = take(9)
    dts, dtx, dtxr, dtz, dtz_s, dtzr = take(6)
    bq, bq_c, bq_s, bq_x, bq_y, bw = take(6)
    vec_cp = pltpu.make_async_copy(small_h, small_v, sem.at[0])
    out_cp = pltpu.make_async_copy(out_h, w_out, sem.at[1])
    vec_cp.start()
    out_cp.start()
    for t in range(8):
        pltpu.make_async_copy(up_h.at[:, pl.ds(t * 512, 512)], w_up.at[t], sem.at[2 + t]).start()
        pltpu.make_async_copy(down_h.at[pl.ds(t * 512, 512)], w_down.at[t], sem.at[10 + t]).start()

    def wait_up(t):
        pltpu.make_async_copy(up_h.at[:, pl.ds(0, 512)], w_up.at[t], sem.at[2 + t]).wait()

    def wait_down(t):
        pltpu.make_async_copy(down_h.at[pl.ds(0, 512)], w_down.at[t], sem.at[10 + t]).wait()

    p, s = Place(), Copies(*refs)
    me = p.xh * 4 + p.z
    peers = sp_peers(p)
    greet(
        [p.to(dy=1), p.to(dy=2), p.to(dy=3), p.to(dx=1), p.to(dx=3), p.to(dc=1)]
        + [d for d, _ in peers]
    )
    sent = []

    def go(src, dst, dev):
        cp = s.remote(src, dst, dev)
        sent.append(cp)
        return cp

    toks = {
        m: Tokens(p, s, GRAD_AXIS[m], left[m], right[m], both_left[m], both_right[m])
        for m in GRAD_NAMES
    }
    vec_cp.wait()
    middle(
        tok,
        ctx,
        cot,
        small_v,
        out_cp.wait,
        wait_up,
        wait_down,
        w_out,
        w_up,
        w_down,
        output,
        gctx,
        gsum,
        left,
        dict(right, low=low),
        small_src,
        vec,
        bup,
        slope,
        hat1,
        base,
        acc,
        toks,
        p,
    )
    do_cps = [
        go(gctx.at[:, pl.ds(pl.multiple_of(t * 128, 128), 128)], do.at[me], d) for d, t in peers
    ]
    do_own = s.local(gctx.at[:, pl.ds(pl.multiple_of(me * 128, 128), 128)], do.at[me])
    small_swap = s.remote(small_src, small_in, p.to(dc=1))
    small_red = Reduce(p, s, "xyz", small_g, small_bufs, small_total)
    toks["down"].swap()
    red = [
        ReduceTwo(p, s, o, gi, b, totals[m].at[:, :, pl.ds(lo, n)])
        for (m, lo, n, o), gi, b in zip(PIECES, g, bufs)
    ]
    kt[...] = qkv[:, 128:256].astype(F32).T.astype(BF)
    toks["up"].swap()
    ready = set()

    def begin(i):
        m, lo, _, _ = PIECES[i]
        if m not in ready:
            toks[m].ready()
            ready.add(m)
        toks[m].multiply(lo, g[i])
        red[i].first()

    begin(0)
    begin(1)
    small_swap.wait_recv()
    small_g[...] = small_src[...] + small_in[...]
    small_red.first()
    do_own.wait()
    for cp in do_cps:
        cp.wait_recv()
    dkv[...] = jnp.zeros_like(dkv)

    def head_block(b, h):
        rows = pl.ds(b * 256, 256)
        lanes = slice(64 * h, 64 * h + 64)
        keys = qkv[:, 128 + 64 * h : 192 + 64 * h]
        vals = qkv[:, 256 + 64 * h : 320 + 64 * h]
        q = qkv[rows, lanes]
        dob = do[2 * b : 2 * b + 2].reshape(256, 128)[:, lanes]
        probs = jnp.exp(nt(keys, q) * 0.125 - lse[h : h + 1, rows])
        dp = nt(vals, dob)
        inner = jnp.sum(probs * dp, axis=0, keepdims=True)
        ds = (probs * (dp - inner)).astype(BF)
        dqt[lanes, rows] = nn(kt[lanes, :], ds) * 0.125
        dkv[:, lanes] += nn(ds, q) * 0.125
        dkv[:, 128 + 64 * h : 192 + 64 * h] += nn(probs.astype(BF), dob)

    for b in range(4):
        for h in range(2):
            head_block(b, h)
        if b == 0:
            begin(2)
            toks["out"].swap()
        if b == 1:
            begin(3)
            red[0].second()
        if b == 2:
            begin(4)
            red[1].second()
    dqkv[:, :128] = dqt[...].T.astype(BF)
    dqkv[:, 128:] = dkv[...].astype(BF)

    def part(i, _):
        rows = pl.ds(pl.multiple_of(i * 256, 256), 256)
        v = nt(dqkv[rows, :], wsel[...].reshape(1024, 384)).astype(BF)
        dts[i // 2, pl.ds(2 * lax.rem(i, 2), 2)] = v.reshape(2, 128, 1024)
        return 0

    lax.fori_loop(0, 4, part, 0)
    first, second = pl.ds(0, 512), pl.ds(512, 512)
    dx_cp = go(dts.at[1 - p.xh, :, :, first], dtx, p.to(dx=2))
    dz_cps = [
        go(dts.at[:, lax.rem(p.z + d, 4), :, second], dtz.at[d - 1], p.to(dz=d)) for d in (1, 3, 2)
    ]

    def rows_of(i, _):
        v = nn(tall_t[pl.ds(pl.multiple_of(i * 256, 256), 256), :], dqkv[...])
        gq[pl.ds(2 * i, 2)] = v.astype(BF).reshape(2, 2, 64, 384)
        return 0

    lax.fori_loop(0, 4, rows_of, 0)
    c_cp = go(gq.at[:, 1 - p.c], gq_c, p.to(dc=1))
    cols = jnp.sum(dqkv[...].astype(F32), axis=0, keepdims=True)
    bq[...] = jnp.zeros_like(bq)
    bq[0:1, :] = cols[:, :128]
    bq[1:2, :] = cols[:, 256:]
    bc_cp = go(bq, bq_c, p.to(dc=1))
    small_red.second()
    red[2].second()
    red[3].second()
    c_cp.wait_recv()

    def add_core(i, _):
        gq_c[i] = (gq_c[i].astype(F32) + gq[i, p.c].astype(F32)).astype(BF)
        return 0

    lax.fori_loop(0, 8, add_core, 0)
    x_cp = go(gq_c.at[pl.ds((1 - p.xl) * 4, 4)], gq_x, p.to(dx=1 - 2 * p.xl))
    bc_cp.wait_recv()
    bq_s[0] = bq[...] + bq_c[...]
    bx_cp = go(bq_s.at[0], bq_x, p.to(dx=1 - 2 * p.xl))
    red[4].second()
    small_red.third()
    red[0].share()
    red[1].share()
    x_cp.wait_recv()

    def add_x(i, _):
        gq_x[i] = (gq_x[i].astype(F32) + gq_c[p.xl * 4 + i].astype(F32)).astype(BF)
        return 0

    lax.fori_loop(0, 4, add_x, 0)
    y_cps = [go(gq_x.at[lax.rem(p.y + d, 4)], gq_y.at[d - 1], p.to(dy=d)) for d in (1, 3, 2)]
    bx_cp.wait_recv()
    bq_s[1] = bq_s[0] + bq_x[...]
    by_cps = [go(bq_s.at[1], bq_y.at[d - 1], p.to(dy=d)) for d in (1, 3, 2)]
    dx_cp.wait_recv()

    def add_far(i, _):
        dtx[i] = (dtx[i].astype(F32) + dts[p.xh, i, :, 0:512].astype(F32)).astype(BF)
        return 0

    lax.fori_loop(0, 4, add_far, 0)
    dz2_cps = [go(dtx.at[lax.rem(p.z + d, 4)], dtxr.at[d - 1], p.to(dz=d)) for d in (1, 3, 2)]
    for cp in dz_cps:
        cp.wait_recv()

    def add_round(i, _):
        v = dts[i, p.z, :, 512:1024].astype(F32)
        for d in range(3):
            v = v + dtz[d, i].astype(F32)
        dtz_s[i] = v.astype(BF)
        return 0

    lax.fori_loop(0, 2, add_round, 0)
    dx2_cp = go(dtz_s.at[1 - p.xh], dtzr, p.to(dx=2))
    red[2].share()
    red[3].share()
    red[4].share()
    small_red.share()
    red[0].spread()
    red[1].spread()
    for cp in y_cps:
        cp.wait_recv()
    acc = gq_x[p.y].astype(F32)
    for i in range(3):
        acc = acc + gq_y[i].astype(F32)
    gw[me] = acc.astype(BF)
    for cp in by_cps:
        cp.wait_recv()
    bw[me] = ((bq_s[1] + bq_y[0]) + (bq_y[1] + bq_y[2]))[0:8, :]
    gw_cps = [go(gw.at[me], gw.at[me], d) for d, _ in peers]
    gw_cps += [go(bw.at[me], bw.at[me], d) for d, _ in peers]
    red[2].spread()
    red[3].spread()
    red[4].spread()
    small_red.spread()
    for cp in dz2_cps:
        cp.wait_recv()
    dx2_cp.wait_recv()
    acc = gsum[:, 0:512] + dtx[p.z].astype(F32)
    for t in range(3):
        acc = acc + dtxr[t].astype(F32)
    grad_tok[:, 0:512] = acc.astype(BF)
    acc = gsum[:, 512:1024] + dtz_s[p.xh].astype(F32) + dtzr[...].astype(F32)
    grad_tok[:, 512:1024] = acc.astype(BF)
    for cp in gw_cps:
        cp.wait_recv()
    for r in red:
        r.done()
    small_red.done()
    for r in red:
        r.finish()
    for m in GRAD_NAMES:
        toks[m].finish()
    small_red.finish()
    small_swap.wait_send()
    small_total[0, 0:2, 0:128] = bw[p.xl * 4 + p.y, 0:2, :]
    for cp in sent:
        cp.wait_send()


def finish_layer(tok, ctx, cot, small_h, out_h, up_h, down_h, tall_t, wsel, qkv, lse):
    scratch = [
        pltpu.VMEM((2, 4, 2, 1, 16, 256), F32),
        pltpu.VMEM((1024, 1024), BF),
        pltpu.VMEM((8, 1024, 512), BF),
        pltpu.VMEM((8, 512, 1024), BF),
        pltpu.VMEM((128, 1024), BF),
        pltpu.VMEM((8, 1024), F32),
        pltpu.VMEM((8, 4096), F32),
        pltpu.VMEM((128, 4096), F32),
        pltpu.VMEM((128, 1024), F32),
        pltpu.VMEM((128, 1024), F32),
        pltpu.VMEM((128, 1024), F32),
        pltpu.SemaphoreType.DMA((18,)),
        pltpu.VMEM((128, 1024), BF),
        pltpu.VMEM((128, 1024), F32),
    ]
    scratch += [pltpu.VMEM((2, 4, 2, ROWS[m], 128), BF) for m in GRAD_NAMES]
    scratch += [pltpu.VMEM((128, COLS[m]), BF) for m in GRAD_NAMES]
    scratch += [
        pltpu.VMEM((8, 2, 2, ROWS[m], 128) if GRAD_AXIS[m] == "y" else (8, 2, 4, 2, ROWS[m], 128), BF)
        for m in GRAD_NAMES
    ]
    scratch += [pltpu.VMEM((1024, 1024), BF) for m in GRAD_NAMES]
    scratch += [pltpu.VMEM(SMALL_SHAPE, F32)] * 3
    scratch += [pltpu.VMEM(x, F32) for x in reduce_shapes("xyz", 8, 256)]
    for m, _, n, o in PIECES:
        scratch.append(pltpu.VMEM((2, 4, PIECE_ROWS[m], n), BF))
        scratch += [pltpu.VMEM(x, BF) for x in reduce_two_shapes(o, PIECE_ROWS[m], n)]
    scratch += [
        pltpu.VMEM((8, 128, 128), BF),
        pltpu.VMEM((128, 1024), BF),
        pltpu.VMEM((128, 1024), F32),
        pltpu.VMEM((1024, 256), F32),
        pltpu.VMEM((1024, 384), BF),
        pltpu.VMEM((8, 2, 64, 384), BF),
        pltpu.VMEM((8, 64, 384), BF),
        pltpu.VMEM((4, 64, 384), BF),
        pltpu.VMEM((3, 64, 384), BF),
        pltpu.VMEM((2, 4, 128, 1024), BF),
        pltpu.VMEM((4, 128, 512), BF),
        pltpu.VMEM((3, 128, 512), BF),
        pltpu.VMEM((3, 2, 128, 512), BF),
        pltpu.VMEM((2, 128, 512), BF),
        pltpu.VMEM((128, 512), BF),
        pltpu.VMEM((8, 128), F32),
        pltpu.VMEM((8, 128), F32),
        pltpu.VMEM((2, 8, 128), F32),
        pltpu.VMEM((8, 128), F32),
        pltpu.VMEM((3, 8, 128), F32),
        pltpu.VMEM((8, 8, 128), F32),
    ]
    scratch += [pltpu.SemaphoreType.DMA((250,)), pltpu.SemaphoreType.DMA((250,))]
    k = len(GRAD_NAMES)
    out = pl.pallas_call(
        backward_kernel,
        out_shape=[jax.ShapeDtypeStruct((4, PIECE_ROWS[m], 1024), BF) for m in GRAD_NAMES]
        + [
            jax.ShapeDtypeStruct((4, 8, 256), F32),
            jax.ShapeDtypeStruct((128, 1024), BF),
            jax.ShapeDtypeStruct((8, 64, 384), BF),
            jax.ShapeDtypeStruct((128, 1024), BF),
        ],
        in_specs=[INSIDE] * 3 + [ANYWHERE] * 4 + [INSIDE] * 4,
        out_specs=[INSIDE] * (k + 4),
        scratch_shapes=scratch,
        compiler_params=pltpu.CompilerParams(
            collective_id=2, has_side_effects=True, vmem_limit_bytes=62 * 2**20
        ),
        name="layer_back",
    )(tok, ctx, cot, small_h, out_h, up_h, down_h, tall_t, wsel, qkv, lse)
    grads = {
        "down": out[0].reshape(256, 1024).astype(F32),
        "up": out[1].transpose(1, 0, 2).reshape(64, 4096).astype(F32),
        "out": out[2].reshape(64, 1024).astype(F32),
    }
    gw = out[k + 2].reshape(8, 64, 3, 128).transpose(1, 2, 0, 3)
    grads["qkv"] = gw.reshape(64, 3072).astype(F32)
    return grads, out[k], out[k + 1], out[k + 3]


def on_device(
    tokens,
    cotangent,
    w_qkv,
    bias_q,
    bias_v,
    w_out,
    bias_out,
    gain_one,
    shift_one,
    w_up,
    bias_up,
    w_down,
    bias_down,
    gain_two,
    shift_two,
):
    num_seqs, slice_len, model_width = tokens.shape
    row_count = num_seqs * slice_len
    inputs = tokens.reshape(row_count, model_width)
    own = dict(
        bias_q=bias_q,
        bias_v=bias_v,
        bias_out=bias_out,
        gain_one=gain_one,
        shift_one=shift_one,
        bias_down=bias_down,
        gain_two=gain_two,
        shift_two=shift_two,
    )
    vectors = jnp.stack([own[k] for k in VECTORS]).astype(F32)
    small, full_out, full_up, full_down, tall_t, wsel, qkv, lse, context_tokens = attend_forward(
        inputs, w_qkv, vectors, bias_up.astype(F32).reshape(1, 256), [w_out, w_up, w_down]
    )
    grads, total, grad_inputs, output = finish_layer(
        inputs,
        context_tokens,
        cotangent.reshape(row_count, model_width),
        small,
        full_out,
        full_up,
        full_down,
        tall_t,
        wsel,
        qkv,
        lse,
    )
    core = lax.axis_index("fsdp") % 2
    mine = lax.dynamic_slice(total, (0, 0, core * 64), (1, 8, 64))
    res = {k: mine[0, r] for r, k in enumerate(VECTORS)}
    res["bias_up"] = lax.dynamic_slice(total, (1, core, 0), (1, 1, 256)).reshape(256)
    return (
        output.reshape(tokens.shape),
        grad_inputs.reshape(tokens.shape),
        grads["qkv"],
        res["bias_q"],
        res["bias_v"],
        grads["out"],
        res["bias_out"],
        res["gain_one"],
        res["shift_one"],
        grads["up"],
        res["bias_up"],
        grads["down"],
        res["bias_down"],
        res["gain_two"],
        res["shift_two"],
    )


def solution(mesh):
    rows, vector = P("fsdp", None), P("fsdp")
    block = P("fsdp", "sp", None)
    params = (rows, vector, vector, rows, vector, vector, vector)
    params += (rows, vector, rows, vector, vector, vector)
    return jax.shard_map(
        on_device,
        mesh=mesh,
        in_specs=(block, block) + params,
        out_specs=(block, block) + params,
        check_vma=False,
    )
```
